32 devices in a mesh: dp: 8 (over z, y), tensor: 4 (over x, core).
Axes of the slice: x: 2, y: 2, z: 4, core: 2. Of those that a mesh axis runs over, the one named last changes fastest.
Arguments:
- tokens: bfloat16 [4096, 1536], P('dp'), may hold values from -6 to 6
- document_numbers: int32 [8, 512], P('dp'), may hold values from 0 to 31, never falling along the last dimension, each value on 1 to 256 neighbouring positions
- picks: int32 [4096, 8], P('dp'), may hold values from 0 to 63, all different within a row
- drop_order: int32 [8, 4096], P('dp'), may hold values from 0 to 4095, each once within a row
- w_query: bfloat16 [1536, 1536], P('dp', 'tensor'), may hold values from -0.15625 to 0.15625
- key_matrix: bfloat16 [1536, 512], P('dp', 'tensor'), may hold values from -0.15625 to 0.15625
- value_matrix: bfloat16 [1536, 512], P('dp', 'tensor'), may hold values from -0.15625 to 0.15625
- w_out: bfloat16 [1536, 1536], P('tensor', 'dp'), may hold values from -0.625 to 0.625
- w_router: bfloat16 [1536, 64], P('dp'), may hold values from -0.078125 to 0.078125
- gain_attn: bfloat16 [1536], P('dp'), may hold values from 0.5 to 1.5
- gain_moe: bfloat16 [1536], P('dp'), may hold values from 0.5 to 1.5
- expert_gate: bfloat16 [64, 1536, 512], P('dp', None, 'tensor'), may hold values from -0.15625 to 0.15625
- expert_up: bfloat16 [64, 1536, 512], P('dp', None, 'tensor'), may hold values from -0.15625 to 0.15625
- expert_down: bfloat16 [64, 512, 1536], P('dp', 'tensor'), may hold values from -0.5 to 0.5
- cotangent: bfloat16 [4096, 1536], P('dp'), may hold values from -6 to 6
Outputs:
- mixed: bfloat16 [4096, 1536], P('dp', 'tensor')
- grad_tokens: float32 [4096, 1536], P('dp', 'tensor')
- grad_query: float32 [1536, 1536], P('dp', 'tensor')
- grad_key: float32 [1536, 512], P('dp', 'tensor')
- grad_value: float32 [1536, 512], P('dp', 'tensor')
- grad_out: float32 [1536, 1536], P('tensor', 'dp')
- grad_router: float32 [1536, 64], P('dp')
- grad_gain_attn: float32 [1536], P('dp')
- grad_gain_moe: float32 [1536], P('dp')
- grad_expert_gate: float32 [64, 1536, 512], P('dp', None, 'tensor')
- grad_expert_up: float32 [64, 1536, 512], P('dp', None, 'tensor')
- grad_expert_down: float32 [64, 512, 1536], P('dp', 'tensor')
The draws below stay inside these ranges and needn't reach their ends.
Inputs may be any that keep to these rules, and one draw needn't show every extreme that they name: `picks`: each token names 8 different experts. `document_numbers`: segment numbers never fall along a sequence; each document has at most half of 512 tokens. `drop_order`: each row holds every number once.
All inputs are finite; a program needn't handle non-finite values.
Results may differ from the reference program's by a relative error of at most 0.018.
Values may be sent and summed in bfloat16 or wider, within the bound.
No kernel may reach another device: no remote copies, remote signals or barrier semaphores. Data moves between devices by JAX's collectives and lax.ppermute only.
A program may use at most 320 MiB of HBM per device.

```python
import math
import jax
import jax.numpy as jnp
import numpy as np
from jax import lax

MODEL_WIDTH = 1536
QUERY_HEADS = 24
KEY_VALUE_HEADS = 8
HEAD_SIZE = 64
EFF = 512
TOP = 8
EXPERTS = 64
SEQUENCE_TOKENS = 512
TOKEN_TOTAL = 4096
CS = 72
N_DP = 8


def shard_levels(rng, shape, cuts, low, high):
    def one(position, parts):
        heights = jax.random.uniform(jax.random.fold_in(jax.random.fold_in(rng, 6), position), (parts,), jnp.float32, low / len(cuts), high / len(cuts))
        return jnp.repeat(jnp.exp(heights), shape[position] // parts).reshape((-1,) + (1,) * (len(shape) - position - 1))

    factor_of = one(*cuts[0])
    for cut in cuts[1:]:
        factor_of = factor_of * one(*cut)
    return factor_of


def different_ones(stream_key, rows, number_of, top, lift):
    ranking = jax.random.permutation(jax.random.fold_in(stream_key, 1), number_of)
    boost = ranking
    for power in range(3):
        boost = boost * boost // number_of
    boost = boost * lift // number_of
    tickets = jax.random.randint(jax.random.fold_in(stream_key, 2), (rows, number_of), 0, 4096) + boost
    sure = jax.random.permutation(jax.random.fold_in(stream_key, 3), rows)[jnp.arange(number_of) % rows]
    tickets = jnp.where(jnp.arange(rows)[:, None] == sure[None, :], 1 << 14, tickets)
    merit = tickets * number_of + jnp.arange(number_of)
    return lax.top_k(merit.astype(jnp.int32), top)[1].astype(jnp.int32)


def length_profile(count, total, limit, lean):
    loads = [(1 << 20) // math.isqrt(rank ** lean) + 1 for rank in range(2, count + 1)]
    surplus, given = total - limit - (count - 1), [1] * (count - 1)
    while surplus > 0:
        candidates = [i for i in range(count - 1) if given[i] < limit]
        whole, remaining = sum([loads[i] for i in candidates]), surplus
        for i in candidates:
            more = min(limit - given[i], max(1, remaining * loads[i] // whole), surplus)
            given[i] = given[i] + more
            surplus = surplus - more
    return np.array([limit] + given)


def uneven_parts(key, amount, total, most, skew):
    if amount == 2:
        one = jax.random.randint(key, (), max(1, total - most), min(most, total - 1) + 1)
        return jnp.stack([one, total - one])
    sizes = jnp.asarray(length_profile(amount, total, most, skew), jnp.int32)
    pairs = (amount - 1) // 2
    source_of, taker = sizes[1:1 + 2 * pairs:2], sizes[2:2 + 2 * pairs:2]
    room = jnp.minimum(source_of - 1, most - taker)
    moved = jax.random.randint(jax.random.fold_in(key, 1), (pairs,), 0, 1 << 20) % (room + 1)
    sizes = sizes.at[1:1 + 2 * pairs:2].set(source_of - moved).at[2:2 + 2 * pairs:2].set(taker + moved)
    return sizes[jax.random.permutation(jax.random.fold_in(key, 2), amount)]


def centred(rng, extent, width, reach, split=(), held_as=jnp.bfloat16):
    drawn = width * jax.random.normal(rng, extent, jnp.float32)
    if split:
        drawn = drawn * shard_levels(rng, extent, split, -0.22, 0.18)
    return jnp.clip(drawn, -reach, reach).astype(held_as)


def setup_inputs(seed: int = 0) -> dict:
    keys = jax.random.split(jax.random.key(seed), 16)
    return {
        "tokens": centred(keys[0], (TOKEN_TOTAL, MODEL_WIDTH), 1.0, 6.0, ((0, 8),)),
        "document_numbers": jax.vmap(lambda own: jnp.searchsorted(jnp.cumsum(uneven_parts(own, SEQUENCE_TOKENS // 16, SEQUENCE_TOKENS, SEQUENCE_TOKENS // 2, 2)), jnp.arange(SEQUENCE_TOKENS), side="right"))(jax.random.split(keys[1], N_DP)).reshape((N_DP, SEQUENCE_TOKENS)).astype(jnp.int32),
        "picks": different_ones(keys[2], TOKEN_TOTAL, EXPERTS, TOP, 1024),
        "drop_order": jax.vmap(lambda own: jax.random.permutation(own, SEQUENCE_TOKENS * TOP))(jax.random.split(keys[3], N_DP)).reshape((N_DP, SEQUENCE_TOKENS * TOP)).astype(jnp.int32),
        "w_query": centred(keys[4], (MODEL_WIDTH, QUERY_HEADS * HEAD_SIZE), MODEL_WIDTH ** -0.5, 0.15625, ((0, 8), (1, 4))),
        "key_matrix": centred(keys[5], (MODEL_WIDTH, KEY_VALUE_HEADS * HEAD_SIZE), MODEL_WIDTH ** -0.5, 0.15625, ((0, 8), (1, 4))),
        "value_matrix": centred(keys[6], (MODEL_WIDTH, KEY_VALUE_HEADS * HEAD_SIZE), MODEL_WIDTH ** -0.5, 0.15625, ((0, 8), (1, 4))),
        "w_out": centred(keys[7], (QUERY_HEADS * HEAD_SIZE, MODEL_WIDTH), (QUERY_HEADS * HEAD_SIZE // 16) ** -0.5, 0.625, ((0, 4), (1, 8))),
        "w_router": centred(keys[8], (MODEL_WIDTH, EXPERTS), (4 * MODEL_WIDTH) ** -0.5, 0.078125, ((0, 8),)),
        "gain_attn": jnp.clip(1.0 + 0.1 * jax.random.normal(keys[9], (MODEL_WIDTH,), jnp.float32), 0.5, 1.5).astype(jnp.bfloat16),
        "gain_moe": jnp.clip(1.0 + 0.1 * jax.random.normal(keys[10], (MODEL_WIDTH,), jnp.float32), 0.5, 1.5).astype(jnp.bfloat16),
        "expert_gate": centred(keys[11], (EXPERTS, MODEL_WIDTH, EFF), MODEL_WIDTH ** -0.5, 0.15625, ((0, 8), (2, 4))),
        "expert_up": centred(keys[12], (EXPERTS, MODEL_WIDTH, EFF), MODEL_WIDTH ** -0.5, 0.15625, ((0, 8), (2, 4))),
        "expert_down": centred(keys[13], (EXPERTS, EFF, MODEL_WIDTH), (EFF // 4) ** -0.5, 0.5, ((0, 8), (1, 4))),
        "cotangent": centred(keys[14], (TOKEN_TOTAL, MODEL_WIDTH), 1.0, 6.0, ((0, 8),)),
    }


@jax.custom_vjp
def reduced_precision(v):
    return lax.optimization_barrier(v.astype(jnp.bfloat16)).astype(jnp.float32)

@jax.custom_vjp
def low_back(v):
    return v

def low_keep(v):
    return (reduced_precision(v), None)

def low_pass(kept, grad):
    return (grad,)

def back_keep(v):
    return (v, None)

def back_low(kept, grad):
    return (reduced_precision(grad),)
reduced_precision.defvjp(low_keep, low_pass)
low_back.defvjp(back_keep, back_low)
epsilon = 1e-05
negative_big = -1e+30
rope_base = 10000.0
highest = lax.Precision.HIGHEST

def rotary_tables(positions, head_width):
    half_width = head_width // 2
    inverse = rope_base ** (-(2.0 * jnp.arange(half_width, dtype=jnp.float32)) / head_width)
    angles = positions.astype(jnp.float32)[:, None] * inverse[None, :]
    return (jnp.cos(angles)[:, None, :], jnp.sin(angles)[:, None, :])

def apply_pair_rotation(values, cosine_values, sine_values):
    half_width = values.shape[-1] // 2
    first_half = values[..., :half_width]
    second_half = values[..., half_width:]
    return jnp.concatenate([first_half * cosine_values - second_half * sine_values, second_half * cosine_values + first_half * sine_values], axis=-1)

def slot_table(chosen_rows, order_row, expert_count, capacity):
    flat_experts = chosen_rows.reshape(-1).astype(jnp.int32)
    pair_count = flat_experts.shape[0]
    sort_keys = flat_experts * pair_count + order_row.astype(jnp.int32)
    ordering = jnp.argsort(sort_keys).astype(jnp.int32)
    sorted_experts = flat_experts[ordering]
    expert_ids = jnp.arange(expert_count, dtype=jnp.int32)
    counts = lax.optimization_barrier(jnp.sum((flat_experts[:, None] == expert_ids[None, :]).astype(jnp.int32), axis=0, dtype=jnp.int32))
    starts = (jnp.cumsum(counts, dtype=jnp.int32) - counts).astype(jnp.int32)
    ranks_sorted = (jnp.arange(pair_count, dtype=jnp.int32) - starts[sorted_experts]).astype(jnp.int32)
    ranks = jnp.zeros((pair_count,), jnp.int32).at[ordering].set(ranks_sorted)
    destination = jnp.where(ranks < capacity, flat_experts * capacity + ranks, expert_count * capacity).astype(jnp.int32)
    table = jnp.full((expert_count * capacity + 1,), pair_count, jnp.int32)
    table = table.at[destination].set(jnp.arange(pair_count, dtype=jnp.int32))
    return (table[:expert_count * capacity], destination)

def reference(tokens, document_numbers, picks, drop_order, w_query, key_matrix, value_matrix, w_out, w_router, gain_attn, gain_moe, expert_gate, expert_up, expert_down, cotangent):
    pairs_dev = SEQUENCE_TOKENS * TOP
    tables = jax.vmap(lambda chosen_rows, order_row: slot_table(chosen_rows, order_row, EXPERTS, CS)[0])(picks.reshape(N_DP, SEQUENCE_TOKENS, TOP), drop_order)
    offsets = (jnp.arange(N_DP, dtype=jnp.int32) * pairs_dev)[:, None]
    global_slots = jnp.where(tables < pairs_dev, tables + offsets, TOKEN_TOTAL * TOP).astype(jnp.int32)
    global_slots = global_slots.reshape(N_DP, EXPERTS, CS).transpose(1, 0, 2).reshape(EXPERTS, N_DP * CS)
    positions = jnp.arange(TOKEN_TOTAL, dtype=jnp.int32) % SEQUENCE_TOKENS
    cosine_values, sine_values = rotary_tables(positions, HEAD_SIZE)
    score_scale = HEAD_SIZE ** (-0.5)

    def attend_sequence(query_seq, key_seq, value_seq, segment_seq):
        group_repeats = QUERY_HEADS // KEY_VALUE_HEADS
        key_wide = jnp.repeat(key_seq, group_repeats, axis=1)
        value_wide = jnp.repeat(value_seq, group_repeats, axis=1)
        raw_scores = low_back(jnp.einsum('qhd,khd->hqk', query_seq, key_wide, precision=highest) * score_scale)
        place = jnp.arange(SEQUENCE_TOKENS, dtype=jnp.int32)
        allowed = (segment_seq[:, None] == segment_seq[None, :]) & (place[None, :] <= place[:, None])
        probs = jax.nn.softmax(jnp.where(allowed[None], raw_scores, negative_big), axis=-1)
        mixed_heads = jnp.einsum('hqk,khd->qhd', reduced_precision(probs), value_wide, precision=highest)
        return reduced_precision(low_back(mixed_heads))
    checked_attend = jax.checkpoint(attend_sequence)

    def attention_update(carry_value, inputs):
        return (carry_value, checked_attend(*inputs))

    def expert_contribution(rows_ext, gate_ext, slot_ids, gate_w, up_w, down_w):
        slot_tokens = slot_ids // TOP
        expert_rows = low_back(rows_ext[slot_tokens])
        gate_val = low_back(jnp.dot(expert_rows, gate_w, precision=highest))
        up_val = low_back(jnp.dot(expert_rows, up_w, precision=highest))
        hidden_val = reduced_precision(jax.nn.silu(gate_val) * up_val)
        expert_outs = reduced_precision(low_back(jnp.dot(hidden_val, down_w, precision=highest)))
        weighted = gate_ext[slot_ids][:, None] * expert_outs
        return jnp.zeros((TOKEN_TOTAL + 1, MODEL_WIDTH), jnp.float32).at[slot_tokens].add(weighted)
    checked_expert = jax.checkpoint(expert_contribution)

    def forward(x_full, wq, wk, wv, wo, wr, g_attn, g_moe, e_gate, e_up, e_down):
        r_attn = lax.rsqrt(lax.optimization_barrier(jnp.mean(x_full * x_full, axis=-1, keepdims=True)) + epsilon)
        x_low = reduced_precision(x_full * r_attn * g_attn)
        q_proj = low_back(jnp.dot(x_low, wq, precision=highest))
        key_projected = low_back(jnp.dot(x_low, wk, precision=highest))
        value_projected = low_back(jnp.dot(x_low, wv, precision=highest))
        query_rotated = reduced_precision(apply_pair_rotation(q_proj.reshape(TOKEN_TOTAL, QUERY_HEADS, HEAD_SIZE), cosine_values, sine_values))
        key_rotated = reduced_precision(apply_pair_rotation(key_projected.reshape(TOKEN_TOTAL, KEY_VALUE_HEADS, HEAD_SIZE), cosine_values, sine_values))
        value_reduced = reduced_precision(value_projected).reshape(TOKEN_TOTAL, KEY_VALUE_HEADS, HEAD_SIZE)
        ignored_loop_state, head_outputs = lax.scan(attention_update, jnp.zeros((), jnp.float32), (query_rotated.reshape(N_DP, SEQUENCE_TOKENS, QUERY_HEADS, HEAD_SIZE), key_rotated.reshape(N_DP, SEQUENCE_TOKENS, KEY_VALUE_HEADS, HEAD_SIZE), value_reduced.reshape(N_DP, SEQUENCE_TOKENS, KEY_VALUE_HEADS, HEAD_SIZE), document_numbers))
        o_low = head_outputs.reshape(TOKEN_TOTAL, QUERY_HEADS * HEAD_SIZE)
        attn = low_back(jnp.dot(o_low, wo, precision=highest))
        h_full = x_full + attn
        r_moe = lax.rsqrt(lax.optimization_barrier(jnp.mean(h_full * h_full, axis=-1, keepdims=True)) + epsilon)
        a_low = reduced_precision(h_full * r_moe * g_moe)
        logits = low_back(jnp.dot(a_low, wr, precision=highest))
        chosen = jnp.take_along_axis(logits, picks, axis=1)
        gates = jax.nn.softmax(chosen, axis=-1)
        rows_ext = jnp.concatenate([a_low, jnp.zeros((1, MODEL_WIDTH), jnp.float32)], axis=0)
        gate_ext = jnp.concatenate([gates.reshape(-1), jnp.zeros((1,), jnp.float32)], axis=0)

        def expert_step(moe_sum, inputs):
            slot_ids, gate_w, up_w, down_w = inputs
            return (moe_sum + checked_expert(rows_ext, gate_ext, slot_ids, gate_w, up_w, down_w), None)
        moe_sum, unused_ys = lax.scan(expert_step, jnp.zeros((TOKEN_TOTAL + 1, MODEL_WIDTH), jnp.float32), (global_slots, e_gate, e_up, e_down))
        return h_full + moe_sum[:TOKEN_TOTAL]
    floats = tuple((item.astype(jnp.float32) for item in (tokens, w_query, key_matrix, value_matrix, w_out, w_router, gain_attn, gain_moe, expert_gate, expert_up, expert_down)))
    mixed, pull_back = jax.vjp(forward, *floats)
    grads = pull_back(cotangent.astype(jnp.float32))
    return (mixed.astype(jnp.bfloat16), grads[0], grads[1], grads[2], grads[3], grads[4], grads[5], grads[6], grads[7], grads[8], grads[9], grads[10])
```

```python
import functools

import jax
import jax.numpy as jnp
import numpy as np
from jax import lax
from jax.experimental import pallas as pl
from jax.experimental.pallas import tpu as pltpu
from jax.sharding import PartitionSpec as P

HEAD_SIZE = 64


epsilon = 1e-05
negative_big = -1e30
rope_base = 10000.0
F32 = jnp.float32
BF16 = jnp.bfloat16
BLK = 256
PAD = 80
VMEM_LIMIT = 62 * 1024 * 1024


def rotary_tables(positions, head_width):
    half_width = head_width // 2
    inverse = rope_base ** (-(2.0 * jnp.arange(half_width, dtype=jnp.float32)) / head_width)
    angles = positions.astype(jnp.float32)[:, None] * inverse[None, :]
    return (jnp.cos(angles)[:, None, :], jnp.sin(angles)[:, None, :])


def apply_pair_rotation(values, cosine_values, sine_values):
    half_width = values.shape[-1] // 2
    first_half = values[..., :half_width]
    second_half = values[..., half_width:]
    return jnp.concatenate(
        [
            first_half * cosine_values - second_half * sine_values,
            second_half * cosine_values + first_half * sine_values,
        ],
        axis=-1,
    )


def unrotate_pairs(values, cosine_values, sine_values):
    half_width = values.shape[-1] // 2
    first_half = values[..., :half_width]
    second_half = values[..., half_width:]
    return jnp.concatenate(
        [
            first_half * cosine_values + second_half * sine_values,
            second_half * cosine_values - first_half * sine_values,
        ],
        axis=-1,
    )


def slot_table(chosen_rows, order_row, expert_count, capacity):
    flat_experts = chosen_rows.reshape(-1)
    pair_count = flat_experts.shape[0]
    sort_keys = flat_experts * pair_count + order_row
    ordering = jnp.argsort(sort_keys)
    sorted_experts = flat_experts[ordering]
    expert_ids = jnp.arange(expert_count, dtype=jnp.int32)
    counts = jnp.sum(
        (flat_experts[:, None] == expert_ids[None, :]).astype(jnp.int32), axis=0, dtype=jnp.int32
    )
    starts = jnp.cumsum(counts, dtype=jnp.int32) - counts
    ranks_sorted = jnp.arange(pair_count, dtype=jnp.int32) - starts[sorted_experts]
    ranks = jnp.zeros((pair_count,), jnp.int32).at[ordering].set(ranks_sorted)
    destination = jnp.where(
        ranks < capacity, flat_experts * capacity + ranks, expert_count * capacity
    )
    table = jnp.full((expert_count * capacity + 1,), pair_count, jnp.int32)
    table = table.at[destination].set(jnp.arange(pair_count, dtype=jnp.int32))
    return (table[: expert_count * capacity], destination)


def on_device(
    tokens,
    document_numbers,
    picks,
    drop_order,
    w_query,
    key_matrix,
    value_matrix,
    w_out,
    w_router,
    gain_attn,
    gain_moe,
    expert_gate,
    expert_up,
    expert_down,
    cotangent,
):
    ranks_dp = lax.axis_size("dp")
    tensor_index = lax.axis_index("tensor")
    wq, wk, wv, wo, wr, g_attn, g_moe = (
        lax.all_gather(w_query, "dp", axis=0, tiled=True),
        lax.all_gather(key_matrix, "dp", axis=0, tiled=True),
        lax.all_gather(value_matrix, "dp", axis=0, tiled=True),
        lax.all_gather(w_out, "dp", axis=1, tiled=True),
        lax.all_gather(w_router, "dp", axis=0, tiled=True),
        lax.all_gather(gain_attn, "dp", axis=0, tiled=True),
        lax.all_gather(gain_moe, "dp", axis=0, tiled=True),
    )
    tok_count, width = tokens.shape
    col_width = width // lax.axis_size("tensor")
    col_start = tensor_index * col_width
    q_heads = wq.shape[1] // HEAD_SIZE
    kv_heads = wk.shape[1] // HEAD_SIZE
    group_repeats = q_heads // kv_heads
    score_scale = HEAD_SIZE ** (-0.5)
    seg_row = document_numbers.reshape(-1)
    positions = jnp.arange(tok_count, dtype=jnp.int32)
    cosine_values, sine_values = rotary_tables(positions, HEAD_SIZE)
    x_full = tokens.astype(jnp.float32)
    r_attn = lax.rsqrt(jnp.mean(x_full * x_full, axis=-1, keepdims=True) + epsilon)
    x_hat = x_full * r_attn
    gain_one = g_attn.astype(jnp.float32)
    x_low = (x_hat * gain_one).astype(jnp.bfloat16)
    q_proj = jnp.dot(x_low, wq, preferred_element_type=jnp.float32)
    key_projected = jnp.dot(x_low, wk, preferred_element_type=jnp.float32)
    value_projected = jnp.dot(x_low, wv, preferred_element_type=jnp.float32)
    query_rotated = apply_pair_rotation(
        q_proj.reshape(tok_count, q_heads, HEAD_SIZE), cosine_values, sine_values
    ).astype(jnp.bfloat16)
    query_rotated = query_rotated.reshape(tok_count, kv_heads, group_repeats, HEAD_SIZE)
    key_rotated = apply_pair_rotation(
        key_projected.reshape(tok_count, kv_heads, HEAD_SIZE), cosine_values, sine_values
    ).astype(jnp.bfloat16)
    value_reduced = value_projected.astype(jnp.bfloat16).reshape(tok_count, kv_heads, HEAD_SIZE)
    block_rows = min(512, tok_count)
    block_count = tok_count // block_rows
    q_blocks = query_rotated.reshape(block_count, block_rows, kv_heads, group_repeats, HEAD_SIZE)
    seg_blocks = seg_row.reshape(block_count, block_rows)
    pos_blocks = positions.reshape(block_count, block_rows)

    def masked_scores(q_block, seg_block, pos_block):
        raw_scores = (
            jnp.einsum("qgrd,kgd->grqk", q_block, key_rotated, preferred_element_type=jnp.float32)
            * score_scale
        )
        allowed = (seg_block[:, None] == seg_row[None, :]) & (
            positions[None, :] <= pos_block[:, None]
        )
        return jnp.where(allowed, raw_scores, negative_big)

    def forward_block(inputs):
        q_block, seg_block, pos_block = inputs
        scores = masked_scores(q_block, seg_block, pos_block)
        highest_score = jnp.max(scores, axis=-1, keepdims=True)
        weights = jnp.exp(scores - highest_score)
        totals = jnp.sum(weights, axis=-1, keepdims=True)
        probs = (weights / totals).astype(jnp.bfloat16)
        heads_block = jnp.einsum(
            "grqk,kgd->qgrd", probs, value_reduced, preferred_element_type=jnp.float32
        )
        return (heads_block.astype(jnp.bfloat16), highest_score + jnp.log(totals))

    head_outputs, log_totals = lax.map(forward_block, (q_blocks, seg_blocks, pos_blocks))
    o_low = head_outputs.reshape(tok_count, q_heads * HEAD_SIZE)
    attn_terms = jnp.dot(o_low, wo, preferred_element_type=jnp.float32)
    attn = lax.psum(attn_terms, "tensor")
    h_full = x_full + attn
    r_moe = lax.rsqrt(jnp.mean(h_full * h_full, axis=-1, keepdims=True) + epsilon)
    h_hat = h_full * r_moe
    gain_two = g_moe.astype(jnp.float32)
    a_low = (h_hat * gain_two).astype(jnp.bfloat16)
    logits = jnp.dot(a_low, wr, preferred_element_type=jnp.float32)
    chosen = jnp.take_along_axis(logits, picks, axis=1)
    gates = jax.nn.softmax(chosen, axis=-1)
    top_count = picks.shape[1]
    experts_all = wr.shape[1]
    capacity = 9 * tok_count * top_count // (8 * experts_all)
    table, destination = slot_table(picks, drop_order.reshape(-1), experts_all, capacity)
    slot_tokens = table // top_count
    local_count = expert_gate.shape[0]
    h_cols = lax.dynamic_slice_in_dim(h_full, col_start, col_width, 1)
    d_out = cotangent.astype(jnp.float32)
    d_out_cols = lax.dynamic_slice_in_dim(d_out, col_start, col_width, 1)
    send_rows = jnp.concatenate([a_low, jnp.zeros((1, width), jnp.bfloat16)], axis=0)[slot_tokens]
    expert_in = lax.all_to_all(
        send_rows.reshape(ranks_dp, -1, width), "dp", split_axis=0, concat_axis=0, tiled=True
    )
    expert_in = expert_in.reshape(ranks_dp, local_count, capacity, width)
    gate_val = jnp.einsum(
        "sjcd,jdf->sjcf", expert_in, expert_gate, preferred_element_type=jnp.float32
    )
    up_val = jnp.einsum("sjcd,jdf->sjcf", expert_in, expert_up, preferred_element_type=jnp.float32)
    sigmoid_gate = jax.nn.sigmoid(gate_val)
    silu_gate = gate_val * sigmoid_gate
    hidden_low = (silu_gate * up_val).astype(jnp.bfloat16)
    slab_count = 4
    slab_rows = ranks_dp // slab_count
    out_pieces = []
    for slab_index in range(slab_count):
        lower = slab_index * slab_rows
        partial_out = jnp.einsum(
            "sjcf,jfd->sjcd",
            hidden_low[lower : lower + slab_rows],
            expert_down,
            preferred_element_type=jnp.float32,
        )
        out_pieces.append(
            lax.psum_scatter(
                partial_out.astype(jnp.bfloat16), "tensor", scatter_dimension=3, tiled=True
            )
        )
    expert_out = jnp.concatenate(out_pieces, axis=0).reshape(
        ranks_dp, local_count * capacity, col_width
    )
    returned = lax.all_to_all(expert_out, "dp", split_axis=0, concat_axis=0, tiled=True).reshape(
        experts_all * capacity, col_width
    )
    returned = jnp.concatenate([returned, jnp.zeros((1, col_width), jnp.bfloat16)], axis=0)
    pair_outs = returned[destination].reshape(tok_count, top_count, col_width).astype(jnp.float32)
    mixed = (h_cols + jnp.sum(gates[:, :, None] * pair_outs, axis=1)).astype(jnp.bfloat16)
    d_gate_terms = jnp.sum(pair_outs * d_out_cols[:, None, :], axis=2)
    d_pairs = (
        (gates[:, :, None] * d_out_cols[:, None, :]).astype(jnp.bfloat16).reshape(-1, col_width)
    )
    d_pairs = jnp.concatenate([d_pairs, jnp.zeros((1, col_width), jnp.bfloat16)], axis=0)
    d_send = d_pairs[table].reshape(ranks_dp, local_count * capacity, col_width)
    d_arrived = lax.all_to_all(d_send, "dp", split_axis=0, concat_axis=0, tiled=True)
    d_arrived = d_arrived.reshape(ranks_dp, local_count, capacity, col_width)
    grad_expert_gate = jnp.zeros(expert_gate.shape, jnp.float32)
    grad_expert_up = jnp.zeros(expert_up.shape, jnp.float32)
    grad_expert_down = jnp.zeros(expert_down.shape, jnp.float32)
    back_pieces = []
    for slab_index in range(slab_count):
        lower = slab_index * slab_rows
        upper = lower + slab_rows
        d_expert_out = lax.all_gather(d_arrived[lower:upper], "tensor", axis=3, tiled=True)
        d_hidden = jnp.einsum(
            "sjcd,jfd->sjcf", d_expert_out, expert_down, preferred_element_type=jnp.float32
        )
        grad_expert_down = grad_expert_down + jnp.einsum(
            "sjcf,sjcd->jfd",
            hidden_low[lower:upper],
            d_expert_out,
            preferred_element_type=jnp.float32,
        )
        slab_gate = gate_val[lower:upper]
        slab_sigmoid = sigmoid_gate[lower:upper]
        d_gate_low = (
            d_hidden * up_val[lower:upper] * slab_sigmoid * (1.0 + slab_gate * (1.0 - slab_sigmoid))
        ).astype(jnp.bfloat16)
        d_up_low = (d_hidden * silu_gate[lower:upper]).astype(jnp.bfloat16)
        slab_inputs = expert_in[lower:upper]
        grad_expert_gate = grad_expert_gate + jnp.einsum(
            "sjcd,sjcf->jdf", slab_inputs, d_gate_low, preferred_element_type=jnp.float32
        )
        grad_expert_up = grad_expert_up + jnp.einsum(
            "sjcd,sjcf->jdf", slab_inputs, d_up_low, preferred_element_type=jnp.float32
        )
        d_in_terms = jnp.einsum(
            "sjcf,jdf->sjcd", d_gate_low, expert_gate, preferred_element_type=jnp.float32
        ) + jnp.einsum("sjcf,jdf->sjcd", d_up_low, expert_up, preferred_element_type=jnp.float32)
        back_pieces.append(
            lax.psum_scatter(
                d_in_terms.astype(jnp.bfloat16), "tensor", scatter_dimension=3, tiled=True
            )
        )
    d_expert_in = jnp.concatenate(back_pieces, axis=0).reshape(
        ranks_dp, local_count * capacity, col_width
    )
    d_returned = lax.all_to_all(d_expert_in, "dp", split_axis=0, concat_axis=0, tiled=True).reshape(
        experts_all * capacity, col_width
    )
    d_returned = jnp.concatenate([d_returned, jnp.zeros((1, col_width), jnp.bfloat16)], axis=0)
    d_token_cols = jnp.sum(
        d_returned[destination].reshape(tok_count, top_count, col_width).astype(jnp.float32), axis=1
    )
    d_experts_full, d_gate_parts = (
        lax.all_gather(d_token_cols.astype(jnp.bfloat16), "tensor", axis=1, tiled=True).astype(
            d_token_cols.dtype
        ),
        lax.all_gather(d_gate_terms.astype(jnp.bfloat16), "tensor", axis=1, tiled=True).astype(
            d_gate_terms.dtype
        ),
    )
    d_gates = jnp.sum(d_gate_parts.reshape(tok_count, -1, top_count), axis=1)
    d_chosen = gates * (d_gates - jnp.sum(gates * d_gates, axis=-1, keepdims=True))
    one_hot = (picks[:, :, None] == jnp.arange(experts_all, dtype=jnp.int32)[None, None, :]).astype(
        jnp.float32
    )
    d_logits = jnp.sum(d_chosen[:, :, None] * one_hot, axis=1).astype(jnp.bfloat16)
    grad_router = jnp.dot(a_low.T, d_logits, preferred_element_type=jnp.float32)
    d_norm_moe = d_experts_full + jnp.dot(d_logits, wr.T, preferred_element_type=jnp.float32)
    grad_gain_moe = jnp.sum(d_norm_moe * h_hat, axis=0)
    d_scaled = d_norm_moe * gain_two
    d_h = d_out + r_moe * (d_scaled - h_hat * jnp.mean(d_scaled * h_hat, axis=-1, keepdims=True))
    d_h_low = d_h.astype(jnp.bfloat16)
    grad_out = jnp.dot(o_low.T, d_h_low, preferred_element_type=jnp.float32)
    d_heads = jnp.dot(d_h_low, wo.T, preferred_element_type=jnp.float32).astype(jnp.bfloat16)
    d_blocks = d_heads.reshape(block_count, block_rows, kv_heads, group_repeats, HEAD_SIZE)

    def backward_block(inputs):
        q_block, d_block, log_block, seg_block, pos_block = inputs
        scores = masked_scores(q_block, seg_block, pos_block)
        probs = jnp.exp(scores - log_block)
        d_probs = jnp.einsum(
            "qgrd,kgd->grqk", d_block, value_reduced, preferred_element_type=jnp.float32
        )
        centre = jnp.sum(probs * d_probs, axis=-1, keepdims=True)
        d_scores = (probs * (d_probs - centre)).astype(jnp.bfloat16)
        d_query = (
            jnp.einsum("grqk,kgd->qgrd", d_scores, key_rotated, preferred_element_type=jnp.float32)
            * score_scale
        )
        d_key = (
            jnp.einsum("grqk,qgrd->kgd", d_scores, q_block, preferred_element_type=jnp.float32)
            * score_scale
        )
        d_value = jnp.einsum(
            "grqk,qgrd->kgd",
            probs.astype(jnp.bfloat16),
            d_block,
            preferred_element_type=jnp.float32,
        )
        return (d_query, d_key, d_value)

    d_query_all, d_key_parts, d_value_parts = lax.map(
        backward_block, (q_blocks, d_blocks, log_totals, seg_blocks, pos_blocks)
    )
    d_query_low = unrotate_pairs(
        d_query_all.reshape(tok_count, q_heads, HEAD_SIZE), cosine_values, sine_values
    )
    d_query_low = d_query_low.astype(jnp.bfloat16).reshape(tok_count, q_heads * HEAD_SIZE)
    d_key_low = unrotate_pairs(jnp.sum(d_key_parts, axis=0), cosine_values, sine_values)
    d_key_low = d_key_low.astype(jnp.bfloat16).reshape(tok_count, kv_heads * HEAD_SIZE)
    d_value_low = (
        jnp.sum(d_value_parts, axis=0).astype(jnp.bfloat16).reshape(tok_count, kv_heads * HEAD_SIZE)
    )
    grad_query = jnp.dot(x_low.T, d_query_low, preferred_element_type=jnp.float32)
    grad_key = jnp.dot(x_low.T, d_key_low, preferred_element_type=jnp.float32)
    grad_value = jnp.dot(x_low.T, d_value_low, preferred_element_type=jnp.float32)
    d_norm_terms = (
        jnp.dot(d_query_low, wq.T, preferred_element_type=jnp.float32)
        + jnp.dot(d_key_low, wk.T, preferred_element_type=jnp.float32)
        + jnp.dot(d_value_low, wv.T, preferred_element_type=jnp.float32)
    )
    d_norm_attn = lax.psum(d_norm_terms.astype(jnp.bfloat16), "tensor").astype(jnp.float32)
    grad_gain_attn = jnp.sum(d_norm_attn * x_hat, axis=0)
    d_scaled_in = d_norm_attn * gain_one
    d_input = d_h + r_attn * (
        d_scaled_in - x_hat * jnp.mean(d_scaled_in * x_hat, axis=-1, keepdims=True)
    )
    grad_tokens = lax.dynamic_slice_in_dim(d_input, col_start, col_width, 1)
    grad_query, grad_key, grad_value, grad_out, grad_router, grad_gain_attn, grad_gain_moe = (
        lax.psum_scatter(grad_query, "dp", scatter_dimension=0, tiled=True),
        lax.psum_scatter(grad_key, "dp", scatter_dimension=0, tiled=True),
        lax.psum_scatter(grad_value, "dp", scatter_dimension=0, tiled=True),
        lax.psum_scatter(grad_out, "dp", scatter_dimension=1, tiled=True),
        lax.psum_scatter(grad_router, "dp", scatter_dimension=0, tiled=True),
        lax.psum_scatter(grad_gain_attn, "dp", scatter_dimension=0, tiled=True),
        lax.psum_scatter(grad_gain_moe, "dp", scatter_dimension=0, tiled=True),
    )
    return (
        mixed,
        grad_tokens,
        grad_query,
        grad_key,
        grad_value,
        grad_out,
        grad_router,
        grad_gain_attn,
        grad_gain_moe,
        grad_expert_gate,
        grad_expert_up,
        grad_expert_down,
    )


def mm(a, b):
    return jnp.dot(a, b, preferred_element_type=F32)


def mm_nt(a, b):
    return lax.dot_general(a, b, (((1,), (1,)), ((), ())), preferred_element_type=F32)


def mm_tn(a, b):
    return lax.dot_general(a, b, (((0,), (0,)), ((), ())), preferred_element_type=F32)


def kernel_call(body, outs, ins, scratch=(), flops=0, name=None):
    smem = pl.BlockSpec(memory_space=pltpu.SMEM)
    vmem = pl.BlockSpec(memory_space=pltpu.VMEM)
    nbytes = sum(int(np.prod(a.shape)) * a.dtype.itemsize for a in list(ins[1:]) + list(outs))
    return pl.pallas_call(
        body,
        out_shape=[jax.ShapeDtypeStruct(o.shape, o.dtype) for o in outs],
        in_specs=[smem] + [vmem] * (len(ins) - 1),
        out_specs=[vmem] * len(outs),
        scratch_shapes=list(scratch),
        compiler_params=pltpu.CompilerParams(vmem_limit_bytes=VMEM_LIMIT),
        cost_estimate=pl.CostEstimate(flops=int(flops), bytes_accessed=int(nbytes), transcendentals=0),
        name=name,
    )(*ins)


def sds(shape, dtype):
    return jax.ShapeDtypeStruct(shape, dtype)


def slots_body(capacity, idx, picks_ref, order_ref, pos_ref):
    experts, tok = pos_ref.shape
    ids = lax.broadcasted_iota(jnp.int32, (experts, tok), 0)
    never = 1 << 28
    order = jnp.full((experts, tok), never, jnp.int32)
    for k in range(picks_ref.shape[0]):
        order = jnp.where(picks_ref[k : k + 1, :] == ids, order_ref[k : k + 1, :], order)
    limit = jnp.zeros((experts, 1), jnp.int32)
    step = 1
    while step < picks_ref.shape[0] * tok:
        step *= 2
    while step:
        tried = limit + step
        count = jnp.sum((order < tried).astype(F32), axis=1, keepdims=True)
        limit = jnp.where(count <= capacity, tried, limit)
        step //= 2
    kept = order < limit
    rows = lax.broadcasted_iota(jnp.int32, (tok, tok), 0)
    cols = lax.broadcasted_iota(jnp.int32, (tok, tok), 1)
    before = (rows < cols).astype(F32).astype(BF16)
    place = mm(kept.astype(F32).astype(BF16), before)
    pos_ref[...] = jnp.where(kept, place, jnp.where(order < never, -1.0, -2.0)).astype(BF16)


def place_body(nz, idx, *refs):
    out = refs[-1]
    rows = refs[0].shape[0]
    for k in range(nz):
        base = lax.rem(idx[1] - k + nz, nz) * 2
        for q in range(2):
            block = base + (idx[2] if q == 0 else 1 - idx[2])
            out[pl.ds(pl.multiple_of(block * rows, rows), rows), :] = refs[q * nz + k][...]


def rotate(v, cos, sin, lane_low):
    swapped = jnp.where(lane_low, pltpu.roll(v, 96, 1), pltpu.roll(v, 32, 1))
    return v * cos + swapped * sin


def low_lanes(tok):
    return lax.rem(lax.broadcasted_iota(jnp.int32, (tok, 128), 1), 64) < 32


def attend_body(nz, idx, *refs):
    blocks = refs[: 2 * nz]
    x_ref, seg_row, seg_col, cos_ref, sin_ref = refs[2 * nz : 2 * nz + 5]
    o_ref, q_ref, k_ref, v_ref, p_ref, w_ref, aux_ref, bias_ref, qkv_ref = refs[2 * nz + 5 :]
    place_body(nz, idx, *blocks, w_ref)
    tok, width = x_ref.shape
    qd, kd = q_ref.shape[1], k_ref.shape[1]
    used = qd + 2 * kd
    aux = w_ref[:, used:].astype(F32).T
    aux_ref[...] = aux.astype(BF16)
    x = x_ref[...].astype(F32)
    r1 = lax.rsqrt(jnp.mean(x * x, axis=1, keepdims=True) + epsilon)
    x_low = (x * r1 * aux[64:65, :]).astype(BF16)
    qkv_ref[...] = mm(x_low, w_ref[:, :used])
    lanes = low_lanes(tok)
    cos, sin = cos_ref[...], sin_ref[...]
    for b in range(qd // 128):
        rot = rotate(qkv_ref[:, b * 128 : b * 128 + 128], cos, sin, lanes).astype(BF16)
        q_ref[:, b * 128 : b * 128 + 128] = (rot.astype(F32) * HEAD_SIZE**-0.5).astype(BF16)
    for b in range(kd // 128):
        rot = rotate(qkv_ref[:, qd + b * 128 : qd + b * 128 + 128], cos, sin, lanes)
        k_ref[:, b * 128 : b * 128 + 128] = rot.astype(BF16)
    v_ref[...] = qkv_ref[:, qd + kd :].astype(BF16)
    rows = lax.broadcasted_iota(jnp.int32, (tok, tok), 0)
    cols = lax.broadcasted_iota(jnp.int32, (tok, tok), 1)
    allowed = (seg_col[...] == seg_row[...]) & (cols <= rows)
    bias_ref[...] = jnp.where(allowed, 0.0, negative_big)
    heads, groups = qd // HEAD_SIZE, kd // HEAD_SIZE
    for h in range(heads):
        g = h // (heads // groups)
        a, b = h * HEAD_SIZE, g * HEAD_SIZE
        s = mm_nt(q_ref[:, a : a + HEAD_SIZE], k_ref[:, b : b + HEAD_SIZE]) + bias_ref[...]
        e = jnp.exp(s - jnp.max(s, axis=1, keepdims=True))
        p = (e / jnp.sum(e, axis=1, keepdims=True)).astype(BF16)
        p_ref[h] = p
        o_ref[:, a : a + HEAD_SIZE] = mm(p, v_ref[:, b : b + HEAD_SIZE]).astype(BF16)


def column_blocks(idx):
    x, c = idx[3], idx[4]
    own = [c, 2 + 2 * x + c, 2 + 2 * (1 - x) + c]
    return own, [1 - c, 2 + 2 * x + 1 - c, 2 + 2 * (1 - x) + 1 - c]


def out_body(idx, x_ref, o0, o1, o23, w0, w1, w23, aux_ref, h_ref, low_ref, own_ref, ring_ref):
    attn = mm_nt(o0[...], w0[...]) + mm_nt(o1[...], w1[...])
    attn = attn + (mm_nt(o23[0], w23[0]) + mm_nt(o23[1], w23[1]))
    h = x_ref[...].astype(F32) + attn
    h_ref[...] = h
    r2 = lax.rsqrt(jnp.mean(h * h, axis=1, keepdims=True) + epsilon)
    low_ref[...] = (h * r2 * aux_ref[64:66, :].astype(F32)[1:2, :]).astype(BF16)
    own, _ = column_blocks(idx)
    for m in range(3):
        block = low_ref[:, pl.ds(pl.multiple_of(own[m] * BLK, BLK), BLK)]
        own_ref[:, m * BLK : m * BLK + BLK] = block
        if m < 2:
            ring_ref[:, m * BLK : m * BLK + BLK] = block


def masked_gates(logits, pos):
    picked = pos > -1.5
    shown = jnp.where(picked, logits, negative_big)
    e = jnp.where(picked, jnp.exp(shown - jnp.max(shown, axis=0, keepdims=True)), 0.0)
    return e / jnp.sum(e, axis=0, keepdims=True)


def split16(v):
    high = v.astype(BF16)
    return high, (v - high.astype(F32)).astype(BF16)


def experts_body(
    local, idx, am_ref, an_ref, dm_ref, dn_ref, gu_ref, down_ref, aux_ref, sel_ref, selt_ref, slot_ref, slott_ref,
    dxm_ref, dxn_ref, ym_ref, yn_ref, xe_ref, dy_ref, dgu_ref, hd_ref,
    pos_s, gate_s, d0_s, acc_s, acc2_s, dgr_s, oh_s, oht_s,
):
    tok = am_ref.shape[1]
    half = pos_s.shape[0] // 2
    c = idx[4]
    mine, theirs = column_blocks(idx)
    parts = list(zip(mine + theirs, [0, 1, 2] * 2, [0] * 3 + [1] * 3))
    hidden = down_ref.shape[1]
    sel, selt = sel_ref[...], selt_ref[...]
    for q in range(2):
        pos_s[pl.ds(pl.multiple_of(c * half, half), half), :] = dm_ref[q, tok:, :tok]
        pos_s[pl.ds(pl.multiple_of((1 - c) * half, half), half), :] = dn_ref[q, tok:, :tok]
        pos = pos_s[...]
        logits = jnp.zeros(pos.shape, F32)
        for b, m, side in parts:
            rows = (an_ref if side else am_ref)[q, :, m * BLK : m * BLK + BLK]
            router = aux_ref[: pos.shape[0], pl.ds(pl.multiple_of(b * BLK, BLK), BLK)]
            logits = logits + mm_nt(router, rows)
        gates = masked_gates(logits, pos.astype(F32))
        hot = (mm(sel, pos) == slot_ref[...]).astype(F32).astype(BF16)
        oh_s[q] = hot
        oht_s[q] = (mm_tn(pos, selt) == slott_ref[...]).astype(F32).astype(BF16)
        high, low = split16(gates)
        spread = (mm_nt(hot, high) + mm_nt(hot, low)) * sel.astype(F32)
        gate = jnp.sum(spread, axis=1, keepdims=True)
        gate_s[:, q] = gate.reshape(local, PAD, 1)
        for b, m, side in parts:
            rows = (an_ref if side else am_ref)[q, :, m * BLK : m * BLK + BLK]
            xe_ref[b, :, q] = mm(hot, rows).astype(BF16).reshape(local, PAD, BLK)
            rows = (dn_ref if side else dm_ref)[q, :tok, m * BLK : m * BLK + BLK]
            got = mm(hot, rows)
            d0_s[b, :, q] = got.astype(BF16).reshape(local, PAD, BLK)
            dy_ref[b, :, q] = (got * gate).astype(BF16).reshape(local, PAD, BLK)
    blocks = xe_ref.shape[0]
    both = 2 * PAD
    for j in range(local):
        gu = jnp.zeros((both, 2 * hidden), F32)
        t = jnp.zeros((both, hidden), F32)
        for b in range(blocks):
            gu = gu + mm(xe_ref[b, j].reshape(both, BLK), gu_ref[j, b * BLK : b * BLK + BLK, :])
            t = t + mm_nt(d0_s[b, j].reshape(both, BLK), down_ref[j, :, b * BLK : b * BLK + BLK])
        gate = gate_s[:, :][j].reshape(both, 1)
        g, u = gu[:, :hidden], gu[:, hidden:]
        sg = jax.nn.sigmoid(g)
        silu = g * sg
        hd = (silu * u).astype(BF16)
        dhd = gate * t
        dg = (dhd * u * sg * (1.0 + g * (1.0 - sg))).astype(BF16)
        du = (dhd * silu).astype(BF16)
        dgate = jnp.sum(hd.astype(F32) * t, axis=1, keepdims=True)
        dgr_s[j] = jnp.broadcast_to(dgate, (both, dgr_s.shape[3])).reshape(2, PAD, dgr_s.shape[3])
        hd_ref[j] = hd.reshape(2, PAD, hidden)
        dgu_ref[j, :, :, :hidden] = dg.reshape(2, PAD, hidden)
        dgu_ref[j, :, :, hidden:] = du.reshape(2, PAD, hidden)
        dgu = jnp.concatenate([dg, du], axis=1)
        for b in range(blocks):
            y = mm(hd, down_ref[j, :, b * BLK : b * BLK + BLK])
            acc_s[b, j] = (y.astype(BF16).astype(F32) * gate).astype(BF16).reshape(2, PAD, BLK)
            dx = mm_nt(dgu, gu_ref[j, b * BLK : b * BLK + BLK, :])
            acc2_s[b, j] = dx.astype(BF16).reshape(2, PAD, BLK)
    slots = local * PAD
    x = idx[3]
    for q in range(2):
        hot, hott = oh_s[q], oht_s[q]
        for b, m, side in parts:
            dx = mm(hott, acc2_s[b, :, q].reshape(slots, BLK)).astype(BF16)
            (dxn_ref if side else dxm_ref)[q, :tok, m * BLK : m * BLK + BLK] = dx
            y = mm(hott, acc_s[b, :, q].reshape(slots, BLK)).astype(BF16)
            (yn_ref if side else ym_ref)[q, :, m * BLK : m * BLK + BLK] = y
        weights = (dgr_s[:, :, :, :][:, q].reshape(slots, -1) * sel.astype(F32)).astype(BF16)
        pos_s[...] = mm_tn(weights, hot).astype(BF16)
        for ref, at in ((dxm_ref, c), (dxn_ref, 1 - c)):
            got = pos_s[pl.ds(pl.multiple_of(at * half, half), half), :]
            ref[q, tok:, :BLK] = got[:, :BLK]
            ref[q, tok:, BLK : 2 * BLK] = (got[:, BLK:].astype(F32) * (1 - x).astype(F32)).astype(BF16)
            ref[q, tok:, 2 * BLK :] = (got[:, BLK:].astype(F32) * x.astype(F32)).astype(BF16)


def hidden_back_body(idx, fm_ref, fn_ref, h_ref, low_ref, aux_ref, pos_ref, dout_ref, o_ref, w_ref,
                     dh_ref, do_ref, rs_ref, full_s, dg_s):
    tok, width = h_ref.shape
    c, experts = idx[4], pos_ref.shape[0]
    half = experts // 2
    mine, theirs = column_blocks(idx)
    for ref, order in ((fm_ref, mine), (fn_ref, theirs)):
        for m in range(3):
            at = pl.ds(pl.multiple_of(order[m] * BLK, BLK), BLK)
            full_s[:, at] = ref[:tok, m * BLK : m * BLK + BLK].astype(F32)
    for ref, at in ((fm_ref, c), (fn_ref, 1 - c)):
        at = pl.ds(pl.multiple_of(at * half, half), half)
        dg_s[at, :BLK] = ref[tok:, :BLK].astype(F32)
        dg_s[at, BLK:] = ref[tok:, BLK : 2 * BLK].astype(F32) + ref[tok:, 2 * BLK :].astype(F32)
    low = low_ref[...]
    router = aux_ref[:experts, :]
    gates = masked_gates(mm_nt(router, low), pos_ref[...].astype(F32))
    dgates = dg_s[...]
    dlogits = (gates * (dgates - jnp.sum(gates * dgates, axis=0, keepdims=True))).astype(BF16)
    h = h_ref[...]
    r2 = lax.rsqrt(jnp.mean(h * h, axis=1, keepdims=True) + epsilon)
    ah = h * r2
    da = full_s[...] + mm_tn(dlogits, router)
    gain_grad = jnp.sum(da * ah, axis=0, keepdims=True)
    scaled = da * aux_ref[64:66, :].astype(F32)[1:2, :]
    dh = dout_ref[...].astype(F32) + r2 * (scaled - ah * jnp.mean(scaled * ah, axis=1, keepdims=True))
    full_s[...] = dh
    cols = dh_ref.shape[1]
    t = idx[3] * 2 + c
    dh_ref[...] = full_s[:, pl.ds(pl.multiple_of(t * cols, 128), cols)]
    dhb = dh.astype(BF16)
    do_ref[...] = mm(dhb, w_ref[...]).astype(BF16)
    rs_ref[:, :cols] = mm_tn(dhb, o_ref[...]).astype(BF16)
    side = jnp.concatenate([mm(dlogits, low), gain_grad, jnp.zeros((63, width), F32)], axis=0)
    rs_ref[:, cols:] = side.T.astype(BF16)


def attend_back_body(idx, do_ref, p_ref, q_ref, k_ref, v_ref, w_ref, x_ref, aux_ref, cos_ref, sin_ref,
                     rs_ref, dm_ref, dn_ref, dq_s, dqkv_s, dxn_s):
    tok, width = x_ref.shape
    qd, kd = q_ref.shape[1], k_ref.shape[1]
    heads, groups = qd // HEAD_SIZE, kd // HEAD_SIZE
    scale = HEAD_SIZE**-0.5
    each = heads // groups
    for g in range(groups):
        b = g * HEAD_SIZE
        kg, vg = k_ref[:, b : b + HEAD_SIZE], v_ref[:, b : b + HEAD_SIZE]
        dk = jnp.zeros((tok, HEAD_SIZE), F32)
        dv = jnp.zeros((tok, HEAD_SIZE), F32)
        for h in range(g * each, (g + 1) * each):
            a = h * HEAD_SIZE
            doh = do_ref[:, a : a + HEAD_SIZE]
            p = p_ref[h].astype(F32)
            dp = mm_nt(doh, vg)
            ds = (p * (dp - jnp.sum(p * dp, axis=1, keepdims=True))).astype(BF16)
            dq_s[:, a : a + HEAD_SIZE] = mm(ds, kg) * scale
            dk = dk + mm_tn(ds, q_ref[:, a : a + HEAD_SIZE])
            dv = dv + mm_tn(p_ref[h], doh)
        dq_s[:, qd + b : qd + b + HEAD_SIZE] = dk
        dqkv_s[:, qd + kd + b : qd + kd + b + HEAD_SIZE] = dv.astype(BF16)
    lanes = low_lanes(tok)
    cos, sin = cos_ref[...], -sin_ref[...]
    for b in range((qd + kd) // 128):
        at = slice(b * 128, b * 128 + 128)
        dqkv_s[:, at] = rotate(dq_s[:, at], cos, sin, lanes).astype(BF16)
    used = qd + 2 * kd
    x = x_ref[...].astype(F32)
    r1 = lax.rsqrt(jnp.mean(x * x, axis=1, keepdims=True) + epsilon)
    xh = x * r1
    gain = aux_ref[64:65, :].astype(F32)
    x_low = (xh * gain).astype(BF16)
    dqkv = dqkv_s[...]
    rows = width // rs_ref.shape[0]
    grads = mm_tn(x_low, dqkv).astype(BF16)
    dxn = mm_nt(dqkv, w_ref[:, :used])
    gain_high, gain_low = split16(jnp.sum(dxn * xh, axis=0, keepdims=True))
    pads = jnp.zeros((14, rows), BF16)
    for i in range(rs_ref.shape[0]):
        rs_ref[i, :rows, :] = grads[i * rows : i * rows + rows, :]
        at = slice(i * rows, i * rows + rows)
        tail = jnp.concatenate([gain_high[:, at].astype(F32), gain_low[:, at].astype(F32), pads.astype(F32)], axis=0)
        rs_ref[i, rows:, :] = jnp.zeros((16, used), BF16)
        rs_ref[i, rows:, :rows] = tail.astype(BF16)
    total = jnp.sum(dxn * xh * gain, axis=1, keepdims=True)
    high, low = split16(total)
    lane = lax.broadcasted_iota(jnp.int32, (tok, 128), 1)
    side = jnp.where(lane == 0, high.astype(F32), jnp.where(lane == 1, low.astype(F32), 0.0)).astype(BF16)
    cols = width // 4
    for i in range(4):
        dxn_s[i] = dxn[:, i * cols : i * cols + cols].astype(BF16)
    ix, c = idx[3], idx[4]
    for ref, core in ((dm_ref, c), (dn_ref, 1 - c)):
        ref[:, :cols] = dxn_s[2 * ix + core]
        ref[:, cols : 2 * cols] = dxn_s[2 * (1 - ix) + core]
        ref[:, 2 * cols :] = side


def mixed_body(idx, fm_ref, fn_ref, h_ref, out_ref, full_s):
    mine, theirs = column_blocks(idx)
    for ref, order in ((fm_ref, mine), (fn_ref, theirs)):
        for m in range(3):
            at = pl.ds(pl.multiple_of(order[m] * BLK, BLK), BLK)
            full_s[:, at] = ref[:, m * BLK : m * BLK + BLK].astype(F32)
    cols = out_ref.shape[1]
    at = pl.ds(pl.multiple_of((idx[3] * 2 + idx[4]) * cols, 128), cols)
    out_ref[...] = (full_s[:, at] + h_ref[:, at]).astype(BF16)


def expert_grads_body(count, *refs):
    xe, dy, dgu, hd = (refs[i * count : i * count + count] for i in range(4))
    gate_ref, up_ref, down_ref = refs[4 * count :]
    hidden = gate_ref.shape[2]
    rows = 2 * PAD

    def join(group, b=None):
        got = [(r[0] if b is None else r[b, 0]) for r in group]
        return jnp.concatenate([v.reshape(rows, v.shape[-1]) for v in got], axis=0)

    d_gu, hd_all = join(dgu), join(hd)
    for b in range(xe[0].shape[0]):
        at = slice(b * BLK, b * BLK + BLK)
        both = mm_tn(join(xe, b), d_gu)
        gate_ref[0, at, :] = both[:, :hidden]
        up_ref[0, at, :] = both[:, hidden:]
        down_ref[0, :, at] = mm_tn(hd_all, join(dy, b))


def expert_grads(xe, dy, dgu, hd, local, width, hidden):
    count = len(xe)
    blocks = width // BLK
    wide = pl.BlockSpec((blocks, 1, 2, PAD, BLK), lambda e: (0, e, 0, 0, 0))
    specs = [wide] * (2 * count)
    specs += [pl.BlockSpec((1, 2, PAD, 2 * hidden), lambda e: (e, 0, 0, 0))] * count
    specs += [pl.BlockSpec((1, 2, PAD, hidden), lambda e: (e, 0, 0, 0))] * count
    slots = count * 2 * PAD * local
    return pl.pallas_call(
        functools.partial(expert_grads_body, count),
        grid=(local,),
        out_shape=[sds((local, width, hidden), F32), sds((local, width, hidden), F32), sds((local, hidden, width), F32)],
        in_specs=specs,
        out_specs=[pl.BlockSpec((1, width, hidden), lambda e: (e, 0, 0))] * 2
        + [pl.BlockSpec((1, hidden, width), lambda e: (e, 0, 0))],
        compiler_params=pltpu.CompilerParams(vmem_limit_bytes=VMEM_LIMIT),
        cost_estimate=pl.CostEstimate(
            flops=6 * slots * width * hidden, bytes_accessed=slots * width * 4 + 12 * local * width * hidden, transcendentals=0
        ),
        name="expert_grads",
    )(*xe, *dy, *dgu, *hd)


def add16(a, b):
    return (a.astype(F32) + b.astype(F32)).astype(BF16)


def on_device_gathered(
    tokens,
    document_numbers,
    picks,
    drop_order,
    w_query,
    key_matrix,
    value_matrix,
    w_out,
    w_router,
    gain_attn,
    gain_moe,
    expert_gate,
    expert_up,
    expert_down,
    cotangent,
):
    n_dp = lax.axis_size("dp")
    nz = n_dp // 2
    r, t = lax.axis_index("dp"), lax.axis_index("tensor")
    z, y, x, c = r // 2, r % 2, t // 2, t % 2
    idx = jnp.stack([r, z, y, x, c]).astype(jnp.int32)

    def shift_z(v):
        return lax.ppermute(v, "dp", [(i, ((i // 2 + 1) % nz) * 2 + i % 2) for i in range(n_dp)])

    def swap_y(v):
        return lax.ppermute(v, "dp", [(i, i ^ 1) for i in range(n_dp)])

    def swap_x(v):
        return lax.ppermute(v, "tensor", [(i, i ^ 2) for i in range(4)])

    def swap_c(v):
        return lax.ppermute(v, "tensor", [(i, i ^ 1) for i in range(4)])

    def ring(v):
        zs = [v]
        for _ in range(nz - 1):
            zs.append(shift_z(zs[-1]))
        return zs, [swap_y(b) for b in zs]

    tok, width = tokens.shape
    rows = w_query.shape[0]
    qd, kd = w_query.shape[1], key_matrix.shape[1]
    used = qd + 2 * kd
    experts = w_router.shape[1]
    local, _, hidden = expert_gate.shape
    capacity = 9 * tok * picks.shape[1] // (8 * experts)
    cols = width // 4

    aux = jnp.concatenate(
        [w_router, gain_attn[:, None], gain_moe[:, None], jnp.zeros((rows, 128 - experts - 2), BF16)], axis=1
    )
    w_zs, w_ys = ring(jnp.concatenate([w_query, key_matrix, value_matrix, aux], axis=1))
    wo_zs, wo_ys = ring(w_out.T)

    pos = kernel_call(
        functools.partial(slots_body, capacity),
        [sds((experts, tok), BF16)],
        [idx, picks.T, drop_order.reshape(tok, -1).T],
        name="slots",
    )[0]

    half = experts // 2

    def columns(v, m):
        return lax.dynamic_slice_in_dim(v, m * BLK, BLK, 1)

    mine, _ = column_blocks(idx)
    d_own = jnp.concatenate([columns(cotangent, m) for m in mine], axis=1)
    pos_own = jnp.concatenate(
        [lax.dynamic_slice_in_dim(pos, c * half, half, 0), jnp.zeros((half, 3 * BLK - tok), BF16)], axis=1
    )
    d_own = jnp.concatenate([d_own, pos_own], axis=0)

    def gather(own, ring_own):
        zs, ys = ring(ring_own)
        got = []
        for k in range(nz):
            if k == 0:
                far = swap_x(ys[0][:, BLK:])
                m = jnp.stack([own, jnp.concatenate([ys[0], far], axis=1)])
            else:
                pair = jnp.stack([zs[k], ys[k]])
                far = swap_x(pair[:, :, BLK:])
                m = jnp.concatenate([pair, far], axis=2)
            got.append((m, swap_c(m)))
        return got

    d_all = gather(d_own, d_own[:, : 2 * BLK])

    positions = np.arange(tok, dtype=np.float32)
    inverse = rope_base ** (-(2.0 * np.arange(HEAD_SIZE // 2, dtype=np.float32)) / HEAD_SIZE)
    angles = positions[:, None] * inverse.astype(np.float32)[None, :]
    cos = jnp.asarray(np.tile(np.cos(angles), (1, 4)).astype(np.float32))
    sin = np.sin(angles)
    sin = jnp.asarray(np.tile(np.concatenate([-sin, sin], axis=1), (1, 2)).astype(np.float32))
    heads = qd // HEAD_SIZE
    seg_row = document_numbers.reshape(1, tok)
    o, q, k, v, p, w_all, aux_t = kernel_call(
        functools.partial(attend_body, nz),
        [sds((tok, qd), BF16), sds((tok, qd), BF16), sds((tok, kd), BF16), sds((tok, kd), BF16),
         sds((heads, tok, tok), BF16), sds((width, used + 128), BF16), sds((128, width), BF16)],
        [idx, *w_zs, *w_ys, tokens, seg_row, seg_row.T, cos, sin],
        scratch=[pltpu.VMEM((tok, tok), F32), pltpu.VMEM((tok, used), F32)],
        flops=4e9,
        name="attend",
    )
    wo = kernel_call(
        functools.partial(place_body, nz), [sds((width, qd), BF16)], [idx, *wo_zs, *wo_ys], name="place"
    )[0]
    wo_x = swap_x(wo)
    wo_c = swap_c(jnp.stack([wo, wo_x]))
    o_x = swap_x(o)
    o_c = swap_c(jnp.stack([o, o_x]))
    h, low, a_own, a_ring = kernel_call(
        out_body,
        [sds((tok, width), F32), sds((tok, width), BF16), sds((tok, 3 * BLK), BF16), sds((tok, 2 * BLK), BF16)],
        [idx, tokens, o, o_x, o_c, wo, wo_x, wo_c, aux_t],
        flops=5e9,
        name="out",
    )
    a_all = gather(a_own, a_ring)

    gu = jnp.concatenate([expert_gate, expert_up], axis=2)
    slot_ids = np.arange(local * PAD)
    sel = (r * local + slot_ids[:, None] // PAD == jnp.arange(experts)[None, :]).astype(BF16)
    slot_col = jnp.asarray((slot_ids % PAD).astype(np.float32)[:, None])
    slot_row = jnp.asarray((slot_ids % PAD).astype(np.float32)[None, :])
    slots = local * PAD
    blocks = width // BLK
    big = (blocks, local, 2, PAD, BLK)
    done = []
    for kk in range(nz):
        am, an = a_all[kk]
        dm, dn = d_all[kk]
        done.append(
            kernel_call(
                functools.partial(experts_body, local),
                [sds(dm.shape, BF16), sds(dm.shape, BF16), sds(am.shape, BF16), sds(am.shape, BF16),
                 sds(big, BF16), sds(big, BF16), sds((local, 2, PAD, 2 * hidden), BF16), sds((local, 2, PAD, hidden), BF16)],
                [idx, am, an, dm, dn, gu, expert_down, aux_t, sel, sel.T, slot_col, slot_row],
                scratch=[
                    pltpu.VMEM((experts, tok), BF16), pltpu.VMEM((local, 2, PAD, 1), F32), pltpu.VMEM(big, BF16),
                    pltpu.VMEM(big, BF16), pltpu.VMEM(big, BF16), pltpu.VMEM((local, 2, PAD, experts), F32),
                    pltpu.VMEM((2, slots, tok), BF16), pltpu.VMEM((2, tok, slots), BF16),
                ],
                flops=12e9,
                name="experts",
            )
        )

    def collect(parts):
        total = None
        for kk in list(range(1, nz)) + [0]:
            m, n = parts[kk]
            s = add16(m, swap_c(n))
            own = add16(s[:, :, BLK : 2 * BLK], swap_x(s[:, :, 2 * BLK :]))
            s = jnp.concatenate([s[:, :, :BLK], own], axis=2)
            s = add16(s[0], swap_y(s[1])) if total is None else (
                s[0].astype(F32) + swap_y(s[1]).astype(F32) + shift_z(total).astype(F32)
            ).astype(BF16)
            total = s
        far = swap_x(total)
        whole = jnp.concatenate([add16(total[:, :BLK], far[:, :BLK]), total[:, BLK:], far[:, BLK:]], axis=1)
        return whole, swap_c(whole)

    fm, fn = collect([d[0:2] for d in done])
    ym, yn = collect([d[2:4] for d in done])
    mixed = kernel_call(
        mixed_body, [sds((tok, cols), BF16)], [idx, ym, yn, h], scratch=[pltpu.VMEM((tok, width), F32)], name="mixed"
    )[0]

    def scatter_dp(v):
        def block(kk, yy):
            return lax.dynamic_index_in_dim(v, ((z - kk) % nz) * 2 + yy, 0, keepdims=False)

        total = None
        for kk in list(range(1, nz)) + [0]:
            s = block(kk, y).astype(F32) + swap_y(block(kk, 1 - y)).astype(F32)
            if total is not None:
                s = s + shift_z(total).astype(F32)
            total = s.astype(BF16)
        return s

    d_h, d_o, early = kernel_call(
        hidden_back_body,
        [sds((tok, cols), F32), sds((tok, qd), BF16), sds((width, qd + 128), BF16)],
        [idx, fm, fn, h, low, aux_t, pos, cotangent, o, wo],
        scratch=[pltpu.VMEM((tok, width), F32), pltpu.VMEM((experts, tok), F32)],
        flops=3e9,
        name="hidden_back",
    )
    early = scatter_dp(early.reshape(n_dp, rows, qd + 128))
    grad_out = early[:, :qd].T
    grad_router = early[:, qd : qd + experts]
    grad_gain_moe = early[:, qd + experts]
    late, dxm, dxn = kernel_call(
        attend_back_body,
        [sds((n_dp, rows + 16, used), BF16), sds((tok, 2 * cols + 128), BF16), sds((tok, 2 * cols + 128), BF16)],
        [idx, d_o, p, q, k, v, w_all, tokens, aux_t, cos, sin],
        scratch=[pltpu.VMEM((tok, used), F32), pltpu.VMEM((tok, used), BF16), pltpu.VMEM((4, tok, cols), BF16)],
        flops=5e9,
        name="attend_back",
    )
    late = scatter_dp(late)
    grad_query = late[:rows, :qd]
    grad_key = late[:rows, qd : qd + kd]
    grad_value = late[:rows, qd + kd :]
    gain_part = late[rows, :rows] + late[rows + 1, :rows]
    gain_part = gain_part + swap_c(gain_part)
    grad_gain_attn = gain_part + swap_x(gain_part)

    got = swap_c(dxn)
    ours = dxm.astype(F32) + got.astype(F32)
    mean_part = ours[:, 2 * cols] + ours[:, 2 * cols + 1]
    high, lowp = split16(mean_part)
    send = jnp.concatenate(
        [ours[:, cols : 2 * cols].astype(BF16), high[:, None], lowp[:, None], jnp.zeros((tok, 126), BF16)], axis=1
    )
    got = swap_x(send)
    d_norm = ours[:, :cols] + got[:, :cols].astype(F32)
    mean = (mean_part + got[:, cols].astype(F32) + got[:, cols + 1].astype(F32))[:, None] / width
    x_full = tokens.astype(F32)
    r1 = lax.rsqrt(jnp.mean(x_full * x_full, axis=-1, keepdims=True) + epsilon)
    x_cols = lax.dynamic_slice_in_dim(tokens, t * cols, cols, 1).astype(F32) * r1
    gain_row = lax.dynamic_slice_in_dim(aux_t[64:65], t * cols, cols, 1).astype(F32)
    grad_tokens = d_h + r1 * (d_norm * gain_row - x_cols * mean)

    grad_gate, grad_up, grad_down = expert_grads(
        [d[4] for d in done], [d[5] for d in done], [d[6] for d in done], [d[7] for d in done], local, width, hidden
    )
    return (
        mixed,
        grad_tokens,
        grad_query,
        grad_key,
        grad_value,
        grad_out,
        grad_router,
        grad_gain_attn,
        grad_gain_moe,
        grad_gate,
        grad_up,
        grad_down,
    )


def solution(mesh):
    few = mesh.shape["tensor"] == 4 and mesh.shape["dp"] in (4, 8)
    return jax.shard_map(
        on_device_gathered if few else on_device,
        mesh=mesh,
        in_specs=(
            P("dp", None),
            P("dp", None),
            P("dp", None),
            P("dp", None),
            P("dp", "tensor"),
            P("dp", "tensor"),
            P("dp", "tensor"),
            P("tensor", "dp"),
            P("dp", None),
            P("dp"),
            P("dp"),
            P("dp", None, "tensor"),
            P("dp", None, "tensor"),
            P("dp", "tensor", None),
            P("dp", None),
        ),
        out_specs=(
            P("dp", "tensor"),
            P("dp", "tensor"),
            P("dp", "tensor"),
            P("dp", "tensor"),
            P("dp", "tensor"),
            P("tensor", "dp"),
            P("dp", None),
            P("dp"),
            P("dp"),
            P("dp", None, "tensor"),
            P("dp", None, "tensor"),
            P("dp", "tensor", None),
        ),
        check_vma=False,
    )
```

```python
import functools

import jax
import jax.numpy as jnp
import numpy as np
from jax import lax
from jax.experimental import pallas as pl
from jax.experimental.pallas import tpu as pltpu
from jax.sharding import PartitionSpec as P

HEAD_SIZE = 64


epsilon = 1e-05
negative_big = -1e30
rope_base = 10000.0
F32 = jnp.float32
BF16 = jnp.bfloat16
BLK = 256
PAD = 80
VMEM_LIMIT = 62 * 1024 * 1024


def rotary_tables(positions, head_width):
    half_width = head_width // 2
    inverse = rope_base ** (-(2.0 * jnp.arange(half_width, dtype=jnp.float32)) / head_width)
    angles = positions.astype(jnp.float32)[:, None] * inverse[None, :]
    return (jnp.cos(angles)[:, None, :], jnp.sin(angles)[:, None, :])


def apply_pair_rotation(values, cosine_values, sine_values):
    half_width = values.shape[-1] // 2
    first_half = values[..., :half_width]
    second_half = values[..., half_width:]
    return jnp.concatenate(
        [
            first_half * cosine_values - second_half * sine_values,
            second_half * cosine_values + first_half * sine_values,
        ],
        axis=-1,
    )


def unrotate_pairs(values, cosine_values, sine_values):
    half_width = values.shape[-1] // 2
    first_half = values[..., :half_width]
    second_half = values[..., half_width:]
    return jnp.concatenate(
        [
            first_half * cosine_values + second_half * sine_values,
            second_half * cosine_values - first_half * sine_values,
        ],
        axis=-1,
    )


def slot_table(chosen_rows, order_row, expert_count, capacity):
    flat_experts = chosen_rows.reshape(-1)
    pair_count = flat_experts.shape[0]
    sort_keys = flat_experts * pair_count + order_row
    ordering = jnp.argsort(sort_keys)
    sorted_experts = flat_experts[ordering]
    expert_ids = jnp.arange(expert_count, dtype=jnp.int32)
    counts = jnp.sum(
        (flat_experts[:, None] == expert_ids[None, :]).astype(jnp.int32), axis=0, dtype=jnp.int32
    )
    starts = jnp.cumsum(counts, dtype=jnp.int32) - counts
    ranks_sorted = jnp.arange(pair_count, dtype=jnp.int32) - starts[sorted_experts]
    ranks = jnp.zeros((pair_count,), jnp.int32).at[ordering].set(ranks_sorted)
    destination = jnp.where(
        ranks < capacity, flat_experts * capacity + ranks, expert_count * capacity
    )
    table = jnp.full((expert_count * capacity + 1,), pair_count, jnp.int32)
    table = table.at[destination].set(jnp.arange(pair_count, dtype=jnp.int32))
    return (table[: expert_count * capacity], destination)


def on_device(
    tokens,
    document_numbers,
    picks,
    drop_order,
    w_query,
    key_matrix,
    value_matrix,
    w_out,
    w_router,
    gain_attn,
    gain_moe,
    expert_gate,
    expert_up,
    expert_down,
    cotangent,
):
    ranks_dp = lax.axis_size("dp")
    tensor_index = lax.axis_index("tensor")
    wq, wk, wv, wo, wr, g_attn, g_moe = (
        lax.all_gather(w_query, "dp", axis=0, tiled=True),
        lax.all_gather(key_matrix, "dp", axis=0, tiled=True),
        lax.all_gather(value_matrix, "dp", axis=0, tiled=True),
        lax.all_gather(w_out, "dp", axis=1, tiled=True),
        lax.all_gather(w_router, "dp", axis=0, tiled=True),
        lax.all_gather(gain_attn, "dp", axis=0, tiled=True),
        lax.all_gather(gain_moe, "dp", axis=0, tiled=True),
    )
    tok_count, width = tokens.shape
    col_width = width // lax.axis_size("tensor")
    col_start = tensor_index * col_width
    q_heads = wq.shape[1] // HEAD_SIZE
    kv_heads = wk.shape[1] // HEAD_SIZE
    group_repeats = q_heads // kv_heads
    score_scale = HEAD_SIZE ** (-0.5)
    seg_row = document_numbers.reshape(-1)
    positions = jnp.arange(tok_count, dtype=jnp.int32)
    cosine_values, sine_values = rotary_tables(positions, HEAD_SIZE)
    x_full = tokens.astype(jnp.float32)
    r_attn = lax.rsqrt(jnp.mean(x_full * x_full, axis=-1, keepdims=True) + epsilon)
    x_hat = x_full * r_attn
    gain_one = g_attn.astype(jnp.float32)
    x_low = (x_hat * gain_one).astype(jnp.bfloat16)
    q_proj = jnp.dot(x_low, wq, preferred_element_type=jnp.float32)
    key_projected = jnp.dot(x_low, wk, preferred_element_type=jnp.float32)
    value_projected = jnp.dot(x_low, wv, preferred_element_type=jnp.float32)
    query_rotated = apply_pair_rotation(
        q_proj.reshape(tok_count, q_heads, HEAD_SIZE), cosine_values, sine_values
    ).astype(jnp.bfloat16)
    query_rotated = query_rotated.reshape(tok_count, kv_heads, group_repeats, HEAD_SIZE)
    key_rotated = apply_pair_rotation(
        key_projected.reshape(tok_count, kv_heads, HEAD_SIZE), cosine_values, sine_values
    ).astype(jnp.bfloat16)
    value_reduced = value_projected.astype(jnp.bfloat16).reshape(tok_count, kv_heads, HEAD_SIZE)
    block_rows = min(512, tok_count)
    block_count = tok_count // block_rows
    q_blocks = query_rotated.reshape(block_count, block_rows, kv_heads, group_repeats, HEAD_SIZE)
    seg_blocks = seg_row.reshape(block_count, block_rows)
    pos_blocks = positions.reshape(block_count, block_rows)

    def masked_scores(q_block, seg_block, pos_block):
        raw_scores = (
            jnp.einsum("qgrd,kgd->grqk", q_block, key_rotated, preferred_element_type=jnp.float32)
            * score_scale
        )
        allowed = (seg_block[:, None] == seg_row[None, :]) & (
            positions[None, :] <= pos_block[:, None]
        )
        return jnp.where(allowed, raw_scores, negative_big)

    def forward_block(inputs):
        q_block, seg_block, pos_block = inputs
        scores = masked_scores(q_block, seg_block, pos_block)
        highest_score = jnp.max(scores, axis=-1, keepdims=True)
        weights = jnp.exp(scores - highest_score)
        totals = jnp.sum(weights, axis=-1, keepdims=True)
        probs = (weights / totals).astype(jnp.bfloat16)
        heads_block = jnp.einsum(
            "grqk,kgd->qgrd", probs, value_reduced, preferred_element_type=jnp.float32
        )
        return (heads_block.astype(jnp.bfloat16), highest_score + jnp.log(totals))

    head_outputs, log_totals = lax.map(forward_block, (q_blocks, seg_blocks, pos_blocks))
    o_low = head_outputs.reshape(tok_count, q_heads * HEAD_SIZE)
    attn_terms = jnp.dot(o_low, wo, preferred_element_type=jnp.float32)
    attn = lax.psum(attn_terms, "tensor")
    h_full = x_full + attn
    r_moe = lax.rsqrt(jnp.mean(h_full * h_full, axis=-1, keepdims=True) + epsilon)
    h_hat = h_full * r_moe
    gain_two = g_moe.astype(jnp.float32)
    a_low = (h_hat * gain_two).astype(jnp.bfloat16)
    logits = jnp.dot(a_low, wr, preferred_element_type=jnp.float32)
    chosen = jnp.take_along_axis(logits, picks, axis=1)
    gates = jax.nn.softmax(chosen, axis=-1)
    top_count = picks.shape[1]
    experts_all = wr.shape[1]
    capacity = 9 * tok_count * top_count // (8 * experts_all)
    table, destination = slot_table(picks, drop_order.reshape(-1), experts_all, capacity)
    slot_tokens = table // top_count
    local_count = expert_gate.shape[0]
    h_cols = lax.dynamic_slice_in_dim(h_full, col_start, col_width, 1)
    d_out = cotangent.astype(jnp.float32)
    d_out_cols = lax.dynamic_slice_in_dim(d_out, col_start, col_width, 1)
    send_rows = jnp.concatenate([a_low, jnp.zeros((1, width), jnp.bfloat16)], axis=0)[slot_tokens]
    expert_in = lax.all_to_all(
        send_rows.reshape(ranks_dp, -1, width), "dp", split_axis=0, concat_axis=0, tiled=True
    )
    expert_in = expert_in.reshape(ranks_dp, local_count, capacity, width)
    gate_val = jnp.einsum(
        "sjcd,jdf->sjcf", expert_in, expert_gate, preferred_element_type=jnp.float32
    )
    up_val = jnp.einsum("sjcd,jdf->sjcf", expert_in, expert_up, preferred_element_type=jnp.float32)
    sigmoid_gate = jax.nn.sigmoid(gate_val)
    silu_gate = gate_val * sigmoid_gate
    hidden_low = (silu_gate * up_val).astype(jnp.bfloat16)
    slab_count = 4
    slab_rows = ranks_dp // slab_count
    out_pieces = []
    for slab_index in range(slab_count):
        lower = slab_index * slab_rows
        partial_out = jnp.einsum(
            "sjcf,jfd->sjcd",
            hidden_low[lower : lower + slab_rows],
            expert_down,
            preferred_element_type=jnp.float32,
        )
        out_pieces.append(
            lax.psum_scatter(
                partial_out.astype(jnp.bfloat16), "tensor", scatter_dimension=3, tiled=True
            )
        )
    expert_out = jnp.concatenate(out_pieces, axis=0).reshape(
        ranks_dp, local_count * capacity, col_width
    )
    returned = lax.all_to_all(expert_out, "dp", split_axis=0, concat_axis=0, tiled=True).reshape(
        experts_all * capacity, col_width
    )
    returned = jnp.concatenate([returned, jnp.zeros((1, col_width), jnp.bfloat16)], axis=0)
    pair_outs = returned[destination].reshape(tok_count, top_count, col_width).astype(jnp.float32)
    mixed = (h_cols + jnp.sum(gates[:, :, None] * pair_outs, axis=1)).astype(jnp.bfloat16)
    d_gate_terms = jnp.sum(pair_outs * d_out_cols[:, None, :], axis=2)
    d_pairs = (
        (gates[:, :, None] * d_out_cols[:, None, :]).astype(jnp.bfloat16).reshape(-1, col_width)
    )
    d_pairs = jnp.concatenate([d_pairs, jnp.zeros((1, col_width), jnp.bfloat16)], axis=0)
    d_send = d_pairs[table].reshape(ranks_dp, local_count * capacity, col_width)
    d_arrived = lax.all_to_all(d_send, "dp", split_axis=0, concat_axis=0, tiled=True)
    d_arrived = d_arrived.reshape(ranks_dp, local_count, capacity, col_width)
    grad_expert_gate = jnp.zeros(expert_gate.shape, jnp.float32)
    grad_expert_up = jnp.zeros(expert_up.shape, jnp.float32)
    grad_expert_down = jnp.zeros(expert_down.shape, jnp.float32)
    back_pieces = []
    for slab_index in range(slab_count):
        lower = slab_index * slab_rows
        upper = lower + slab_rows
        d_expert_out = lax.all_gather(d_arrived[lower:upper], "tensor", axis=3, tiled=True)
        d_hidden = jnp.einsum(
            "sjcd,jfd->sjcf", d_expert_out, expert_down, preferred_element_type=jnp.float32
        )
        grad_expert_down = grad_expert_down + jnp.einsum(
            "sjcf,sjcd->jfd",
            hidden_low[lower:upper],
            d_expert_out,
            preferred_element_type=jnp.float32,
        )
        slab_gate = gate_val[lower:upper]
        slab_sigmoid = sigmoid_gate[lower:upper]
        d_gate_low = (
            d_hidden * up_val[lower:upper] * slab_sigmoid * (1.0 + slab_gate * (1.0 - slab_sigmoid))
        ).astype(jnp.bfloat16)
        d_up_low = (d_hidden * silu_gate[lower:upper]).astype(jnp.bfloat16)
        slab_inputs = expert_in[lower:upper]
        grad_expert_gate = grad_expert_gate + jnp.einsum(
            "sjcd,sjcf->jdf", slab_inputs, d_gate_low, preferred_element_type=jnp.float32
        )
        grad_expert_up = grad_expert_up + jnp.einsum(
            "sjcd,sjcf->jdf", slab_inputs, d_up_low, preferred_element_type=jnp.float32
        )
        d_in_terms = jnp.einsum(
            "sjcf,jdf->sjcd", d_gate_low, expert_gate, preferred_element_type=jnp.float32
        ) + jnp.einsum("sjcf,jdf->sjcd", d_up_low, expert_up, preferred_element_type=jnp.float32)
        back_pieces.append(
            lax.psum_scatter(
                d_in_terms.astype(jnp.bfloat16), "tensor", scatter_dimension=3, tiled=True
            )
        )
    d_expert_in = jnp.concatenate(back_pieces, axis=0).reshape(
        ranks_dp, local_count * capacity, col_width
    )
    d_returned = lax.all_to_all(d_expert_in, "dp", split_axis=0, concat_axis=0, tiled=True).reshape(
        experts_all * capacity, col_width
    )
    d_returned = jnp.concatenate([d_returned, jnp.zeros((1, col_width), jnp.bfloat16)], axis=0)
    d_token_cols = jnp.sum(
        d_returned[destination].reshape(tok_count, top_count, col_width).astype(jnp.float32), axis=1
    )
    d_experts_full, d_gate_parts = (
        lax.all_gather(d_token_cols.astype(jnp.bfloat16), "tensor", axis=1, tiled=True).astype(
            d_token_cols.dtype
        ),
        lax.all_gather(d_gate_terms.astype(jnp.bfloat16), "tensor", axis=1, tiled=True).astype(
            d_gate_terms.dtype
        ),
    )
    d_gates = jnp.sum(d_gate_parts.reshape(tok_count, -1, top_count), axis=1)
    d_chosen = gates * (d_gates - jnp.sum(gates * d_gates, axis=-1, keepdims=True))
    one_hot = (picks[:, :, None] == jnp.arange(experts_all, dtype=jnp.int32)[None, None, :]).astype(
        jnp.float32
    )
    d_logits = jnp.sum(d_chosen[:, :, None] * one_hot, axis=1).astype(jnp.bfloat16)
    grad_router = jnp.dot(a_low.T, d_logits, preferred_element_type=jnp.float32)
    d_norm_moe = d_experts_full + jnp.dot(d_logits, wr.T, preferred_element_type=jnp.float32)
    grad_gain_moe = jnp.sum(d_norm_moe * h_hat, axis=0)
    d_scaled = d_norm_moe * gain_two
    d_h = d_out + r_moe * (d_scaled - h_hat * jnp.mean(d_scaled * h_hat, axis=-1, keepdims=True))
    d_h_low = d_h.astype(jnp.bfloat16)
    grad_out = jnp.dot(o_low.T, d_h_low, preferred_element_type=jnp.float32)
    d_heads = jnp.dot(d_h_low, wo.T, preferred_element_type=jnp.float32).astype(jnp.bfloat16)
    d_blocks = d_heads.reshape(block_count, block_rows, kv_heads, group_repeats, HEAD_SIZE)

    def backward_block(inputs):
        q_block, d_block, log_block, seg_block, pos_block = inputs
        scores = masked_scores(q_block, seg_block, pos_block)
        probs = jnp.exp(scores - log_block)
        d_probs = jnp.einsum(
            "qgrd,kgd->grqk", d_block, value_reduced, preferred_element_type=jnp.float32
        )
        centre = jnp.sum(probs * d_probs, axis=-1, keepdims=True)
        d_scores = (probs * (d_probs - centre)).astype(jnp.bfloat16)
        d_query = (
            jnp.einsum("grqk,kgd->qgrd", d_scores, key_rotated, preferred_element_type=jnp.float32)
            * score_scale
        )
        d_key = (
            jnp.einsum("grqk,qgrd->kgd", d_scores, q_block, preferred_element_type=jnp.float32)
            * score_scale
        )
        d_value = jnp.einsum(
            "grqk,qgrd->kgd",
            probs.astype(jnp.bfloat16),
            d_block,
            preferred_element_type=jnp.float32,
        )
        return (d_query, d_key, d_value)

    d_query_all, d_key_parts, d_value_parts = lax.map(
        backward_block, (q_blocks, d_blocks, log_totals, seg_blocks, pos_blocks)
    )
    d_query_low = unrotate_pairs(
        d_query_all.reshape(tok_count, q_heads, HEAD_SIZE), cosine_values, sine_values
    )
    d_query_low = d_query_low.astype(jnp.bfloat16).reshape(tok_count, q_heads * HEAD_SIZE)
    d_key_low = unrotate_pairs(jnp.sum(d_key_parts, axis=0), cosine_values, sine_values)
    d_key_low = d_key_low.astype(jnp.bfloat16).reshape(tok_count, kv_heads * HEAD_SIZE)
    d_value_low = (
        jnp.sum(d_value_parts, axis=0).astype(jnp.bfloat16).reshape(tok_count, kv_heads * HEAD_SIZE)
    )
    grad_query = jnp.dot(x_low.T, d_query_low, preferred_element_type=jnp.float32)
    grad_key = jnp.dot(x_low.T, d_key_low, preferred_element_type=jnp.float32)
    grad_value = jnp.dot(x_low.T, d_value_low, preferred_element_type=jnp.float32)
    d_norm_terms = (
        jnp.dot(d_query_low, wq.T, preferred_element_type=jnp.float32)
        + jnp.dot(d_key_low, wk.T, preferred_element_type=jnp.float32)
        + jnp.dot(d_value_low, wv.T, preferred_element_type=jnp.float32)
    )
    d_norm_attn = lax.psum(d_norm_terms.astype(jnp.bfloat16), "tensor").astype(jnp.float32)
    grad_gain_attn = jnp.sum(d_norm_attn * x_hat, axis=0)
    d_scaled_in = d_norm_attn * gain_one
    d_input = d_h + r_attn * (
        d_scaled_in - x_hat * jnp.mean(d_scaled_in * x_hat, axis=-1, keepdims=True)
    )
    grad_tokens = lax.dynamic_slice_in_dim(d_input, col_start, col_width, 1)
    grad_query, grad_key, grad_value, grad_out, grad_router, grad_gain_attn, grad_gain_moe = (
        lax.psum_scatter(grad_query, "dp", scatter_dimension=0, tiled=True),
        lax.psum_scatter(grad_key, "dp", scatter_dimension=0, tiled=True),
        lax.psum_scatter(grad_value, "dp", scatter_dimension=0, tiled=True),
        lax.psum_scatter(grad_out, "dp", scatter_dimension=1, tiled=True),
        lax.psum_scatter(grad_router, "dp", scatter_dimension=0, tiled=True),
        lax.psum_scatter(grad_gain_attn, "dp", scatter_dimension=0, tiled=True),
        lax.psum_scatter(grad_gain_moe, "dp", scatter_dimension=0, tiled=True),
    )
    return (
        mixed,
        grad_tokens,
        grad_query,
        grad_key,
        grad_value,
        grad_out,
        grad_router,
        grad_gain_attn,
        grad_gain_moe,
        grad_expert_gate,
        grad_expert_up,
        grad_expert_down,
    )


def mm(a, b):
    return jnp.dot(a, b, preferred_element_type=F32)


def mm_nt(a, b):
    return lax.dot_general(a, b, (((1,), (1,)), ((), ())), preferred_element_type=F32)


def mm_tn(a, b):
    return lax.dot_general(a, b, (((0,), (0,)), ((), ())), preferred_element_type=F32)


def bytes_of(arrays):
    return sum(int(np.prod(a.shape)) * jnp.dtype(a.dtype).itemsize for a in arrays)


def after(v, *done):
    return lax.optimization_barrier((v, *done))[0]


def sync(*values):
    return lax.optimization_barrier(values)


def kernel_call(body, outs, ins, scratch=(), flops=0, name=None):
    smem = pl.BlockSpec(memory_space=pltpu.SMEM)
    vmem = pl.BlockSpec(memory_space=pltpu.VMEM)
    nbytes = bytes_of(list(ins[1:]) + list(outs))
    need = nbytes + bytes_of(scratch) + (16 << 20)
    return pl.pallas_call(
        body,
        out_shape=[sds(o.shape, o.dtype) for o in outs],
        in_specs=[smem] + [vmem] * (len(ins) - 1),
        out_specs=[vmem] * len(outs),
        scratch_shapes=list(scratch),
        compiler_params=pltpu.CompilerParams(vmem_limit_bytes=min(need, VMEM_LIMIT)),
        cost_estimate=pl.CostEstimate(flops=int(flops), bytes_accessed=nbytes, transcendentals=0),
        name=name,
    )(*ins)


def sds(shape, dtype):
    return jax.ShapeDtypeStruct(shape, dtype)


def slots_body(capacity, idx, picks_ref, order_ref, pos_ref):
    experts, tok = pos_ref.shape
    ids = lax.broadcasted_iota(jnp.int32, (experts, tok), 0)
    never = 1 << 28
    order = jnp.full((experts, tok), never, jnp.int32)
    for k in range(picks_ref.shape[0]):
        order = jnp.where(picks_ref[k : k + 1, :] == ids, order_ref[k : k + 1, :], order)
    limit = jnp.zeros((experts, 1), jnp.int32)
    step = 1
    while step < picks_ref.shape[0] * tok:
        step *= 2
    while step:
        tried = limit + step
        count = jnp.sum((order < tried).astype(F32), axis=1, keepdims=True)
        limit = jnp.where(count <= capacity, tried, limit)
        step //= 2
    kept = order < limit
    rows = lax.broadcasted_iota(jnp.int32, (tok, tok), 0)
    cols = lax.broadcasted_iota(jnp.int32, (tok, tok), 1)
    before = (rows < cols).astype(F32).astype(BF16)
    place = mm(kept.astype(F32).astype(BF16), before)
    pos_ref[...] = jnp.where(kept, place, jnp.where(order < never, -1.0, -2.0)).astype(BF16)


def place_body(nz, idx, *refs):
    out = refs[-1]
    rows, cols = refs[0].shape[0], out.shape[1]
    for k in range(nz):
        base = lax.rem(idx[1] - k + nz, nz) * 2
        for q in range(2):
            block = base + (idx[2] if q == 0 else 1 - idx[2])
            out[pl.ds(pl.multiple_of(block * rows, rows), rows), :] = refs[q * nz + k][:, :cols]


def place_both_body(nz, idx, *refs):
    out = refs[-1]
    rows = refs[0].shape[0]
    for k in range(nz):
        base = lax.rem(idx[1] - k + nz, nz) * 2
        for q in range(2):
            block = base + (idx[2] if q == 0 else 1 - idx[2])
            at = pl.ds(pl.multiple_of(block * rows, rows), rows)
            out[0, at, :] = refs[q * nz + k][:, refs[0].shape[1] - out.shape[2] :]
            out[1, at, :] = refs[2 * nz + k][q]


def rotate(v, cos, sin, lane_low):
    swapped = jnp.where(lane_low, pltpu.roll(v, 96, 1), pltpu.roll(v, 32, 1))
    return v * cos + swapped * sin


def low_lanes(tok):
    return lax.rem(lax.broadcasted_iota(jnp.int32, (tok, 128), 1), 64) < 32


def attend_body(nz, idx, *refs):
    blocks = refs[: 2 * nz]
    x_ref, seg_row, seg_col, cos_ref, sin_ref = refs[2 * nz : 2 * nz + 5]
    refs = refs[2 * nz + 5 :]
    (o_ref, q_ref, k_ref, v_ref, w_ref, aux_ref), heads_p, (bias_ref, qkv_ref) = refs[:6], refs[6:-2], refs[-2:]
    place_body(nz, idx, *blocks, w_ref)
    tok, width = x_ref.shape
    qd, kd = q_ref.shape[1], k_ref.shape[1]
    used = qd + 2 * kd
    aux = w_ref[:, used:].astype(F32).T
    aux_ref[...] = aux.astype(BF16)
    x = x_ref[...].astype(F32)
    r1 = lax.rsqrt(jnp.mean(x * x, axis=1, keepdims=True) + epsilon)
    x_low = (x * r1 * aux[64:65, :]).astype(BF16)
    qkv_ref[...] = mm(x_low, w_ref[:, :used])
    lanes = low_lanes(tok)
    cos, sin = cos_ref[...], sin_ref[...]
    for b in range(qd // 128):
        rot = rotate(qkv_ref[:, b * 128 : b * 128 + 128], cos, sin, lanes).astype(BF16)
        q_ref[:, b * 128 : b * 128 + 128] = (rot.astype(F32) * HEAD_SIZE**-0.5).astype(BF16)
    for b in range(kd // 128):
        rot = rotate(qkv_ref[:, qd + b * 128 : qd + b * 128 + 128], cos, sin, lanes)
        k_ref[:, b * 128 : b * 128 + 128] = rot.astype(BF16)
    v_ref[...] = qkv_ref[:, qd + kd :].astype(BF16)
    rows = lax.broadcasted_iota(jnp.int32, (tok, tok), 0)
    cols = lax.broadcasted_iota(jnp.int32, (tok, tok), 1)
    allowed = (seg_col[...] == seg_row[...]) & (cols <= rows)
    bias_ref[...] = jnp.where(allowed, 0.0, negative_big)
    heads, groups = qd // HEAD_SIZE, kd // HEAD_SIZE
    for h in range(heads):
        g = h // (heads // groups)
        a, b = h * HEAD_SIZE, g * HEAD_SIZE
        s = mm_nt(q_ref[:, a : a + HEAD_SIZE], k_ref[:, b : b + HEAD_SIZE]) + bias_ref[...]
        e = jnp.exp(s - jnp.max(s, axis=1, keepdims=True))
        p = (e / jnp.sum(e, axis=1, keepdims=True)).astype(BF16)
        heads_p[h][...] = p
        o_ref[:, a : a + HEAD_SIZE] = mm(p, v_ref[:, b : b + HEAD_SIZE]).astype(BF16)


def column_places(idx, width):
    x, c = idx[3], idx[4]
    part = width // 4

    def at(b):
        return pl.ds(pl.multiple_of(b * part, 128), part)

    return [at(2 * x + c), at(2 * (1 - x) + c)], [at(2 * x + 1 - c), at(2 * (1 - x) + 1 - c)]


def out_body(idx, x_ref, o0, o1, o23, w01, w23, aux_ref, h_ref, low_ref, ring_ref):
    tok, width = x_ref.shape
    attn = mm_nt(o0[...], w01[0]) + mm_nt(o1[...], w01[1])
    attn = attn + (mm_nt(o23[0], w23[0]) + mm_nt(o23[1], w23[1]))
    h = x_ref[...].astype(F32) + attn
    h_ref[...] = h
    r2 = lax.rsqrt(jnp.mean(h * h, axis=1, keepdims=True) + epsilon)
    low_ref[...] = (h * r2 * aux_ref[64:66, :].astype(F32)[1:2, :]).astype(BF16)
    part = width // 4
    for m, at in enumerate(column_places(idx, width)[0]):
        ring_ref[:, m * part : m * part + part] = low_ref[:, at]


def masked_gates(logits, pos):
    picked = pos > -1.5
    shown = jnp.where(picked, logits, negative_big)
    e = jnp.where(picked, jnp.exp(shown - jnp.max(shown, axis=0, keepdims=True)), 0.0)
    return e / jnp.sum(e, axis=0, keepdims=True)


def split16(v):
    high = v.astype(BF16)
    return high, (v - high.astype(F32)).astype(BF16)


def experts_body(
    local, idx, aux_ref, sel_ref, selt_ref, slot_ref, slott_ref, *refs
):
    rows_hbm, d_hbm, (gu_hbm, down_hbm), refs = refs[:4], refs[4:8], refs[8:10], refs[10:]
    dx_hbm, y_hbm, (xe_hbm, d0_hbm, dgu_hbm, hd_hbm) = refs[:2], refs[2:4], refs[4:8]
    am_s, an_s, dm_s, dn_s, gu_s, down_s = refs[8:14]
    dx_out, y_out, (xe_s, d0_s, dgu_s, hd_s) = refs[14:16], refs[16:18], refs[18:22]
    pos_s, gate_s, y_s, dx_s, dgr_s, oh_s, oht_s, in_sem, w_sem, out_sem = refs[22:]
    tok, width = am_s.shape[1], xe_s.shape[3]
    half = pos_s.shape[0] // 2
    x, c = idx[3], idx[4]
    part = width // 4
    sides = column_places(idx, width)
    hidden = down_s.shape[1]
    both, slots = 2 * PAD, local * PAD

    def arriving(q):
        pairs = [(rows_hbm[q], am_s.at[q]), (rows_hbm[2 + q], an_s.at[q])]
        for i, d_s in enumerate((dm_s, dn_s)):
            for m in range(2):
                pairs.append((d_hbm[2 * i + m].at[q], d_s.at[q, :, m * part : m * part + part]))
        return [pltpu.make_async_copy(h, v, in_sem.at[q, i]) for i, (h, v) in enumerate(pairs)]

    weights = [pltpu.make_async_copy(gu_hbm, gu_s, w_sem.at[0]), pltpu.make_async_copy(down_hbm, down_s, w_sem.at[1])]
    for cp in arriving(0):
        cp.start()
    for cp in arriving(1):
        cp.start()
    for cp in weights:
        cp.start()
    leaving = []

    def leave(src, dst):
        cp = pltpu.make_async_copy(src, dst, out_sem.at[len(leaving)])
        cp.start()
        leaving.append(cp)

    sel, selt = sel_ref[...], selt_ref[...]
    for q in range(2):
        for cp in arriving(q):
            cp.wait()
        for d_s, core in ((dm_s, c), (dn_s, 1 - c)):
            for m, chip in enumerate((x, 1 - x)):
                at = pl.ds(pl.multiple_of((2 * chip + core) * 128, 128), 128)
                pos_s[:, at] = d_s[q, tok:, m * part : m * part + 128]
        pos = pos_s[...]
        logits = jnp.zeros(pos.shape, F32)
        for rows, places in zip((am_s, an_s), sides):
            for m, at in enumerate(places):
                logits = logits + mm_nt(aux_ref[: pos.shape[0], at], rows[q, :, m * part : m * part + part])
        gates = masked_gates(logits, pos.astype(F32))
        hot = (mm(sel, pos) == slot_ref[...]).astype(F32).astype(BF16)
        oh_s[q] = hot
        oht_s[q] = (mm_tn(pos, selt) == slott_ref[...]).astype(F32).astype(BF16)
        high, low = split16(gates)
        spread = (mm_nt(hot, high) + mm_nt(hot, low)) * sel.astype(F32)
        gate_s[:, q] = jnp.sum(spread, axis=1, keepdims=True).reshape(local, PAD, 1)
        for rows, outs in (((am_s, an_s), xe_s), ((dm_s, dn_s), d0_s)):
            for side, places in enumerate(sides):
                got = mm(hot, rows[side][q, :tok, :]).astype(BF16)
                for m, at in enumerate(places):
                    outs[:, q, :, at] = got[:, m * part : m * part + part].reshape(local, PAD, part)
    leave(xe_s, xe_hbm)
    leave(d0_s, d0_hbm)
    for cp in weights:
        cp.wait()
    for j in range(local):
        gu = mm(xe_s[j].reshape(both, width), gu_s[j])
        t = mm_nt(d0_s[j].reshape(both, width), down_s[j])
        gate = gate_s[j].reshape(both, 1)
        g, u = gu[:, :hidden], gu[:, hidden:]
        sg = jax.nn.sigmoid(g)
        silu = g * sg
        hd = (silu * u).astype(BF16)
        dhd = gate * t
        dg = (dhd * u * sg * (1.0 + g * (1.0 - sg))).astype(BF16)
        du = (dhd * silu).astype(BF16)
        dgate = jnp.sum(hd.astype(F32) * t, axis=1, keepdims=True)
        dgr_s[j] = jnp.broadcast_to(dgate, (both, dgr_s.shape[3])).reshape(2, PAD, dgr_s.shape[3])
        hd_s[j] = (hd.astype(F32) * gate).astype(BF16).reshape(2, PAD, hidden)
        dgu = jnp.concatenate([dg, du], axis=1)
        dgu_s[j] = dgu.reshape(2, PAD, 2 * hidden)
        dx_s[j] = mm_nt(dgu, gu_s[j]).astype(BF16).reshape(2, PAD, width)
        y = mm(hd, down_s[j])
        y_s[j] = (y.astype(BF16).astype(F32) * gate).astype(BF16).reshape(2, PAD, width)
    leave(hd_s, hd_hbm)
    leave(dgu_s, dgu_hbm)
    for q in range(2):
        hot, hott = oh_s[q], oht_s[q]

        def scatter(rows_s, outs):
            for out, places in zip(outs, sides):
                rows = [rows_s[:, q, :, at].reshape(slots, part) for at in places]
                out[q, :tok, :] = mm(hott, jnp.concatenate(rows, axis=1)).astype(BF16)

        scatter(dx_s, dx_out)
        spread = (dgr_s[:, q].reshape(slots, -1) * sel.astype(F32)).astype(BF16)
        pos_s[...] = mm_tn(spread, hot).astype(BF16)
        for out, at in zip(dx_out, (c, 1 - c)):
            out[q, tok:, :tok] = pos_s[pl.ds(pl.multiple_of(at * half, half), half), :]
            out[q, tok:, tok:] = jnp.zeros((half, out.shape[2] - tok), BF16)
        for v, h in zip(dx_out, dx_hbm):
            leave(v.at[q], h.at[q])
        scatter(y_s, y_out)
        for v, h in zip(y_out, y_hbm):
            leave(v.at[q], h.at[q])
    for cp in leaving:
        cp.wait()


def experts_call(idx, a, d, gu, down, aux_t, sel, slot_col, slot_row):
    local, width, hidden2 = gu.shape
    hidden = hidden2 // 2
    experts = sel.shape[1]
    tok = a[0].shape[0]
    rows = tok + experts // 2
    slots = local * PAD
    big = (local, 2, PAD, width)
    outs = [sds((2, n, width // 2), BF16) for n in (rows, rows, tok, tok)]
    outs += [sds(big, BF16), sds(big, BF16), sds((local, 2, PAD, hidden2), BF16), sds((local, 2, PAD, hidden), BF16)]
    kept = [idx, aux_t, sel, sel.T, slot_col, slot_row]
    scratch = [pltpu.VMEM((2, n, width // 2), BF16) for n in (tok, tok, tok + experts, tok + experts)]
    scratch += [pltpu.VMEM(v.shape, v.dtype) for v in [gu, down] + outs]
    scratch += [
        pltpu.VMEM((experts, tok), BF16), pltpu.VMEM((local, 2, PAD, 1), F32), pltpu.VMEM(big, BF16), pltpu.VMEM(big, BF16),
        pltpu.VMEM((local, 2, PAD, experts), F32), pltpu.VMEM((2, slots, tok), BF16), pltpu.VMEM((2, tok, slots), BF16),
    ]
    scratch += [pltpu.SemaphoreType.DMA((2, 6)), pltpu.SemaphoreType.DMA((2,)), pltpu.SemaphoreType.DMA((20,))]
    moved = [*a, *d, gu, down]
    smem = pl.BlockSpec(memory_space=pltpu.SMEM)
    vmem = pl.BlockSpec(memory_space=pltpu.VMEM)
    hbm = pl.BlockSpec(memory_space=pl.ANY)
    return pl.pallas_call(
        functools.partial(experts_body, local),
        out_shape=outs,
        in_specs=[smem] + [vmem] * 5 + [hbm] * len(moved),
        out_specs=[hbm] * len(outs),
        scratch_shapes=scratch,
        compiler_params=pltpu.CompilerParams(vmem_limit_bytes=VMEM_LIMIT),
        cost_estimate=pl.CostEstimate(
            flops=16 * slots * tok * width + 36 * slots * width * hidden,
            bytes_accessed=bytes_of(moved + outs),
            transcendentals=0,
        ),
        name="experts",
    )(*kept, *moved)


def in_ring_order(nz, idx, blocks_s, outs):
    for k in range(nz):
        base = lax.rem(idx[1] - k + nz, nz) * 2
        outs[k][...] = blocks_s[base + idx[2]]
        outs[nz + k][...] = blocks_s[base + 1 - idx[2]]


def hidden_back_body(nz, idx, fm_ref, fn_ref, h_ref, low_ref, aux_ref, pos_ref, dout_ref, o_ref, w_ref,
                     dh_ref, do_ref, *refs):
    outs, (full_s, dg_s, rs_s) = refs[:-3], refs[-3:]
    tok, width = h_ref.shape
    c, experts = idx[4], pos_ref.shape[0]
    half = experts // 2
    part = width // 4
    for ref, places in zip((fm_ref, fn_ref), column_places(idx, width)):
        for m, at in enumerate(places):
            full_s[:, at] = ref[:tok, m * part : m * part + part].astype(F32)
    for ref, at in ((fm_ref, c), (fn_ref, 1 - c)):
        dg_s[pl.ds(pl.multiple_of(at * half, half), half), :] = ref[tok:, :tok].astype(F32)
    low = low_ref[...]
    router = aux_ref[:experts, :]
    gates = masked_gates(mm_nt(router, low), pos_ref[...].astype(F32))
    dgates = dg_s[...]
    dlogits = (gates * (dgates - jnp.sum(gates * dgates, axis=0, keepdims=True))).astype(BF16)
    h = h_ref[...]
    r2 = lax.rsqrt(jnp.mean(h * h, axis=1, keepdims=True) + epsilon)
    ah = h * r2
    da = full_s[...] + mm_tn(dlogits, router)
    gain_grad = jnp.sum(da * ah, axis=0, keepdims=True)
    scaled = da * aux_ref[64:66, :].astype(F32)[1:2, :]
    dh = dout_ref[...].astype(F32) + r2 * (scaled - ah * jnp.mean(scaled * ah, axis=1, keepdims=True))
    full_s[...] = dh
    cols = dh_ref.shape[1]
    t = idx[3] * 2 + c
    dh_ref[...] = full_s[:, pl.ds(pl.multiple_of(t * cols, 128), cols)]
    dhb = dh.astype(BF16)
    do_ref[...] = mm(dhb, w_ref[0]).astype(BF16)
    turned = mm_tn(dhb, o_ref[...]).astype(BF16)
    side = jnp.concatenate([mm(dlogits, low), gain_grad, jnp.zeros((63, width), F32)], axis=0)
    side = side.T.astype(BF16)
    rows = rs_s.shape[1]
    for i in range(2 * nz):
        rs_s[i, :, :cols] = turned[i * rows : i * rows + rows]
        rs_s[i, :, cols:] = side[i * rows : i * rows + rows]
    in_ring_order(nz, idx, rs_s, outs)


def attend_back_body(nz, idx, do_ref, v_ref, k_ref, q_ref, cos_ref, sin_ref, x_ref, aux_ref, w_ref, *refs):
    heads_p, refs = refs[: q_ref.shape[1] // HEAD_SIZE], refs[q_ref.shape[1] // HEAD_SIZE :]
    dm_ref, dn_ref, outs, (dq_s, dqkv_s, dxn_s, rs_ref) = refs[0], refs[1], refs[2:-4], refs[-4:]
    tok, width = x_ref.shape
    qd, kd = q_ref.shape[1], k_ref.shape[1]
    heads, groups = qd // HEAD_SIZE, kd // HEAD_SIZE
    scale = HEAD_SIZE**-0.5
    each = heads // groups
    for g in range(groups):
        b = g * HEAD_SIZE
        kg, vg = k_ref[:, b : b + HEAD_SIZE], v_ref[:, b : b + HEAD_SIZE]
        dk = jnp.zeros((tok, HEAD_SIZE), F32)
        dv = jnp.zeros((tok, HEAD_SIZE), F32)
        for h in range(g * each, (g + 1) * each):
            a = h * HEAD_SIZE
            doh = do_ref[:, a : a + HEAD_SIZE]
            p = heads_p[h][...].astype(F32)
            dp = mm_nt(doh, vg)
            ds = (p * (dp - jnp.sum(p * dp, axis=1, keepdims=True))).astype(BF16)
            dq_s[:, a : a + HEAD_SIZE] = mm(ds, kg) * scale
            dk = dk + mm_tn(ds, q_ref[:, a : a + HEAD_SIZE])
            dv = dv + mm_tn(heads_p[h][...], doh)
        dq_s[:, qd + b : qd + b + HEAD_SIZE] = dk
        dqkv_s[:, qd + kd + b : qd + kd + b + HEAD_SIZE] = dv.astype(BF16)
    lanes = low_lanes(tok)
    cos, sin = cos_ref[...], -sin_ref[...]
    for b in range((qd + kd) // 128):
        at = slice(b * 128, b * 128 + 128)
        dqkv_s[:, at] = rotate(dq_s[:, at], cos, sin, lanes).astype(BF16)
    used = qd + 2 * kd
    x = x_ref[...].astype(F32)
    r1 = lax.rsqrt(jnp.mean(x * x, axis=1, keepdims=True) + epsilon)
    xh = x * r1
    gain = aux_ref[64:65, :].astype(F32)
    x_low = (xh * gain).astype(BF16)
    dqkv = dqkv_s[...]
    rows = width // rs_ref.shape[0]
    grads = mm_tn(x_low, dqkv).astype(BF16)
    dxn = mm_nt(dqkv, w_ref[:, :used])
    gain_high, gain_low = split16(jnp.sum(dxn * xh, axis=0, keepdims=True))
    pads = jnp.zeros((14, rows), BF16)
    for i in range(rs_ref.shape[0]):
        rs_ref[i, :rows, :] = grads[i * rows : i * rows + rows, :]
        at = slice(i * rows, i * rows + rows)
        tail = jnp.concatenate([gain_high[:, at].astype(F32), gain_low[:, at].astype(F32), pads.astype(F32)], axis=0)
        rs_ref[i, rows:, :] = jnp.zeros((16, used), BF16)
        rs_ref[i, rows:, :rows] = tail.astype(BF16)
    in_ring_order(nz, idx, rs_ref, outs)
    total = jnp.sum(dxn * xh * gain, axis=1, keepdims=True)
    high, low = split16(total)
    lane = lax.broadcasted_iota(jnp.int32, (tok, 128), 1)
    side = jnp.where(lane == 0, high.astype(F32), jnp.where(lane == 1, low.astype(F32), 0.0)).astype(BF16)
    cols = width // 4
    for i in range(4):
        dxn_s[i] = dxn[:, i * cols : i * cols + cols].astype(BF16)
    ix, c = idx[3], idx[4]
    for ref, core in ((dm_ref, c), (dn_ref, 1 - c)):
        ref[:, :cols] = dxn_s[2 * ix + core]
        ref[:, cols : 2 * cols] = dxn_s[2 * (1 - ix) + core]
        ref[:, 2 * cols :] = side


def early_end_body(idx, kept, side, ring, out_ref, router_ref, gain_ref):
    total = kept[...].astype(F32) + side[...].astype(F32) + ring[...].astype(F32)
    cols, experts = out_ref.shape[0], router_ref.shape[1]
    out_ref[...] = total[:, :cols].T
    router_ref[...] = total[:, cols : cols + experts]
    gain_ref[...] = total[:, cols:].T[experts : experts + 8]


def late_end_body(idx, kept, side, ring, query_ref, key_ref, value_ref, gain_ref):
    total = kept[...].astype(F32) + side[...].astype(F32) + ring[...].astype(F32)
    rows, qd = query_ref.shape
    kd = key_ref.shape[1]
    gain_ref[...] = total[rows : rows + 8, : gain_ref.shape[1]]
    query_ref[...] = total[:rows, :qd]
    key_ref[...] = total[:rows, qd : qd + kd]
    value_ref[...] = total[:rows, qd + kd :]


def expert_grads_body(count, *refs):
    xe, d0, dgu, hd = (refs[i * count : i * count + count] for i in range(4))
    gate_ref, up_ref, down_ref = refs[4 * count :]
    hidden = gate_ref.shape[2]

    def join(group, at=slice(None)):
        return jnp.concatenate([r[0, :, :, at].reshape(2 * PAD, -1) for r in group], axis=0)

    d_gu, hd_all = join(dgu), join(hd)
    for b in range(gate_ref.shape[1] // BLK):
        at = slice(b * BLK, b * BLK + BLK)
        both = mm_tn(join(xe, at), d_gu)
        gate_ref[0, at, :] = both[:, :hidden]
        up_ref[0, at, :] = both[:, hidden:]
        down_ref[0, :, at] = mm_tn(hd_all, join(d0, at))


class ExpertGrads:
    def __init__(self, xe, d0, dgu, hd, pieces=4):
        self.ins, self.outs = (*xe, *d0, *dgu, *hd), {}
        self.count, self.pieces = len(xe), pieces
        self.local, _, _, self.width = xe[0].shape
        self.hidden = hd[0].shape[3]

    def run(self, piece):
        local, width, hidden, count = self.local, self.width, self.hidden, self.count
        each = local // self.pieces
        first = each * piece

        def whole(n):
            return pl.BlockSpec((1, 2, PAD, n), lambda e: (e + first, 0, 0, 0))

        slots = count * 2 * PAD * each
        earlier = list(self.outs[0]) if self.outs else []
        body = functools.partial(expert_grads_body, count)
        n = len(self.ins)

        def with_earlier(*refs):
            body(*refs[:n], *refs[n + len(earlier) :])

        self.outs[0] = pl.pallas_call(
            with_earlier,
            grid=(each,),
            out_shape=[sds((local, width, hidden), F32), sds((local, width, hidden), F32), sds((local, hidden, width), F32)],
            in_specs=[whole(width)] * (2 * count) + [whole(2 * hidden)] * count + [whole(hidden)] * count
            + [pl.BlockSpec(memory_space=pl.ANY)] * len(earlier),
            out_specs=[pl.BlockSpec((1, width, hidden), lambda e: (e + first, 0, 0))] * 2
            + [pl.BlockSpec((1, hidden, width), lambda e: (e + first, 0, 0))],
            input_output_aliases={n + i: i for i in range(len(earlier))},
            compiler_params=pltpu.CompilerParams(vmem_limit_bytes=32 << 20),
            cost_estimate=pl.CostEstimate(
                flops=6 * slots * width * hidden, bytes_accessed=slots * width * 4 + 12 * each * width * hidden, transcendentals=0
            ),
            name="expert_grads",
        )(*self.ins, *earlier)


def add16(a, b):
    return (a.astype(F32) + b.astype(F32)).astype(BF16)


def on_device_gathered(
    tokens,
    document_numbers,
    picks,
    drop_order,
    w_query,
    key_matrix,
    value_matrix,
    w_out,
    w_router,
    gain_attn,
    gain_moe,
    expert_gate,
    expert_up,
    expert_down,
    cotangent,
):
    n_dp = lax.axis_size("dp")
    nz = n_dp // 2
    r, t = lax.axis_index("dp"), lax.axis_index("tensor")
    z, y, x, c = r // 2, r % 2, t // 2, t % 2
    idx = jnp.stack([r, z, y, x, c]).astype(jnp.int32)

    def shift_z(v):
        return lax.ppermute(v, "dp", [(i, ((i // 2 + 1) % nz) * 2 + i % 2) for i in range(n_dp)])

    def swap_y(v):
        return lax.ppermute(v, "dp", [(i, i ^ 1) for i in range(n_dp)])

    def swap_x(v):
        return lax.ppermute(v, "tensor", [(i, i ^ 2) for i in range(4)])

    def swap_c(v):
        return lax.ppermute(v, "tensor", [(i, i ^ 1) for i in range(4)])

    tok, width = tokens.shape
    rows = w_query.shape[0]
    qd, kd = w_query.shape[1], key_matrix.shape[1]
    used = qd + 2 * kd
    experts = w_router.shape[1]
    local, _, hidden = expert_gate.shape
    capacity = 9 * tok * picks.shape[1] // (8 * experts)
    cols = width // 4

    aux = jnp.concatenate(
        [w_router, gain_attn[:, None], gain_moe[:, None], jnp.zeros((rows, 128 - experts - 2), BF16)], axis=1
    )
    wz = [jnp.concatenate([w_query, key_matrix, value_matrix, aux, w_out.T], axis=1)]
    wy, wx = [], []

    def out_pair(k):
        return swap_x(jnp.stack([wz[k][:, used + 128 :], wy[k][:, used + 128 :]]))

    pos = kernel_call(
        functools.partial(slots_body, capacity),
        [sds((experts, tok), BF16)],
        [idx, picks.T, drop_order.reshape(tok, -1).T],
        name="slots",
    )[0]
    part = tok // 4
    pos_own = lax.dynamic_slice_in_dim(pos, t * part, part, 1)
    d_own = jnp.concatenate(
        [
            lax.dynamic_slice_in_dim(cotangent, t * cols, cols, 1),
            jnp.concatenate([pos_own, jnp.zeros((experts, cols - part), BF16)], axis=1),
        ],
        axis=0,
    )

    class Rows:
        def __init__(self, own):
            self.z, self.y, self.cz, self.cy = {0: own}, {}, {}, {}

        def ring(self, k):
            self.z[k] = shift_z(self.z[k - 1])

        def side(self, k):
            self.y[k] = swap_y(self.z[k])

        def core_ring(self, k):
            self.cz[k] = swap_c(self.z[k])

        def core_side(self, k):
            self.cy[k] = swap_c(self.y[k])

        def all(self, k):
            return [v[k] for v in (self.z, self.y, self.cz, self.cy)]

    class Split(Rows):
        def __init__(self, own):
            super().__init__(own)
            self.s, self.x, self.cs, self.cx = {}, {}, {}, {}

        def chip(self, k):
            self.s[k] = jnp.stack([self.z[k], self.y[k]])
            self.x[k] = swap_x(self.s[k])

        def core_own(self, k):
            self.cs[k] = swap_c(self.s[k])

        def core(self, k):
            self.cx[k] = swap_c(self.x[k])

        def all(self, k):
            return [v[k] for v in (self.s, self.x, self.cs, self.cx)]

    def meet(*items):
        places = [(getattr(o, n), k) for o, names, k in items for n in names.split()]
        values = sync(*[d[k] for d, k in places])
        for (d, k), v in zip(places, values):
            d[k] = v

    last = nz - 1
    for k in range(last):
        wz.append(shift_z(wz[k]))
        wy.append(swap_y(wz[k]))
        if k:
            wx.append(out_pair(k - 1))
        if k == 0:
            wz[1], wy[0], d_own = sync(wz[1], wy[0], d_own)
        else:
            wz[k + 1], wy[k] = sync(wz[k + 1], wy[k])
    wx.append(out_pair(last - 1))
    wy.append(swap_y(wz[last]))
    d = Split(after(d_own, wz[last]))
    d.ring(1)
    gu = jnp.concatenate([expert_gate, expert_up], axis=2)
    wy[last], wx[0], gu = sync(wy[last], wx[0], gu)
    wx.append(out_pair(last))

    positions = np.arange(tok, dtype=np.float32)
    inverse = rope_base ** (-(2.0 * np.arange(HEAD_SIZE // 2, dtype=np.float32)) / HEAD_SIZE)
    angles = positions[:, None] * inverse.astype(np.float32)[None, :]
    cos = jnp.asarray(np.tile(np.cos(angles), (1, 4)).astype(np.float32))
    sin = np.sin(angles)
    sin = jnp.asarray(np.tile(np.concatenate([-sin, sin], axis=1), (1, 2)).astype(np.float32))
    heads = qd // HEAD_SIZE
    seg_row = document_numbers.reshape(1, tok)
    o, q, k_rot, v, w_all, aux_t, *heads_p = kernel_call(
        functools.partial(attend_body, nz),
        [sds((tok, qd), BF16), sds((tok, qd), BF16), sds((tok, kd), BF16), sds((tok, kd), BF16),
         sds((width, used + 128), BF16), sds((128, width), BF16)] + [sds((tok, tok), BF16)] * heads,
        [idx, *wz, *wy, tokens, seg_row, seg_row.T, cos, sin],
        scratch=[pltpu.VMEM((tok, tok), F32), pltpu.VMEM((tok, used), F32)],
        flops=4e9,
        name="attend",
    )
    o, d.z[1], d.z[0], *wx[1:] = sync(o, d.z[1], d.z[0], *wx[1:])
    o_x = swap_x(o)
    d.ring(2)
    d.side(0)
    wo = kernel_call(
        functools.partial(place_both_body, nz), [sds((2, width, qd), BF16)], [idx, *wz, *wy, *wx], name="place"
    )[0]
    wo_c = swap_c(wo)
    slot_ids = np.arange(local * PAD)
    sel = (r * local + slot_ids[:, None] // PAD == jnp.arange(experts)[None, :]).astype(BF16)
    slot_col = jnp.asarray((slot_ids % PAD).astype(np.float32)[:, None])
    slot_row = jnp.asarray((slot_ids % PAD).astype(np.float32)[None, :])
    o_x, wo_c, sel, d.z[2], d.y[0] = sync(o_x, wo_c, sel, d.z[2], d.y[0])
    d.ring(3)
    d.side(1)
    d.chip(0)
    d.core_own(0)
    o_c = swap_c(jnp.stack([o, o_x]))
    h, low, ring0 = kernel_call(
        out_body,
        [sds((tok, width), F32), sds((tok, width), BF16), sds((tok, 2 * cols), BF16)],
        [idx, tokens, o, o_x, o_c, wo, wo_c, aux_t],
        flops=5e9,
        name="out",
    )
    ring0, d.z[3], d.y[1], d.x[0], d.cs[0] = sync(ring0, d.z[3], d.y[1], d.x[0], d.cs[0])
    a = Rows(ring0)
    done = {}

    def run_experts(k):
        done[k] = experts_call(idx, a.all(k), d.all(k), gu, expert_down, aux_t, sel, slot_col, slot_row)

    class Sums:
        def __init__(self, at):
            self.at, self.c, self.s, self.y, self.total = at, {}, {}, {}, {}

        def core(self, k):
            self.c[k] = swap_c(done[k][self.at + 1])

        def side(self, k):
            m, n = done[k][self.at], self.c[k]
            self.s[k] = add16(m[0], n[0])
            self.y[k] = swap_y(add16(m[1], n[1]))

        def ring(self, k):
            total = self.s[k].astype(F32) + self.y[k].astype(F32)
            if self.total:
                total = total + self.total[0].astype(F32)
            total = total.astype(BF16)
            self.total[0] = total if k == 0 else shift_z(total)

    class SplitSums(Sums):
        def __init__(self, at):
            super().__init__(at)
            self.x = {}

        def chip(self, k):
            self.x[k] = swap_x(add16(done[k][self.at][:, :, cols:], self.c[k][:, :, cols:]))

        def side(self, k):
            m, n, far = done[k][self.at], self.c[k], self.x[k]
            own = [(m[q, :, :cols].astype(F32) + n[q, :, :cols].astype(F32) + far[q].astype(F32)).astype(BF16) for q in (0, 1)]
            self.s[k] = own[0]
            self.y[k] = swap_y(own[1])

    sx, sy = Sums(0), SplitSums(2)

    class Ran:
        out = done

    ran = Ran()
    a.ring(1)
    a.side(0)
    a.core_ring(0)
    d.chip(1)
    d.core_own(1)
    d.core(0)
    meet((a, "z", 1), (a, "y cz", 0), (d, "x cs", 1), (d, "cx", 0))
    a.ring(2)
    a.side(1)
    a.core_side(0)
    a.core_ring(1)
    d.side(2)
    d.core(1)
    run_experts(0)
    meet((a, "z", 2), (a, "y cz", 1), (ran, "out", 0), (d, "y", 2), (d, "cx", 1))
    a.ring(3)
    a.side(2)
    a.core_side(1)
    a.core_ring(2)
    d.side(3)
    d.chip(2)
    d.core_own(2)
    run_experts(1)
    meet((a, "z", 3), (a, "y cz", 2), (ran, "out", 1), (d, "y", 3), (d, "x cs", 2))
    a.side(3)
    a.core_side(2)
    d.core(2)
    sx.core(1)
    meet((a, "cy", 2), (sx, "c", 1), (d, "cx", 2), (ran, "out", 1))
    a.core_ring(3)
    d.chip(3)
    d.core_own(3)
    sx.side(1)
    sy.core(1)
    run_experts(2)
    meet((a, "y cz", 3), (sx, "s y", 1), (sy, "c", 1), (ran, "out", 2), (d, "x cs", 3))
    sx.ring(1)
    a.core_side(3)
    d.core(3)
    sx.core(2)
    meet((a, "cy", 3), (sx, "c", 2), (d, "cx", 3), (ran, "out", 1), (ran, "out", 2), (sy, "c", 1))
    sx.side(2)
    sy.chip(1)
    sy.core(2)
    run_experts(3)
    meet((sx, "s y", 2), (sx, "total", 0), (sy, "x", 1), (sy, "c", 2), (ran, "out", 3))
    grads = ExpertGrads(*[[done[k][i] for k in range(nz)] for i in range(4, 8)])
    sx.ring(2)
    sx.core(3)
    meet((sx, "c", 3), (ran, "out", 3), (sy, "c", 2))
    sx.side(3)
    sx.core(0)
    sy.chip(2)
    sy.core(3)
    grads.run(0)
    grads.run(1)
    meet((sx, "s y", 3), (sx, "total", 0), (sx, "c", 0), (sy, "x", 2), (sy, "c", 3), (grads, "outs", 0))
    sx.ring(3)
    sx.side(0)
    sy.chip(3)
    sy.core(0)
    grads.run(2)
    meet((sx, "s y", 0), (sx, "total", 0), (sy, "x", 3), (sy, "c", 0), (grads, "outs", 0))
    sx.ring(0)
    far = swap_x(sx.total[0])
    sy.side(1)
    sy.side(2)
    grads.run(3)
    sx.total[0], far, *rest = sync(sx.total[0], far, sy.s[1], sy.y[1], sy.s[2], sy.y[2], sy.x[3], sy.c[0], grads.outs[0])
    sy.s[1], sy.y[1], sy.s[2], sy.y[2], sy.x[3], sy.c[0], grads.outs[0] = rest
    mine = sx.total[0].astype(F32) + jnp.concatenate([far[:, cols:], far[:, :cols]], axis=1).astype(F32)
    head, tail = mine[:tok], sx.total[0][tok:].astype(F32) + far[tok:].astype(F32)
    fm = jnp.concatenate([head.astype(BF16), tail.astype(BF16)], axis=0)
    fn = swap_c(fm)
    fm, fn, sy.y[1], sy.x[3], sy.c[0] = sync(fm, fn, sy.y[1], sy.x[3], sy.c[0])
    sy.side(3)
    sy.ring(1)
    sy.chip(0)
    d_h, d_o, *early = kernel_call(
        functools.partial(hidden_back_body, nz),
        [sds((tok, cols), F32), sds((tok, qd), BF16)] + [sds((rows, qd + 128), BF16)] * n_dp,
        [idx, fm, fn, h, low, aux_t, pos, cotangent, o, wo],
        scratch=[pltpu.VMEM((tok, width), F32), pltpu.VMEM((experts, tok), F32), pltpu.VMEM((n_dp, rows, qd + 128), BF16)],
        flops=3e9,
        name="hidden_back",
    )
    d_o, early, sy.total[0], sy.s[3], sy.y[3], sy.x[0] = sync(d_o, early, sy.total[0], sy.s[3], sy.y[3], sy.x[0])

    class Weights:
        def __init__(self, v):
            self.kept, self.sent, self.y, self.total = v[:nz], v[nz:], {}, {}

        def side(self, k):
            self.y[k] = swap_y(self.sent[k])

        def ring(self, k):
            total = self.kept[k].astype(F32) + self.y[k].astype(F32)
            if self.total:
                total = total + self.total[0].astype(F32)
            self.total[0] = shift_z(total.astype(BF16))

        def last(self):
            return self.kept[0], self.y[0], self.total[0]

    early = Weights(early)
    early.side(1)
    sy.side(0)
    sy.ring(2)
    late, dxm, dxn = [], None, None
    dxm, dxn, *late = kernel_call(
        functools.partial(attend_back_body, nz),
        [sds((tok, 2 * cols + 128), BF16), sds((tok, 2 * cols + 128), BF16)] + [sds((rows + 16, used), BF16)] * n_dp,
        [idx, d_o, v, k_rot, q, cos, sin, tokens, aux_t, w_all, *heads_p],
        scratch=[
            pltpu.VMEM((tok, used), F32), pltpu.VMEM((tok, used), BF16), pltpu.VMEM((4, tok, cols), BF16),
            pltpu.VMEM((n_dp, rows + 16, used), BF16),
        ],
        flops=5e9,
        name="attend_back",
    )
    late, dxm, dxn, early.y[1], sy.y[0], sy.s[0], sy.total[0] = sync(
        late, dxm, dxn, early.y[1], sy.y[0], sy.s[0], sy.total[0]
    )
    late = Weights(late)
    late.side(1)
    early.side(2)
    early.ring(1)
    sy.ring(3)
    got = swap_c(dxn)
    late.y[1], early.y[2], early.total[0], sy.total[0], got = sync(
        late.y[1], early.y[2], early.total[0], sy.total[0], got
    )
    late.side(2)
    late.ring(1)
    early.side(3)
    early.ring(2)
    ours = dxm.astype(F32) + got.astype(F32)
    mean_part = ours[:, 2 * cols] + ours[:, 2 * cols + 1]
    high, lowp = split16(mean_part)
    send = jnp.concatenate(
        [ours[:, cols : 2 * cols].astype(BF16), high[:, None], lowp[:, None], jnp.zeros((tok, 126), BF16)], axis=1
    )
    got = swap_x(send)
    y_sum = sy.s[0].astype(F32) + sy.y[0].astype(F32) + sy.total[0].astype(F32)
    mixed = (y_sum + lax.dynamic_slice_in_dim(h, t * cols, cols, 1)).astype(BF16)
    late.y[2], late.total[0], early.y[3], early.total[0], got, mixed = sync(
        late.y[2], late.total[0], early.y[3], early.total[0], got, mixed
    )
    late.side(3)
    late.ring(2)
    early.side(0)
    early.ring(3)
    x_full = tokens.astype(F32)
    r1 = lax.rsqrt(jnp.mean(x_full * x_full, axis=-1, keepdims=True) + epsilon)
    d_norm = ours[:, :cols] + got[:, :cols].astype(F32)
    mean = (mean_part + got[:, cols].astype(F32) + got[:, cols + 1].astype(F32))[:, None] / width
    x_cols = lax.dynamic_slice_in_dim(tokens, t * cols, cols, 1).astype(F32) * r1
    gain_row = lax.dynamic_slice_in_dim(aux_t[64:65], t * cols, cols, 1).astype(F32)
    grad_tokens = d_h + r1 * (d_norm * gain_row - x_cols * mean)
    late.y[3], late.total[0], early.y[0], early.total[0], grad_tokens = sync(
        late.y[3], late.total[0], early.y[0], early.total[0], grad_tokens
    )
    late.side(0)
    late.ring(3)
    grad_out, grad_router, gain_rows = kernel_call(
        early_end_body,
        [sds((qd, rows), F32), sds((rows, experts), F32), sds((8, rows), F32)],
        [idx, *early.last()],
        name="early_end",
    )
    grad_gain_moe = gain_rows[0]
    late.y[0], late.total[0], grad_out = sync(late.y[0], late.total[0], grad_out)
    grad_query, grad_key, grad_value, gain_rows = kernel_call(
        late_end_body,
        [sds((rows, qd), F32), sds((rows, kd), F32), sds((rows, kd), F32), sds((8, rows), F32)],
        [idx, *late.last()],
        name="late_end",
    )
    gain_part = gain_rows[0] + gain_rows[1]
    gain_part = gain_part + swap_c(gain_part)
    grad_gain_attn = gain_part + swap_x(gain_part)
    grad_gate, grad_up, grad_down = grads.outs[0]
    return (
        mixed,
        grad_tokens,
        grad_query,
        grad_key,
        grad_value,
        grad_out,
        grad_router,
        grad_gain_attn,
        grad_gain_moe,
        grad_gate,
        grad_up,
        grad_down,
    )


def solution(mesh):
    few = mesh.shape["tensor"] == 4 and mesh.shape["dp"] in (4, 8)
    return jax.shard_map(
        on_device_gathered if few else on_device,
        mesh=mesh,
        in_specs=(
            P("dp", None),
            P("dp", None),
            P("dp", None),
            P("dp", None),
            P("dp", "tensor"),
            P("dp", "tensor"),
            P("dp", "tensor"),
            P("tensor", "dp"),
            P("dp", None),
            P("dp"),
            P("dp"),
            P("dp", None, "tensor"),
            P("dp", None, "tensor"),
            P("dp", "tensor", None),
            P("dp", None),
        ),
        out_specs=(
            P("dp", "tensor"),
            P("dp", "tensor"),
            P("dp", "tensor"),
            P("dp", "tensor"),
            P("dp", "tensor"),
            P("tensor", "dp"),
            P("dp", None),
            P("dp"),
            P("dp"),
            P("dp", None, "tensor"),
            P("dp", None, "tensor"),
            P("dp", "tensor", None),
        ),
        check_vma=False,
    )
```

```python
import functools

import jax
import jax.numpy as jnp
import numpy as np
from jax import lax
from jax.experimental import pallas as pl
from jax.experimental.pallas import tpu as pltpu
from jax.sharding import PartitionSpec as P

HEAD_SIZE = 64


epsilon = 1e-05
negative_big = -1e30
rope_base = 10000.0
F32 = jnp.float32
BF16 = jnp.bfloat16
BLK = 256
PAD = 80
VMEM_LIMIT = 62 * 1024 * 1024


def rotary_tables(positions, head_width):
    half_width = head_width // 2
    inverse = rope_base ** (-(2.0 * jnp.arange(half_width, dtype=jnp.float32)) / head_width)
    angles = positions.astype(jnp.float32)[:, None] * inverse[None, :]
    return (jnp.cos(angles)[:, None, :], jnp.sin(angles)[:, None, :])


def apply_pair_rotation(values, cosine_values, sine_values):
    half_width = values.shape[-1] // 2
    first_half = values[..., :half_width]
    second_half = values[..., half_width:]
    return jnp.concatenate(
        [
            first_half * cosine_values - second_half * sine_values,
            second_half * cosine_values + first_half * sine_values,
        ],
        axis=-1,
    )


def unrotate_pairs(values, cosine_values, sine_values):
    half_width = values.shape[-1] // 2
    first_half = values[..., :half_width]
    second_half = values[..., half_width:]
    return jnp.concatenate(
        [
            first_half * cosine_values + second_half * sine_values,
            second_half * cosine_values - first_half * sine_values,
        ],
        axis=-1,
    )


def slot_table(chosen_rows, order_row, expert_count, capacity):
    flat_experts = chosen_rows.reshape(-1)
    pair_count = flat_experts.shape[0]
    sort_keys = flat_experts * pair_count + order_row
    ordering = jnp.argsort(sort_keys)
    sorted_experts = flat_experts[ordering]
    expert_ids = jnp.arange(expert_count, dtype=jnp.int32)
    counts = jnp.sum(
        (flat_experts[:, None] == expert_ids[None, :]).astype(jnp.int32), axis=0, dtype=jnp.int32
    )
    starts = jnp.cumsum(counts, dtype=jnp.int32) - counts
    ranks_sorted = jnp.arange(pair_count, dtype=jnp.int32) - starts[sorted_experts]
    ranks = jnp.zeros((pair_count,), jnp.int32).at[ordering].set(ranks_sorted)
    destination = jnp.where(
        ranks < capacity, flat_experts * capacity + ranks, expert_count * capacity
    )
    table = jnp.full((expert_count * capacity + 1,), pair_count, jnp.int32)
    table = table.at[destination].set(jnp.arange(pair_count, dtype=jnp.int32))
    return (table[: expert_count * capacity], destination)


def on_device(
    tokens,
    document_numbers,
    picks,
    drop_order,
    w_query,
    key_matrix,
    value_matrix,
    w_out,
    w_router,
    gain_attn,
    gain_moe,
    expert_gate,
    expert_up,
    expert_down,
    cotangent,
):
    ranks_dp = lax.axis_size("dp")
    tensor_index = lax.axis_index("tensor")
    wq, wk, wv, wo, wr, g_attn, g_moe = (
        lax.all_gather(w_query, "dp", axis=0, tiled=True),
        lax.all_gather(key_matrix, "dp", axis=0, tiled=True),
        lax.all_gather(value_matrix, "dp", axis=0, tiled=True),
        lax.all_gather(w_out, "dp", axis=1, tiled=True),
        lax.all_gather(w_router, "dp", axis=0, tiled=True),
        lax.all_gather(gain_attn, "dp", axis=0, tiled=True),
        lax.all_gather(gain_moe, "dp", axis=0, tiled=True),
    )
    tok_count, width = tokens.shape
    col_width = width // lax.axis_size("tensor")
    col_start = tensor_index * col_width
    q_heads = wq.shape[1] // HEAD_SIZE
    kv_heads = wk.shape[1] // HEAD_SIZE
    group_repeats = q_heads // kv_heads
    score_scale = HEAD_SIZE ** (-0.5)
    seg_row = document_numbers.reshape(-1)
    positions = jnp.arange(tok_count, dtype=jnp.int32)
    cosine_values, sine_values = rotary_tables(positions, HEAD_SIZE)
    x_full = tokens.astype(jnp.float32)
    r_attn = lax.rsqrt(jnp.mean(x_full * x_full, axis=-1, keepdims=True) + epsilon)
    x_hat = x_full * r_attn
    gain_one = g_attn.astype(jnp.float32)
    x_low = (x_hat * gain_one).astype(jnp.bfloat16)
    q_proj = jnp.dot(x_low, wq, preferred_element_type=jnp.float32)
    key_projected = jnp.dot(x_low, wk, preferred_element_type=jnp.float32)
    value_projected = jnp.dot(x_low, wv, preferred_element_type=jnp.float32)
    query_rotated = apply_pair_rotation(
        q_proj.reshape(tok_count, q_heads, HEAD_SIZE), cosine_values, sine_values
    ).astype(jnp.bfloat16)
    query_rotated = query_rotated.reshape(tok_count, kv_heads, group_repeats, HEAD_SIZE)
    key_rotated = apply_pair_rotation(
        key_projected.reshape(tok_count, kv_heads, HEAD_SIZE), cosine_values, sine_values
    ).astype(jnp.bfloat16)
    value_reduced = value_projected.astype(jnp.bfloat16).reshape(tok_count, kv_heads, HEAD_SIZE)
    block_rows = min(512, tok_count)
    block_count = tok_count // block_rows
    q_blocks = query_rotated.reshape(block_count, block_rows, kv_heads, group_repeats, HEAD_SIZE)
    seg_blocks = seg_row.reshape(block_count, block_rows)
    pos_blocks = positions.reshape(block_count, block_rows)

    def masked_scores(q_block, seg_block, pos_block):
        raw_scores = (
            jnp.einsum("qgrd,kgd->grqk", q_block, key_rotated, preferred_element_type=jnp.float32)
            * score_scale
        )
        allowed = (seg_block[:, None] == seg_row[None, :]) & (
            positions[None, :] <= pos_block[:, None]
        )
        return jnp.where(allowed, raw_scores, negative_big)

    def forward_block(inputs):
        q_block, seg_block, pos_block = inputs
        scores = masked_scores(q_block, seg_block, pos_block)
        highest_score = jnp.max(scores, axis=-1, keepdims=True)
        weights = jnp.exp(scores - highest_score)
        totals = jnp.sum(weights, axis=-1, keepdims=True)
        probs = (weights / totals).astype(jnp.bfloat16)
        heads_block = jnp.einsum(
            "grqk,kgd->qgrd", probs, value_reduced, preferred_element_type=jnp.float32
        )
        return (heads_block.astype(jnp.bfloat16), highest_score + jnp.log(totals))

    head_outputs, log_totals = lax.map(forward_block, (q_blocks, seg_blocks, pos_blocks))
    o_low = head_outputs.reshape(tok_count, q_heads * HEAD_SIZE)
    attn_terms = jnp.dot(o_low, wo, preferred_element_type=jnp.float32)
    attn = lax.psum(attn_terms, "tensor")
    h_full = x_full + attn
    r_moe = lax.rsqrt(jnp.mean(h_full * h_full, axis=-1, keepdims=True) + epsilon)
    h_hat = h_full * r_moe
    gain_two = g_moe.astype(jnp.float32)
    a_low = (h_hat * gain_two).astype(jnp.bfloat16)
    logits = jnp.dot(a_low, wr, preferred_element_type=jnp.float32)
    chosen = jnp.take_along_axis(logits, picks, axis=1)
    gates = jax.nn.softmax(chosen, axis=-1)
    top_count = picks.shape[1]
    experts_all = wr.shape[1]
    capacity = 9 * tok_count * top_count // (8 * experts_all)
    table, destination = slot_table(picks, drop_order.reshape(-1), experts_all, capacity)
    slot_tokens = table // top_count
    local_count = expert_gate.shape[0]
    h_cols = lax.dynamic_slice_in_dim(h_full, col_start, col_width, 1)
    d_out = cotangent.astype(jnp.float32)
    d_out_cols = lax.dynamic_slice_in_dim(d_out, col_start, col_width, 1)
    send_rows = jnp.concatenate([a_low, jnp.zeros((1, width), jnp.bfloat16)], axis=0)[slot_tokens]
    expert_in = lax.all_to_all(
        send_rows.reshape(ranks_dp, -1, width), "dp", split_axis=0, concat_axis=0, tiled=True
    )
    expert_in = expert_in.reshape(ranks_dp, local_count, capacity, width)
    gate_val = jnp.einsum(
        "sjcd,jdf->sjcf", expert_in, expert_gate, preferred_element_type=jnp.float32
    )
    up_val = jnp.einsum("sjcd,jdf->sjcf", expert_in, expert_up, preferred_element_type=jnp.float32)
    sigmoid_gate = jax.nn.sigmoid(gate_val)
    silu_gate = gate_val * sigmoid_gate
    hidden_low = (silu_gate * up_val).astype(jnp.bfloat16)
    slab_count = 4
    slab_rows = ranks_dp // slab_count
    out_pieces = []
    for slab_index in range(slab_count):
        lower = slab_index * slab_rows
        partial_out = jnp.einsum(
            "sjcf,jfd->sjcd",
            hidden_low[lower : lower + slab_rows],
            expert_down,
            preferred_element_type=jnp.float32,
        )
        out_pieces.append(
            lax.psum_scatter(
                partial_out.astype(jnp.bfloat16), "tensor", scatter_dimension=3, tiled=True
            )
        )
    expert_out = jnp.concatenate(out_pieces, axis=0).reshape(
        ranks_dp, local_count * capacity, col_width
    )
    returned = lax.all_to_all(expert_out, "dp", split_axis=0, concat_axis=0, tiled=True).reshape(
        experts_all * capacity, col_width
    )
    returned = jnp.concatenate([returned, jnp.zeros((1, col_width), jnp.bfloat16)], axis=0)
    pair_outs = returned[destination].reshape(tok_count, top_count, col_width).astype(jnp.float32)
    mixed = (h_cols + jnp.sum(gates[:, :, None] * pair_outs, axis=1)).astype(jnp.bfloat16)
    d_gate_terms = jnp.sum(pair_outs * d_out_cols[:, None, :], axis=2)
    d_pairs = (
        (gates[:, :, None] * d_out_cols[:, None, :]).astype(jnp.bfloat16).reshape(-1, col_width)
    )
    d_pairs = jnp.concatenate([d_pairs, jnp.zeros((1, col_width), jnp.bfloat16)], axis=0)
    d_send = d_pairs[table].reshape(ranks_dp, local_count * capacity, col_width)
    d_arrived = lax.all_to_all(d_send, "dp", split_axis=0, concat_axis=0, tiled=True)
    d_arrived = d_arrived.reshape(ranks_dp, local_count, capacity, col_width)
    grad_expert_gate = jnp.zeros(expert_gate.shape, jnp.float32)
    grad_expert_up = jnp.zeros(expert_up.shape, jnp.float32)
    grad_expert_down = jnp.zeros(expert_down.shape, jnp.float32)
    back_pieces = []
    for slab_index in range(slab_count):
        lower = slab_index * slab_rows
        upper = lower + slab_rows
        d_expert_out = lax.all_gather(d_arrived[lower:upper], "tensor", axis=3, tiled=True)
        d_hidden = jnp.einsum(
            "sjcd,jfd->sjcf", d_expert_out, expert_down, preferred_element_type=jnp.float32
        )
        grad_expert_down = grad_expert_down + jnp.einsum(
            "sjcf,sjcd->jfd",
            hidden_low[lower:upper],
            d_expert_out,
            preferred_element_type=jnp.float32,
        )
        slab_gate = gate_val[lower:upper]
        slab_sigmoid = sigmoid_gate[lower:upper]
        d_gate_low = (
            d_hidden * up_val[lower:upper] * slab_sigmoid * (1.0 + slab_gate * (1.0 - slab_sigmoid))
        ).astype(jnp.bfloat16)
        d_up_low = (d_hidden * silu_gate[lower:upper]).astype(jnp.bfloat16)
        slab_inputs = expert_in[lower:upper]
        grad_expert_gate = grad_expert_gate + jnp.einsum(
            "sjcd,sjcf->jdf", slab_inputs, d_gate_low, preferred_element_type=jnp.float32
        )
        grad_expert_up = grad_expert_up + jnp.einsum(
            "sjcd,sjcf->jdf", slab_inputs, d_up_low, preferred_element_type=jnp.float32
        )
        d_in_terms = jnp.einsum(
            "sjcf,jdf->sjcd", d_gate_low, expert_gate, preferred_element_type=jnp.float32
        ) + jnp.einsum("sjcf,jdf->sjcd", d_up_low, expert_up, preferred_element_type=jnp.float32)
        back_pieces.append(
            lax.psum_scatter(
                d_in_terms.astype(jnp.bfloat16), "tensor", scatter_dimension=3, tiled=True
            )
        )
    d_expert_in = jnp.concatenate(back_pieces, axis=0).reshape(
        ranks_dp, local_count * capacity, col_width
    )
    d_returned = lax.all_to_all(d_expert_in, "dp", split_axis=0, concat_axis=0, tiled=True).reshape(
        experts_all * capacity, col_width
    )
    d_returned = jnp.concatenate([d_returned, jnp.zeros((1, col_width), jnp.bfloat16)], axis=0)
    d_token_cols = jnp.sum(
        d_returned[destination].reshape(tok_count, top_count, col_width).astype(jnp.float32), axis=1
    )
    d_experts_full, d_gate_parts = (
        lax.all_gather(d_token_cols.astype(jnp.bfloat16), "tensor", axis=1, tiled=True).astype(
            d_token_cols.dtype
        ),
        lax.all_gather(d_gate_terms.astype(jnp.bfloat16), "tensor", axis=1, tiled=True).astype(
            d_gate_terms.dtype
        ),
    )
    d_gates = jnp.sum(d_gate_parts.reshape(tok_count, -1, top_count), axis=1)
    d_chosen = gates * (d_gates - jnp.sum(gates * d_gates, axis=-1, keepdims=True))
    one_hot = (picks[:, :, None] == jnp.arange(experts_all, dtype=jnp.int32)[None, None, :]).astype(
        jnp.float32
    )
    d_logits = jnp.sum(d_chosen[:, :, None] * one_hot, axis=1).astype(jnp.bfloat16)
    grad_router = jnp.dot(a_low.T, d_logits, preferred_element_type=jnp.float32)
    d_norm_moe = d_experts_full + jnp.dot(d_logits, wr.T, preferred_element_type=jnp.float32)
    grad_gain_moe = jnp.sum(d_norm_moe * h_hat, axis=0)
    d_scaled = d_norm_moe * gain_two
    d_h = d_out + r_moe * (d_scaled - h_hat * jnp.mean(d_scaled * h_hat, axis=-1, keepdims=True))
    d_h_low = d_h.astype(jnp.bfloat16)
    grad_out = jnp.dot(o_low.T, d_h_low, preferred_element_type=jnp.float32)
    d_heads = jnp.dot(d_h_low, wo.T, preferred_element_type=jnp.float32).astype(jnp.bfloat16)
    d_blocks = d_heads.reshape(block_count, block_rows, kv_heads, group_repeats, HEAD_SIZE)

    def backward_block(inputs):
        q_block, d_block, log_block, seg_block, pos_block = inputs
        scores = masked_scores(q_block, seg_block, pos_block)
        probs = jnp.exp(scores - log_block)
        d_probs = jnp.einsum(
            "qgrd,kgd->grqk", d_block, value_reduced, preferred_element_type=jnp.float32
        )
        centre = jnp.sum(probs * d_probs, axis=-1, keepdims=True)
        d_scores = (probs * (d_probs - centre)).astype(jnp.bfloat16)
        d_query = (
            jnp.einsum("grqk,kgd->qgrd", d_scores, key_rotated, preferred_element_type=jnp.float32)
            * score_scale
        )
        d_key = (
            jnp.einsum("grqk,qgrd->kgd", d_scores, q_block, preferred_element_type=jnp.float32)
            * score_scale
        )
        d_value = jnp.einsum(
            "grqk,qgrd->kgd",
            probs.astype(jnp.bfloat16),
            d_block,
            preferred_element_type=jnp.float32,
        )
        return (d_query, d_key, d_value)

    d_query_all, d_key_parts, d_value_parts = lax.map(
        backward_block, (q_blocks, d_blocks, log_totals, seg_blocks, pos_blocks)
    )
    d_query_low = unrotate_pairs(
        d_query_all.reshape(tok_count, q_heads, HEAD_SIZE), cosine_values, sine_values
    )
    d_query_low = d_query_low.astype(jnp.bfloat16).reshape(tok_count, q_heads * HEAD_SIZE)
    d_key_low = unrotate_pairs(jnp.sum(d_key_parts, axis=0), cosine_values, sine_values)
    d_key_low = d_key_low.astype(jnp.bfloat16).reshape(tok_count, kv_heads * HEAD_SIZE)
    d_value_low = (
        jnp.sum(d_value_parts, axis=0).astype(jnp.bfloat16).reshape(tok_count, kv_heads * HEAD_SIZE)
    )
    grad_query = jnp.dot(x_low.T, d_query_low, preferred_element_type=jnp.float32)
    grad_key = jnp.dot(x_low.T, d_key_low, preferred_element_type=jnp.float32)
    grad_value = jnp.dot(x_low.T, d_value_low, preferred_element_type=jnp.float32)
    d_norm_terms = (
        jnp.dot(d_query_low, wq.T, preferred_element_type=jnp.float32)
        + jnp.dot(d_key_low, wk.T, preferred_element_type=jnp.float32)
        + jnp.dot(d_value_low, wv.T, preferred_element_type=jnp.float32)
    )
    d_norm_attn = lax.psum(d_norm_terms.astype(jnp.bfloat16), "tensor").astype(jnp.float32)
    grad_gain_attn = jnp.sum(d_norm_attn * x_hat, axis=0)
    d_scaled_in = d_norm_attn * gain_one
    d_input = d_h + r_attn * (
        d_scaled_in - x_hat * jnp.mean(d_scaled_in * x_hat, axis=-1, keepdims=True)
    )
    grad_tokens = lax.dynamic_slice_in_dim(d_input, col_start, col_width, 1)
    grad_query, grad_key, grad_value, grad_out, grad_router, grad_gain_attn, grad_gain_moe = (
        lax.psum_scatter(grad_query, "dp", scatter_dimension=0, tiled=True),
        lax.psum_scatter(grad_key, "dp", scatter_dimension=0, tiled=True),
        lax.psum_scatter(grad_value, "dp", scatter_dimension=0, tiled=True),
        lax.psum_scatter(grad_out, "dp", scatter_dimension=1, tiled=True),
        lax.psum_scatter(grad_router, "dp", scatter_dimension=0, tiled=True),
        lax.psum_scatter(grad_gain_attn, "dp", scatter_dimension=0, tiled=True),
        lax.psum_scatter(grad_gain_moe, "dp", scatter_dimension=0, tiled=True),
    )
    return (
        mixed,
        grad_tokens,
        grad_query,
        grad_key,
        grad_value,
        grad_out,
        grad_router,
        grad_gain_attn,
        grad_gain_moe,
        grad_expert_gate,
        grad_expert_up,
        grad_expert_down,
    )


def mm(a, b):
    return jnp.dot(a, b, preferred_element_type=F32)


def mm_nt(a, b):
    return lax.dot_general(a, b, (((1,), (1,)), ((), ())), preferred_element_type=F32)


def mm_tn(a, b):
    return lax.dot_general(a, b, (((0,), (0,)), ((), ())), preferred_element_type=F32)


def bytes_of(arrays):
    return sum(int(np.prod(a.shape)) * jnp.dtype(a.dtype).itemsize for a in arrays)


def after(v, *done):
    return lax.optimization_barrier((v, *done))[0]


def sync(*values):
    return lax.optimization_barrier(values)


def kernel_call(body, outs, ins, scratch=(), flops=0, name=None):
    smem = pl.BlockSpec(memory_space=pltpu.SMEM)
    vmem = pl.BlockSpec(memory_space=pltpu.VMEM)
    nbytes = bytes_of(list(ins[1:]) + list(outs))
    need = nbytes + bytes_of(scratch) + (16 << 20)
    return pl.pallas_call(
        body,
        out_shape=[sds(o.shape, o.dtype) for o in outs],
        in_specs=[smem] + [vmem] * (len(ins) - 1),
        out_specs=[vmem] * len(outs),
        scratch_shapes=list(scratch),
        compiler_params=pltpu.CompilerParams(vmem_limit_bytes=min(need, VMEM_LIMIT)),
        cost_estimate=pl.CostEstimate(flops=int(flops), bytes_accessed=nbytes, transcendentals=0),
        name=name,
    )(*ins)


def sds(shape, dtype):
    return jax.ShapeDtypeStruct(shape, dtype)


def slots_body(capacity, idx, picks_ref, order_ref, pos_ref):
    experts, tok = pos_ref.shape
    ids = lax.broadcasted_iota(jnp.int32, (experts, tok), 0)
    never = 1 << 28
    order = jnp.full((experts, tok), never, jnp.int32)
    for k in range(picks_ref.shape[0]):
        order = jnp.where(picks_ref[k : k + 1, :] == ids, order_ref[k : k + 1, :], order)
    limit = jnp.zeros((experts, 1), jnp.int32)
    step = 1
    while step < picks_ref.shape[0] * tok:
        step *= 2
    while step:
        tried = limit + step
        count = jnp.sum((order < tried).astype(F32), axis=1, keepdims=True)
        limit = jnp.where(count <= capacity, tried, limit)
        step //= 2
    kept = order < limit
    rows = lax.broadcasted_iota(jnp.int32, (tok, tok), 0)
    cols = lax.broadcasted_iota(jnp.int32, (tok, tok), 1)
    before = (rows < cols).astype(F32).astype(BF16)
    place = mm(kept.astype(F32).astype(BF16), before)
    pos_ref[...] = jnp.where(kept, place, jnp.where(order < never, -1.0, -2.0)).astype(BF16)


def place_body(nz, idx, *refs):
    out = refs[-1]
    rows, cols = refs[0].shape[0], out.shape[1]
    for k in range(nz):
        base = lax.rem(idx[1] - k + nz, nz) * 2
        for q in range(2):
            block = base + (idx[2] if q == 0 else 1 - idx[2])
            out[pl.ds(pl.multiple_of(block * rows, rows), rows), :] = refs[q * nz + k][:, :cols]


def place_both_body(nz, idx, *refs):
    out = refs[-1]
    rows = refs[0].shape[0]
    for k in range(nz):
        base = lax.rem(idx[1] - k + nz, nz) * 2
        for q in range(2):
            block = base + (idx[2] if q == 0 else 1 - idx[2])
            at = pl.ds(pl.multiple_of(block * rows, rows), rows)
            out[0, at, :] = refs[q * nz + k][:, refs[0].shape[1] - out.shape[2] :]
            out[1, at, :] = refs[2 * nz + k][q]


def rotate(v, cos, sin, lane_low):
    swapped = jnp.where(lane_low, pltpu.roll(v, 96, 1), pltpu.roll(v, 32, 1))
    return v * cos + swapped * sin


def low_lanes(tok):
    return lax.rem(lax.broadcasted_iota(jnp.int32, (tok, 128), 1), 64) < 32


def attend_body(nz, idx, *refs):
    blocks = refs[: 2 * nz]
    x_ref, seg_row, seg_col, cos_ref, sin_ref = refs[2 * nz : 2 * nz + 5]
    refs = refs[2 * nz + 5 :]
    (o_ref, q_ref, k_ref, v_ref, w_ref, aux_ref), heads_p, (bias_ref, qkv_ref) = refs[:6], refs[6:-2], refs[-2:]
    place_body(nz, idx, *blocks, w_ref)
    tok, width = x_ref.shape
    qd, kd = q_ref.shape[1], k_ref.shape[1]
    used = qd + 2 * kd
    aux = w_ref[:, used:].astype(F32).T
    aux_ref[...] = aux.astype(BF16)
    x = x_ref[...].astype(F32)
    r1 = lax.rsqrt(jnp.mean(x * x, axis=1, keepdims=True) + epsilon)
    x_low = (x * r1 * aux[64:65, :]).astype(BF16)
    qkv_ref[...] = mm(x_low, w_ref[:, :used])
    lanes = low_lanes(tok)
    cos, sin = cos_ref[...], sin_ref[...]
    for b in range(qd // 128):
        rot = rotate(qkv_ref[:, b * 128 : b * 128 + 128], cos, sin, lanes).astype(BF16)
        q_ref[:, b * 128 : b * 128 + 128] = (rot.astype(F32) * HEAD_SIZE**-0.5).astype(BF16)
    for b in range(kd // 128):
        rot = rotate(qkv_ref[:, qd + b * 128 : qd + b * 128 + 128], cos, sin, lanes)
        k_ref[:, b * 128 : b * 128 + 128] = rot.astype(BF16)
    v_ref[...] = qkv_ref[:, qd + kd :].astype(BF16)
    rows = lax.broadcasted_iota(jnp.int32, (tok, tok), 0)
    cols = lax.broadcasted_iota(jnp.int32, (tok, tok), 1)
    allowed = (seg_col[...] == seg_row[...]) & (cols <= rows)
    bias_ref[...] = jnp.where(allowed, 0.0, negative_big)
    heads, groups = qd // HEAD_SIZE, kd // HEAD_SIZE
    for h in range(heads):
        g = h // (heads // groups)
        a, b = h * HEAD_SIZE, g * HEAD_SIZE
        s = mm_nt(q_ref[:, a : a + HEAD_SIZE], k_ref[:, b : b + HEAD_SIZE]) + bias_ref[...]
        e = jnp.exp(s - jnp.max(s, axis=1, keepdims=True))
        p = (e / jnp.sum(e, axis=1, keepdims=True)).astype(BF16)
        heads_p[h][...] = p
        o_ref[:, a : a + HEAD_SIZE] = mm(p, v_ref[:, b : b + HEAD_SIZE]).astype(BF16)


def column_places(idx, width):
    x, c = idx[3], idx[4]
    part = width // 4

    def at(b):
        return pl.ds(pl.multiple_of(b * part, 128), part)

    return [at(2 * x + c), at(2 * (1 - x) + c)], [at(2 * x + 1 - c), at(2 * (1 - x) + 1 - c)]


def out_body(idx, x_ref, o0, o1, o2, o3, w01, w23, aux_ref, h_ref, low_ref, ring_ref):
    tok, width = x_ref.shape
    attn = mm_nt(o0[...], w01[0]) + mm_nt(o1[...], w01[1])
    attn = attn + (mm_nt(o2[...], w23[0]) + mm_nt(o3[...], w23[1]))
    h = x_ref[...].astype(F32) + attn
    h_ref[...] = h
    r2 = lax.rsqrt(jnp.mean(h * h, axis=1, keepdims=True) + epsilon)
    low_ref[...] = (h * r2 * aux_ref[64:66, :].astype(F32)[1:2, :]).astype(BF16)
    part = width // 4
    for m, at in enumerate(column_places(idx, width)[0]):
        ring_ref[:, m * part : m * part + part] = low_ref[:, at]


def masked_gates(logits, pos):
    picked = pos > -1.5
    shown = jnp.where(picked, logits, negative_big)
    e = jnp.where(picked, jnp.exp(shown - jnp.max(shown, axis=0, keepdims=True)), 0.0)
    return e / jnp.sum(e, axis=0, keepdims=True)


def split16(v):
    high = v.astype(BF16)
    return high, (v - high.astype(F32)).astype(BF16)


def experts_body(
    local, idx, aux_ref, sel_ref, selt_ref, slot_ref, slott_ref, *refs
):
    rows_hbm, d_hbm, (gu_hbm, down_hbm), refs = refs[:4], refs[4:8], refs[8:10], refs[10:]
    dx_hbm, y_hbm, (xe_hbm, d0_hbm, dgu_hbm, hd_hbm) = refs[:2], refs[2:4], refs[4:8]
    am_s, an_s, dm_s, dn_s, gu_s, down_s = refs[8:14]
    dx_out, y_out, (xe_s, d0_s, dgu_s, hd_s) = refs[14:16], refs[16:18], refs[18:22]
    pos_s, gate_s, y_s, dx_s, dgr_s, oh_s, oht_s, in_sem, w_sem, out_sem = refs[22:]
    tok, width = am_s.shape[1], xe_s.shape[3]
    half = pos_s.shape[0] // 2
    x, c = idx[3], idx[4]
    part = width // 4
    sides = column_places(idx, width)
    hidden = down_s.shape[1]
    both, slots = 2 * PAD, local * PAD

    def arriving(q):
        pairs = [(rows_hbm[q], am_s.at[q]), (rows_hbm[2 + q], an_s.at[q])]
        for i, d_s in enumerate((dm_s, dn_s)):
            for m in range(2):
                pairs.append((d_hbm[2 * i + m].at[q], d_s.at[q, :, m * part : m * part + part]))
        return [pltpu.make_async_copy(h, v, in_sem.at[q, i]) for i, (h, v) in enumerate(pairs)]

    weights = [pltpu.make_async_copy(gu_hbm, gu_s, w_sem.at[0]), pltpu.make_async_copy(down_hbm, down_s, w_sem.at[1])]
    for cp in arriving(0):
        cp.start()
    for cp in arriving(1):
        cp.start()
    for cp in weights:
        cp.start()
    leaving = []

    def leave(src, dst):
        cp = pltpu.make_async_copy(src, dst, out_sem.at[len(leaving)])
        cp.start()
        leaving.append(cp)

    sel, selt = sel_ref[...], selt_ref[...]
    for q in range(2):
        for cp in arriving(q):
            cp.wait()
        for d_s, core in ((dm_s, c), (dn_s, 1 - c)):
            for m, chip in enumerate((x, 1 - x)):
                at = pl.ds(pl.multiple_of((2 * chip + core) * 128, 128), 128)
                pos_s[:, at] = d_s[q, tok:, m * part : m * part + 128]
        pos = pos_s[...]
        logits = jnp.zeros(pos.shape, F32)
        for rows, places in zip((am_s, an_s), sides):
            for m, at in enumerate(places):
                logits = logits + mm_nt(aux_ref[: pos.shape[0], at], rows[q, :, m * part : m * part + part])
        gates = masked_gates(logits, pos.astype(F32))
        hot = (mm(sel, pos) == slot_ref[...]).astype(F32).astype(BF16)
        oh_s[q] = hot
        oht_s[q] = (mm_tn(pos, selt) == slott_ref[...]).astype(F32).astype(BF16)
        high, low = split16(gates)
        spread = (mm_nt(hot, high) + mm_nt(hot, low)) * sel.astype(F32)
        gate_s[:, q] = jnp.sum(spread, axis=1, keepdims=True).reshape(local, PAD, 1)
        for rows, outs in (((am_s, an_s), xe_s), ((dm_s, dn_s), d0_s)):
            for side, places in enumerate(sides):
                got = mm(hot, rows[side][q, :tok, :]).astype(BF16)
                for m, at in enumerate(places):
                    outs[:, q, :, at] = got[:, m * part : m * part + part].reshape(local, PAD, part)
    leave(xe_s, xe_hbm)
    leave(d0_s, d0_hbm)
    for cp in weights:
        cp.wait()
    for j in range(local):
        gu = mm(xe_s[j].reshape(both, width), gu_s[j])
        t = mm_nt(d0_s[j].reshape(both, width), down_s[j])
        gate = gate_s[j].reshape(both, 1)
        g, u = gu[:, :hidden], gu[:, hidden:]
        sg = jax.nn.sigmoid(g)
        silu = g * sg
        hd = (silu * u).astype(BF16)
        dhd = gate * t
        dg = (dhd * u * sg * (1.0 + g * (1.0 - sg))).astype(BF16)
        du = (dhd * silu).astype(BF16)
        dgate = jnp.sum(hd.astype(F32) * t, axis=1, keepdims=True)
        dgr_s[j] = jnp.broadcast_to(dgate, (both, dgr_s.shape[3])).reshape(2, PAD, dgr_s.shape[3])
        hd_s[j] = (hd.astype(F32) * gate).astype(BF16).reshape(2, PAD, hidden)
        dgu = jnp.concatenate([dg, du], axis=1)
        dgu_s[j] = dgu.reshape(2, PAD, 2 * hidden)
        dx_s[j] = mm_nt(dgu, gu_s[j]).astype(BF16).reshape(2, PAD, width)
        y = mm(hd, down_s[j])
        y_s[j] = (y.astype(BF16).astype(F32) * gate).astype(BF16).reshape(2, PAD, width)
    leave(hd_s, hd_hbm)
    leave(dgu_s, dgu_hbm)
    for q in range(2):
        hot, hott = oh_s[q], oht_s[q]

        def scatter(rows_s, outs):
            for out, places in zip(outs, sides):
                rows = [rows_s[:, q, :, at].reshape(slots, part) for at in places]
                out[q, :tok, :] = mm(hott, jnp.concatenate(rows, axis=1)).astype(BF16)

        scatter(dx_s, dx_out)
        spread = (dgr_s[:, q].reshape(slots, -1) * sel.astype(F32)).astype(BF16)
        pos_s[...] = mm_tn(spread, hot).astype(BF16)
        for out, at in zip(dx_out, (c, 1 - c)):
            out[q, tok:, :tok] = pos_s[pl.ds(pl.multiple_of(at * half, half), half), :]
            out[q, tok:, tok:] = jnp.zeros((half, out.shape[2] - tok), BF16)
        for v, h in zip(dx_out, dx_hbm):
            leave(v.at[q], h.at[q])
        scatter(y_s, y_out)
        for v, h in zip(y_out, y_hbm):
            leave(v.at[q], h.at[q])
    for cp in leaving:
        cp.wait()


def experts_call(idx, a, d, gu, down, aux_t, sel, slot_col, slot_row):
    local, width, hidden2 = gu.shape
    hidden = hidden2 // 2
    experts = sel.shape[1]
    tok = a[0].shape[0]
    rows = tok + experts // 2
    slots = local * PAD
    big = (local, 2, PAD, width)
    outs = [sds((2, n, width // 2), BF16) for n in (rows, rows, tok, tok)]
    outs += [sds(big, BF16), sds(big, BF16), sds((local, 2, PAD, hidden2), BF16), sds((local, 2, PAD, hidden), BF16)]
    kept = [idx, aux_t, sel, sel.T, slot_col, slot_row]
    scratch = [pltpu.VMEM((2, n, width // 2), BF16) for n in (tok, tok, tok + experts, tok + experts)]
    scratch += [pltpu.VMEM(v.shape, v.dtype) for v in [gu, down] + outs]
    scratch += [
        pltpu.VMEM((experts, tok), BF16), pltpu.VMEM((local, 2, PAD, 1), F32), pltpu.VMEM(big, BF16), pltpu.VMEM(big, BF16),
        pltpu.VMEM((local, 2, PAD, experts), F32), pltpu.VMEM((2, slots, tok), BF16), pltpu.VMEM((2, tok, slots), BF16),
    ]
    scratch += [pltpu.SemaphoreType.DMA((2, 6)), pltpu.SemaphoreType.DMA((2,)), pltpu.SemaphoreType.DMA((20,))]
    moved = [*a, *d, gu, down]
    smem = pl.BlockSpec(memory_space=pltpu.SMEM)
    vmem = pl.BlockSpec(memory_space=pltpu.VMEM)
    hbm = pl.BlockSpec(memory_space=pl.ANY)
    return pl.pallas_call(
        functools.partial(experts_body, local),
        out_shape=outs,
        in_specs=[smem] + [vmem] * 5 + [hbm] * len(moved),
        out_specs=[hbm] * len(outs),
        scratch_shapes=scratch,
        compiler_params=pltpu.CompilerParams(vmem_limit_bytes=VMEM_LIMIT),
        cost_estimate=pl.CostEstimate(
            flops=16 * slots * tok * width + 36 * slots * width * hidden,
            bytes_accessed=bytes_of(moved + outs),
            transcendentals=0,
        ),
        name="experts",
    )(*kept, *moved)


def in_ring_order(nz, idx, blocks_s, groups, outs):
    bases = [lax.rem(idx[1] - k + nz, nz) * 2 for k in range(nz)]
    for k in range(nz):
        outs[k][...] = blocks_s[bases[k] + idx[2]]
    for out, group in zip(outs[nz:], groups):
        for i, k in enumerate(group):
            out[i] = blocks_s[bases[k] + 1 - idx[2]]


def sent_groups(nz):
    early = [list(range(1, nz)), [0]]
    late = [[1], list(range(2, nz)), [0]]
    return [g for g in early if g], [g for g in late if g]


def hidden_back_body(nz, idx, fm_ref, fn_ref, h_ref, low_ref, aux_ref, pos_ref, dout_ref, o_ref, w_ref,
                     dh_ref, do_ref, *refs):
    outs, (full_s, dg_s, rs_s) = refs[:-3], refs[-3:]
    tok, width = h_ref.shape
    c, experts = idx[4], pos_ref.shape[0]
    half = experts // 2
    part = width // 4
    for ref, places in zip((fm_ref, fn_ref), column_places(idx, width)):
        for m, at in enumerate(places):
            full_s[:, at] = ref[:tok, m * part : m * part + part].astype(F32)
    for ref, at in ((fm_ref, c), (fn_ref, 1 - c)):
        dg_s[pl.ds(pl.multiple_of(at * half, half), half), :] = ref[tok:, :tok].astype(F32)
    low = low_ref[...]
    router = aux_ref[:experts, :]
    gates = masked_gates(mm_nt(router, low), pos_ref[...].astype(F32))
    dgates = dg_s[...]
    dlogits = (gates * (dgates - jnp.sum(gates * dgates, axis=0, keepdims=True))).astype(BF16)
    h = h_ref[...]
    r2 = lax.rsqrt(jnp.mean(h * h, axis=1, keepdims=True) + epsilon)
    ah = h * r2
    da = full_s[...] + mm_tn(dlogits, router)
    gain_grad = jnp.sum(da * ah, axis=0, keepdims=True)
    scaled = da * aux_ref[64:66, :].astype(F32)[1:2, :]
    dh = dout_ref[...].astype(F32) + r2 * (scaled - ah * jnp.mean(scaled * ah, axis=1, keepdims=True))
    full_s[...] = dh
    cols = dh_ref.shape[1]
    t = idx[3] * 2 + c
    dh_ref[...] = full_s[:, pl.ds(pl.multiple_of(t * cols, 128), cols)]
    dhb = dh.astype(BF16)
    do_ref[...] = mm(dhb, w_ref[0]).astype(BF16)
    turned = mm_tn(dhb, o_ref[...]).astype(BF16)
    side = jnp.concatenate([mm(dlogits, low), gain_grad, jnp.zeros((63, width), F32)], axis=0)
    side = side.T.astype(BF16)
    rows = rs_s.shape[1]
    for i in range(2 * nz):
        rs_s[i, :, :cols] = turned[i * rows : i * rows + rows]
        rs_s[i, :, cols:] = side[i * rows : i * rows + rows]
    in_ring_order(nz, idx, rs_s, sent_groups(nz)[0], outs)


def attend_back_body(nz, idx, do_ref, v_ref, k_ref, q_ref, cos_ref, sin_ref, x_ref, aux_ref, w_ref, *refs):
    heads_p, refs = refs[: q_ref.shape[1] // HEAD_SIZE], refs[q_ref.shape[1] // HEAD_SIZE :]
    dm_ref, dn_ref, outs, (dq_s, dqkv_s, dxn_s, rs_ref) = refs[0], refs[1], refs[2:-4], refs[-4:]
    tok, width = x_ref.shape
    qd, kd = q_ref.shape[1], k_ref.shape[1]
    heads, groups = qd // HEAD_SIZE, kd // HEAD_SIZE
    scale = HEAD_SIZE**-0.5
    each = heads // groups
    for g in range(groups):
        b = g * HEAD_SIZE
        kg, vg = k_ref[:, b : b + HEAD_SIZE], v_ref[:, b : b + HEAD_SIZE]
        dk = jnp.zeros((tok, HEAD_SIZE), F32)
        dv = jnp.zeros((tok, HEAD_SIZE), F32)
        for h in range(g * each, (g + 1) * each):
            a = h * HEAD_SIZE
            doh = do_ref[:, a : a + HEAD_SIZE]
            p = heads_p[h][...].astype(F32)
            dp = mm_nt(doh, vg)
            ds = (p * (dp - jnp.sum(p * dp, axis=1, keepdims=True))).astype(BF16)
            dq_s[:, a : a + HEAD_SIZE] = mm(ds, kg) * scale
            dk = dk + mm_tn(ds, q_ref[:, a : a + HEAD_SIZE])
            dv = dv + mm_tn(heads_p[h][...], doh)
        dq_s[:, qd + b : qd + b + HEAD_SIZE] = dk
        dqkv_s[:, qd + kd + b : qd + kd + b + HEAD_SIZE] = dv.astype(BF16)
    lanes = low_lanes(tok)
    cos, sin = cos_ref[...], -sin_ref[...]
    for b in range((qd + kd) // 128):
        at = slice(b * 128, b * 128 + 128)
        dqkv_s[:, at] = rotate(dq_s[:, at], cos, sin, lanes).astype(BF16)
    used = qd + 2 * kd
    x = x_ref[...].astype(F32)
    r1 = lax.rsqrt(jnp.mean(x * x, axis=1, keepdims=True) + epsilon)
    xh = x * r1
    gain = aux_ref[64:65, :].astype(F32)
    x_low = (xh * gain).astype(BF16)
    dqkv = dqkv_s[...]
    rows = width // rs_ref.shape[0]
    grads = mm_tn(x_low, dqkv).astype(BF16)
    dxn = mm_nt(dqkv, w_ref[:, :used])
    gain_high, gain_low = split16(jnp.sum(dxn * xh, axis=0, keepdims=True))
    pads = jnp.zeros((14, rows), BF16)
    for i in range(rs_ref.shape[0]):
        rs_ref[i, :rows, :] = grads[i * rows : i * rows + rows, :]
        at = slice(i * rows, i * rows + rows)
        tail = jnp.concatenate([gain_high[:, at].astype(F32), gain_low[:, at].astype(F32), pads.astype(F32)], axis=0)
        rs_ref[i, rows:, :] = jnp.zeros((16, used), BF16)
        rs_ref[i, rows:, :rows] = tail.astype(BF16)
    in_ring_order(nz, idx, rs_ref, sent_groups(nz)[1], outs)
    total = jnp.sum(dxn * xh * gain, axis=1, keepdims=True)
    high, low = split16(total)
    lane = lax.broadcasted_iota(jnp.int32, (tok, 128), 1)
    side = jnp.where(lane == 0, high.astype(F32), jnp.where(lane == 1, low.astype(F32), 0.0)).astype(BF16)
    cols = width // 4
    for i in range(4):
        dxn_s[i] = dxn[:, i * cols : i * cols + cols].astype(BF16)
    ix, c = idx[3], idx[4]
    for ref, core in ((dm_ref, c), (dn_ref, 1 - c)):
        ref[:, :cols] = dxn_s[2 * ix + core]
        ref[:, cols : 2 * cols] = dxn_s[2 * (1 - ix) + core]
        ref[:, 2 * cols :] = side


def early_end_body(idx, kept, side, ring, out_ref, router_ref, gain_ref):
    total = kept[...].astype(F32) + side[...].astype(F32) + ring[...].astype(F32)
    cols, experts = out_ref.shape[0], router_ref.shape[1]
    out_ref[...] = total[:, :cols].T
    router_ref[...] = total[:, cols : cols + experts]
    gain_ref[...] = total[:, cols:].T[experts : experts + 8]


def late_end_body(idx, kept, side, ring, query_ref, key_ref, value_ref, gain_ref):
    total = kept[...].astype(F32) + side[...].astype(F32) + ring[...].astype(F32)
    rows, qd = query_ref.shape
    kd = key_ref.shape[1]
    gain_ref[...] = total[rows : rows + 8, : gain_ref.shape[1]]
    query_ref[...] = total[:rows, :qd]
    key_ref[...] = total[:rows, qd : qd + kd]
    value_ref[...] = total[:rows, qd + kd :]


def expert_grads_body(count, *refs):
    xe, d0, dgu, hd = (refs[i * count : i * count + count] for i in range(4))
    gate_ref, up_ref, down_ref = refs[4 * count :]
    hidden = gate_ref.shape[2]

    def join(group, at=slice(None)):
        return jnp.concatenate([r[0, :, :, at].reshape(2 * PAD, -1) for r in group], axis=0)

    d_gu, hd_all = join(dgu), join(hd)
    for b in range(gate_ref.shape[1] // BLK):
        at = slice(b * BLK, b * BLK + BLK)
        both = mm_tn(join(xe, at), d_gu)
        gate_ref[0, at, :] = both[:, :hidden]
        up_ref[0, at, :] = both[:, hidden:]
        down_ref[0, :, at] = mm_tn(hd_all, join(d0, at))


class ExpertGrads:
    def __init__(self, xe, d0, dgu, hd, pieces=4):
        self.ins, self.outs = (*xe, *d0, *dgu, *hd), {}
        self.count, self.pieces = len(xe), pieces
        self.local, _, _, self.width = xe[0].shape
        self.hidden = hd[0].shape[3]

    def run(self, piece):
        local, width, hidden, count = self.local, self.width, self.hidden, self.count
        each = local // self.pieces
        first = each * piece

        def whole(n):
            return pl.BlockSpec((1, 2, PAD, n), lambda e: (e + first, 0, 0, 0))

        slots = count * 2 * PAD * each
        earlier = list(self.outs[0]) if self.outs else []
        body = functools.partial(expert_grads_body, count)
        n = len(self.ins)

        def with_earlier(*refs):
            body(*refs[:n], *refs[n + len(earlier) :])

        self.outs[0] = pl.pallas_call(
            with_earlier,
            grid=(each,),
            out_shape=[sds((local, width, hidden), F32), sds((local, width, hidden), F32), sds((local, hidden, width), F32)],
            in_specs=[whole(width)] * (2 * count) + [whole(2 * hidden)] * count + [whole(hidden)] * count
            + [pl.BlockSpec(memory_space=pl.ANY)] * len(earlier),
            out_specs=[pl.BlockSpec((1, width, hidden), lambda e: (e + first, 0, 0))] * 2
            + [pl.BlockSpec((1, hidden, width), lambda e: (e + first, 0, 0))],
            input_output_aliases={n + i: i for i in range(len(earlier))},
            compiler_params=pltpu.CompilerParams(vmem_limit_bytes=32 << 20),
            cost_estimate=pl.CostEstimate(
                flops=6 * slots * width * hidden, bytes_accessed=slots * width * 4 + 12 * each * width * hidden, transcendentals=0
            ),
            name="expert_grads",
        )(*self.ins, *earlier)


def add16(a, b):
    return (a.astype(F32) + b.astype(F32)).astype(BF16)


def on_device_gathered(
    tokens,
    document_numbers,
    picks,
    drop_order,
    w_query,
    key_matrix,
    value_matrix,
    w_out,
    w_router,
    gain_attn,
    gain_moe,
    expert_gate,
    expert_up,
    expert_down,
    cotangent,
):
    n_dp = lax.axis_size("dp")
    nz = n_dp // 2
    r, t = lax.axis_index("dp"), lax.axis_index("tensor")
    z, y, x, c = r // 2, r % 2, t // 2, t % 2
    idx = jnp.stack([r, z, y, x, c]).astype(jnp.int32)

    def shift_z(v):
        return lax.ppermute(v, "dp", [(i, ((i // 2 + 1) % nz) * 2 + i % 2) for i in range(n_dp)])

    def swap_y(v):
        return lax.ppermute(v, "dp", [(i, i ^ 1) for i in range(n_dp)])

    def swap_x(v):
        return lax.ppermute(v, "tensor", [(i, i ^ 2) for i in range(4)])

    def swap_c(v):
        return lax.ppermute(v, "tensor", [(i, i ^ 1) for i in range(4)])

    tok, width = tokens.shape
    rows = w_query.shape[0]
    qd, kd = w_query.shape[1], key_matrix.shape[1]
    used = qd + 2 * kd
    experts = w_router.shape[1]
    local, _, hidden = expert_gate.shape
    capacity = 9 * tok * picks.shape[1] // (8 * experts)
    cols = width // 4

    aux = jnp.concatenate(
        [w_router, gain_attn[:, None], gain_moe[:, None], jnp.zeros((rows, 128 - experts - 2), BF16)], axis=1
    )
    wz = [jnp.concatenate([w_query, key_matrix, value_matrix, aux, w_out.T], axis=1)]
    wy, wx = [], []

    def out_pair(k):
        return swap_x(jnp.stack([wz[k][:, used + 128 :], wy[k][:, used + 128 :]]))

    pos = kernel_call(
        functools.partial(slots_body, capacity),
        [sds((experts, tok), BF16)],
        [idx, picks.T, drop_order.reshape(tok, -1).T],
        name="slots",
    )[0]
    part = tok // 4
    def quarter(t):
        slots = jnp.pad(lax.dynamic_slice_in_dim(pos, t * part, part, 1), ((0, 0), (0, cols - part)))
        return jnp.concatenate([lax.dynamic_slice_in_dim(cotangent, t * cols, cols, 1), slots], axis=0)

    d_own, d_far = quarter(t), quarter(2 * (1 - x) + c)

    class Rows:
        def __init__(self, own):
            self.z, self.y, self.cz, self.cy = {0: own}, {}, {}, {}

        def ring(self, k):
            self.z[k] = shift_z(self.z[k - 1])

        def side(self, k):
            self.y[k] = swap_y(self.z[k])

        def core_ring(self, k):
            self.cz[k] = swap_c(self.z[k])

        def core_side(self, k):
            self.cy[k] = swap_c(self.y[k])

        def all(self, k):
            return [v[k] for v in (self.z, self.y, self.cz, self.cy)]

    class Split(Rows):
        def __init__(self, own, far):
            super().__init__(own)
            self.far, self.s, self.x, self.cs, self.cx = far, {}, {}, {}, {}

        def chip(self, k):
            self.s[k] = jnp.stack([self.z[k], self.y[k]])
            self.x[k] = swap_x(self.s[k] if k else self.y[0])

        def core_own(self, k):
            self.cs[k] = swap_c(self.s[k])

        def core(self, k):
            if k == 0:
                self.x[0] = jnp.stack([self.far, self.x[0]])
            self.cx[k] = swap_c(self.x[k])

        def all(self, k):
            return [v[k] for v in (self.s, self.x, self.cs, self.cx)]

    def meet(*items):
        places = [(getattr(o, n), k) for o, names, k in items for n in names.split()]
        values = sync(*[d[k] for d, k in places])
        for (d, k), v in zip(places, values):
            d[k] = v

    last = nz - 1
    for k in range(last):
        wz.append(shift_z(wz[k]))
        wy.append(swap_y(wz[k]))
        if k:
            wx.append(out_pair(k - 1))
        if k == 0:
            wz[1], wy[0], d_own, d_far = sync(wz[1], wy[0], d_own, d_far)
        else:
            wz[k + 1], wy[k] = sync(wz[k + 1], wy[k])
    wx.append(out_pair(last - 1))
    wy.append(swap_y(wz[last]))
    d = Split(after(d_own, wz[last]), d_far)
    d.ring(1)
    gu = jnp.concatenate(sync(expert_gate, expert_up, wz[last])[:2], axis=2)
    wy[last], wx[0], gu = sync(wy[last], wx[0], gu)
    wx.append(out_pair(last))

    positions = np.arange(tok, dtype=np.float32)
    inverse = rope_base ** (-(2.0 * np.arange(HEAD_SIZE // 2, dtype=np.float32)) / HEAD_SIZE)
    angles = positions[:, None] * inverse.astype(np.float32)[None, :]
    cos = jnp.asarray(np.tile(np.cos(angles), (1, 4)).astype(np.float32))
    sin = np.sin(angles)
    sin = jnp.asarray(np.tile(np.concatenate([-sin, sin], axis=1), (1, 2)).astype(np.float32))
    heads = qd // HEAD_SIZE
    seg_row = document_numbers.reshape(1, tok)
    o, q, k_rot, v, w_all, aux_t, *heads_p = kernel_call(
        functools.partial(attend_body, nz),
        [sds((tok, qd), BF16), sds((tok, qd), BF16), sds((tok, kd), BF16), sds((tok, kd), BF16),
         sds((width, used + 128), BF16), sds((128, width), BF16)] + [sds((tok, tok), BF16)] * heads,
        [idx, *wz, *wy, tokens, seg_row, seg_row.T, cos, sin],
        scratch=[pltpu.VMEM((tok, tok), F32), pltpu.VMEM((tok, used), F32)],
        flops=4e9,
        name="attend",
    )
    o, d.z[1], d.z[0], *wx[1:] = sync(o, d.z[1], d.z[0], *wx[1:])
    o_x, o_c0 = swap_x(o), swap_c(o)
    d.ring(2)
    d.side(0)
    wo = kernel_call(
        functools.partial(place_both_body, nz), [sds((2, width, qd), BF16)], [idx, *wz, *wy, *wx], name="place"
    )[0]
    wo_c = swap_c(wo)
    slot_ids = np.arange(local * PAD)
    sel = (r * local + slot_ids[:, None] // PAD == jnp.arange(experts)[None, :]).astype(BF16)
    slot_col = jnp.asarray((slot_ids % PAD).astype(np.float32)[:, None])
    slot_row = jnp.asarray((slot_ids % PAD).astype(np.float32)[None, :])
    o_x, o_c0, wo_c, sel, d.z[2], d.y[0] = sync(o_x, o_c0, wo_c, sel, d.z[2], d.y[0])
    d.ring(3)
    d.side(1)
    d.side(2)
    d.chip(0)
    d.core_own(0)
    o_c1 = swap_c(o_x)
    h, low, ring0 = kernel_call(
        out_body,
        [sds((tok, width), F32), sds((tok, width), BF16), sds((tok, 2 * cols), BF16)],
        [idx, tokens, o, o_x, o_c0, o_c1, wo, wo_c, aux_t],
        flops=5e9,
        name="out",
    )
    ring0, d.y[1], d.y[2], d.z[3], d.x[0], d.cs[0] = sync(ring0, d.y[1], d.y[2], d.z[3], d.x[0], d.cs[0])
    a = Rows(ring0)
    done = {}

    def run_experts(k):
        done[k] = experts_call(idx, a.all(k), d.all(k), gu, expert_down, aux_t, sel, slot_col, slot_row)

    class Sums:
        def __init__(self, at):
            self.at, self.c, self.s, self.y, self.total = at, {}, {}, {}, {}

        def core(self, k):
            self.c[k] = swap_c(done[k][self.at + 1])

        def side(self, k):
            m, n = done[k][self.at], self.c[k]
            self.s[k] = add16(m[0], n[0])
            self.y[k] = swap_y(add16(m[1], n[1]))

        def ring(self, k):
            total = self.s[k].astype(F32) + self.y[k].astype(F32)
            if self.total:
                total = total + self.total[0].astype(F32)
            total = total.astype(BF16)
            self.total[0] = total if k == 0 else shift_z(total)

    class SplitSums(Sums):
        def __init__(self, at):
            super().__init__(at)
            self.x = {}

        def chip(self, k):
            self.x[k] = swap_x(add16(done[k][self.at][:, :, cols:], self.c[k][:, :, cols:]))

        def side(self, k):
            m, n, far = done[k][self.at], self.c[k], self.x[k]
            own = [(m[q, :, :cols].astype(F32) + n[q, :, :cols].astype(F32) + far[q].astype(F32)).astype(BF16) for q in (0, 1)]
            self.s[k] = own[0]
            self.y[k] = swap_y(own[1])

    sx, sy = Sums(0), SplitSums(2)

    class Ran:
        out = done

    ran = Ran()
    a.ring(1)
    a.side(0)
    d.chip(1)
    d.core(0)
    meet((a, "z", 1), (a, "y", 0), (d, "x", 1), (d, "cx", 0))
    a.core_side(0)
    a.core_ring(0)
    d.core_own(1)
    meet((a, "cy cz", 0), (d, "cs x", 1))
    a.ring(2)
    a.side(1)
    d.side(3)
    d.chip(2)
    run_experts(0)
    meet((a, "z", 2), (a, "y", 1), (ran, "out", 0), (d, "y", 3), (d, "x", 2), (d, "x", 1))
    a.core_side(1)
    a.core_ring(1)
    d.core(1)
    meet((a, "cy cz", 1), (d, "cx", 1), (d, "x", 2), (ran, "out", 0))
    a.ring(3)
    a.side(2)
    d.chip(3)
    d.core_own(2)
    d.core(2)
    run_experts(1)
    meet((a, "z", 3), (a, "y", 2), (ran, "out", 1), (d, "x", 3), (d, "cx cs", 2))
    a.side(3)
    a.core_side(2)
    a.core_ring(2)
    sx.core(1)
    sy.core(0)
    meet((a, "cy cz", 2), (sx, "c", 1), (sy, "c", 0), (ran, "out", 1), (d, "x", 3))
    sx.side(1)
    sy.chip(0)
    d.core_own(3)
    d.core(3)
    run_experts(2)
    meet((a, "y", 3), (sx, "s y", 1), (sy, "x", 0), (ran, "out", 2), (d, "cs cx", 3))
    sx.ring(1)
    a.core_side(3)
    a.core_ring(3)
    sx.core(2)
    sy.core(1)
    meet((a, "cy cz", 3), (sx, "c", 2), (ran, "out", 2), (sy, "c", 1))
    sx.side(2)
    sy.chip(1)
    sy.side(0)
    run_experts(3)
    meet((sx, "s y", 2), (sx, "total", 0), (sy, "x", 1), (sy, "s y", 0), (ran, "out", 3))
    grads = ExpertGrads(*[[done[k][i] for k in range(nz)] for i in range(4, 8)])
    sx.ring(2)
    sx.core(3)
    sy.core(2)
    meet((sx, "c", 3), (ran, "out", 3), (sy, "c", 2))
    sx.side(3)
    sx.core(0)
    sy.chip(2)
    sy.core(3)
    grads.run(0)
    grads.run(1)
    meet((sx, "s y", 3), (sx, "total", 0), (sx, "c", 0), (sy, "x", 1), (sy, "x", 2), (sy, "c", 3), (grads, "outs", 0))
    sx.ring(3)
    sx.side(0)
    sy.chip(3)
    grads.run(2)
    meet((sx, "s y", 0), (sx, "total", 0), (sy, "x", 2), (sy, "x", 3), (grads, "outs", 0))
    sx.ring(0)
    far = swap_x(sx.total[0])
    sy.side(1)
    sy.side(2)
    grads.run(3)
    sx.total[0], far, *rest = sync(sx.total[0], far, sy.s[1], sy.y[1], sy.s[2], sy.y[2], sy.x[3], grads.outs[0])
    sy.s[1], sy.y[1], sy.s[2], sy.y[2], sy.x[3], grads.outs[0] = rest
    mine = sx.total[0].astype(F32) + jnp.concatenate([far[:, cols:], far[:, :cols]], axis=1).astype(F32)
    head, tail = mine[:tok], sx.total[0][tok:].astype(F32) + far[tok:].astype(F32)
    fm = jnp.concatenate([head.astype(BF16), tail.astype(BF16)], axis=0)
    fn = swap_c(fm)
    fm, fn, sy.y[1], sy.x[3] = sync(fm, fn, sy.y[1], sy.x[3])
    sy.side(3)
    sy.ring(1)
    groups = sent_groups(nz)

    def blocks_of(n, width, groups):
        return [sds((n, width), BF16)] * nz + [sds((len(g), n, width), BF16) for g in groups]

    d_h, d_o, *early = kernel_call(
        functools.partial(hidden_back_body, nz),
        [sds((tok, cols), F32), sds((tok, qd), BF16)] + blocks_of(rows, qd + 128, groups[0]),
        [idx, fm, fn, h, low, aux_t, pos, cotangent, o, wo],
        scratch=[pltpu.VMEM((tok, width), F32), pltpu.VMEM((experts, tok), F32), pltpu.VMEM((n_dp, rows, qd + 128), BF16)],
        flops=3e9,
        name="hidden_back",
    )
    d_o, early, sy.total[0], sy.s[3], sy.y[3] = sync(d_o, early, sy.total[0], sy.s[3], sy.y[3])

    class Weights:
        def __init__(self, v, groups):
            self.kept, self.sent, self.groups, self.y, self.total = v[:nz], v[nz:], groups, {}, {}

        def side(self, i):
            got = swap_y(self.sent[i])
            for at, k in enumerate(self.groups[i]):
                self.y[k] = got[at]

        def ring(self, k):
            total = self.kept[k].astype(F32) + self.y[k].astype(F32)
            if self.total:
                total = total + self.total[0].astype(F32)
            self.total[0] = shift_z(total.astype(BF16))

        def last(self):
            return self.kept[0], self.y[0], self.total[0]

    early = Weights(early, groups[0])
    early.side(0)
    sy.ring(2)
    dxm, dxn, *late = kernel_call(
        functools.partial(attend_back_body, nz),
        [sds((tok, 2 * cols + 128), BF16), sds((tok, 2 * cols + 128), BF16)] + blocks_of(rows + 16, used, groups[1]),
        [idx, d_o, v, k_rot, q, cos, sin, tokens, aux_t, w_all, *heads_p],
        scratch=[
            pltpu.VMEM((tok, used), F32), pltpu.VMEM((tok, used), BF16), pltpu.VMEM((4, tok, cols), BF16),
            pltpu.VMEM((n_dp, rows + 16, used), BF16),
        ],
        flops=5e9,
        name="attend_back",
    )
    late, dxm, dxn, early.y, early.sent, sy.total[0] = sync(late, dxm, dxn, early.y, early.sent, sy.total[0])
    late = Weights(late, groups[1])
    late.side(0)
    sy.ring(3)
    got = swap_c(dxn)
    late.y, late.sent, early.sent, early.y, got = sync(late.y, late.sent, early.sent, early.y, got)
    late.side(1)
    late.ring(1)
    early.ring(1)
    ours = dxm.astype(F32) + got.astype(F32)
    mean_part = ours[:, 2 * cols] + ours[:, 2 * cols + 1]
    high, lowp = split16(mean_part)
    send = jnp.concatenate(
        [ours[:, cols : 2 * cols].astype(BF16), high[:, None], lowp[:, None], jnp.zeros((tok, 126), BF16)], axis=1
    )
    got = swap_x(send)
    late.y, late.sent, late.total[0], early.total[0], got, sy.total[0] = sync(
        late.y, late.sent, late.total[0], early.total[0], got, sy.total[0]
    )
    late.side(2)
    late.ring(2)
    early.side(1)
    early.ring(2)
    y_sum = sy.s[0].astype(F32) + sy.y[0].astype(F32) + sy.total[0].astype(F32)
    mixed = (y_sum + lax.dynamic_slice_in_dim(h, t * cols, cols, 1)).astype(BF16)
    x_full = tokens.astype(F32)
    r1 = lax.rsqrt(jnp.mean(x_full * x_full, axis=-1, keepdims=True) + epsilon)
    d_norm = ours[:, :cols] + got[:, :cols].astype(F32)
    mean = (mean_part + got[:, cols].astype(F32) + got[:, cols + 1].astype(F32))[:, None] / width
    x_cols = lax.dynamic_slice_in_dim(tokens, t * cols, cols, 1).astype(F32) * r1
    gain_row = lax.dynamic_slice_in_dim(aux_t[64:65], t * cols, cols, 1).astype(F32)
    grad_tokens = d_h + r1 * (d_norm * gain_row - x_cols * mean)
    late.y, late.total[0], early.y, early.total[0], grad_tokens, mixed = sync(
        late.y, late.total[0], early.y, early.total[0], grad_tokens, mixed
    )
    late.ring(3)
    early.ring(3)
    late.total[0], early.total[0] = sync(late.total[0], early.total[0])
    grad_out, grad_router, gain_rows = kernel_call(
        early_end_body,
        [sds((qd, rows), F32), sds((rows, experts), F32), sds((8, rows), F32)],
        [idx, *early.last()],
        name="early_end",
    )
    grad_gain_moe = gain_rows[0]
    grad_query, grad_key, grad_value, gain_rows = kernel_call(
        late_end_body,
        [sds((rows, qd), F32), sds((rows, kd), F32), sds((rows, kd), F32), sds((8, rows), F32)],
        [idx, *late.last()],
        name="late_end",
    )
    gain_part = gain_rows[0] + gain_rows[1]
    gain_part = gain_part + swap_c(gain_part)
    grad_gain_attn = gain_part + swap_x(gain_part)
    grad_gate, grad_up, grad_down = grads.outs[0]
    return (
        mixed,
        grad_tokens,
        grad_query,
        grad_key,
        grad_value,
        grad_out,
        grad_router,
        grad_gain_attn,
        grad_gain_moe,
        grad_gate,
        grad_up,
        grad_down,
    )


def solution(mesh):
    few = mesh.shape["tensor"] == 4 and mesh.shape["dp"] in (4, 8)
    return jax.shard_map(
        on_device_gathered if few else on_device,
        mesh=mesh,
        in_specs=(
            P("dp", None),
            P("dp", None),
            P("dp", None),
            P("dp", None),
            P("dp", "tensor"),
            P("dp", "tensor"),
            P("dp", "tensor"),
            P("tensor", "dp"),
            P("dp", None),
            P("dp"),
            P("dp"),
            P("dp", None, "tensor"),
            P("dp", None, "tensor"),
            P("dp", "tensor", None),
            P("dp", None),
        ),
        out_specs=(
            P("dp", "tensor"),
            P("dp", "tensor"),
            P("dp", "tensor"),
            P("dp", "tensor"),
            P("dp", "tensor"),
            P("tensor", "dp"),
            P("dp", None),
            P("dp"),
            P("dp"),
            P("dp", None, "tensor"),
            P("dp", None, "tensor"),
            P("dp", "tensor", None),
        ),
        check_vma=False,
    )
```

```python
import functools

import jax
import jax.numpy as jnp
import numpy as np
from jax import lax
from jax.experimental import pallas as pl
from jax.experimental.pallas import tpu as pltpu
from jax.sharding import PartitionSpec as P

HEAD_SIZE = 64


epsilon = 1e-05
negative_big = -1e30
rope_base = 10000.0
F32 = jnp.float32
BF16 = jnp.bfloat16
BLK = 256
PAD = 80
VMEM_LIMIT = 62 * 1024 * 1024


def rotary_tables(positions, head_width):
    half_width = head_width // 2
    inverse = rope_base ** (-(2.0 * jnp.arange(half_width, dtype=jnp.float32)) / head_width)
    angles = positions.astype(jnp.float32)[:, None] * inverse[None, :]
    return (jnp.cos(angles)[:, None, :], jnp.sin(angles)[:, None, :])


def apply_pair_rotation(values, cosine_values, sine_values):
    half_width = values.shape[-1] // 2
    first_half = values[..., :half_width]
    second_half = values[..., half_width:]
    return jnp.concatenate(
        [
            first_half * cosine_values - second_half * sine_values,
            second_half * cosine_values + first_half * sine_values,
        ],
        axis=-1,
    )


def unrotate_pairs(values, cosine_values, sine_values):
    half_width = values.shape[-1] // 2
    first_half = values[..., :half_width]
    second_half = values[..., half_width:]
    return jnp.concatenate(
        [
            first_half * cosine_values + second_half * sine_values,
            second_half * cosine_values - first_half * sine_values,
        ],
        axis=-1,
    )


def slot_table(chosen_rows, order_row, expert_count, capacity):
    flat_experts = chosen_rows.reshape(-1)
    pair_count = flat_experts.shape[0]
    sort_keys = flat_experts * pair_count + order_row
    ordering = jnp.argsort(sort_keys)
    sorted_experts = flat_experts[ordering]
    expert_ids = jnp.arange(expert_count, dtype=jnp.int32)
    counts = jnp.sum(
        (flat_experts[:, None] == expert_ids[None, :]).astype(jnp.int32), axis=0, dtype=jnp.int32
    )
    starts = jnp.cumsum(counts, dtype=jnp.int32) - counts
    ranks_sorted = jnp.arange(pair_count, dtype=jnp.int32) - starts[sorted_experts]
    ranks = jnp.zeros((pair_count,), jnp.int32).at[ordering].set(ranks_sorted)
    destination = jnp.where(
        ranks < capacity, flat_experts * capacity + ranks, expert_count * capacity
    )
    table = jnp.full((expert_count * capacity + 1,), pair_count, jnp.int32)
    table = table.at[destination].set(jnp.arange(pair_count, dtype=jnp.int32))
    return (table[: expert_count * capacity], destination)


def on_device(
    tokens,
    document_numbers,
    picks,
    drop_order,
    w_query,
    key_matrix,
    value_matrix,
    w_out,
    w_router,
    gain_attn,
    gain_moe,
    expert_gate,
    expert_up,
    expert_down,
    cotangent,
):
    ranks_dp = lax.axis_size("dp")
    tensor_index = lax.axis_index("tensor")
    wq, wk, wv, wo, wr, g_attn, g_moe = (
        lax.all_gather(w_query, "dp", axis=0, tiled=True),
        lax.all_gather(key_matrix, "dp", axis=0, tiled=True),
        lax.all_gather(value_matrix, "dp", axis=0, tiled=True),
        lax.all_gather(w_out, "dp", axis=1, tiled=True),
        lax.all_gather(w_router, "dp", axis=0, tiled=True),
        lax.all_gather(gain_attn, "dp", axis=0, tiled=True),
        lax.all_gather(gain_moe, "dp", axis=0, tiled=True),
    )
    tok_count, width = tokens.shape
    col_width = width // lax.axis_size("tensor")
    col_start = tensor_index * col_width
    q_heads = wq.shape[1] // HEAD_SIZE
    kv_heads = wk.shape[1] // HEAD_SIZE
    group_repeats = q_heads // kv_heads
    score_scale = HEAD_SIZE ** (-0.5)
    seg_row = document_numbers.reshape(-1)
    positions = jnp.arange(tok_count, dtype=jnp.int32)
    cosine_values, sine_values = rotary_tables(positions, HEAD_SIZE)
    x_full = tokens.astype(jnp.float32)
    r_attn = lax.rsqrt(jnp.mean(x_full * x_full, axis=-1, keepdims=True) + epsilon)
    x_hat = x_full * r_attn
    gain_one = g_attn.astype(jnp.float32)
    x_low = (x_hat * gain_one).astype(jnp.bfloat16)
    q_proj = jnp.dot(x_low, wq, preferred_element_type=jnp.float32)
    key_projected = jnp.dot(x_low, wk, preferred_element_type=jnp.float32)
    value_projected = jnp.dot(x_low, wv, preferred_element_type=jnp.float32)
    query_rotated = apply_pair_rotation(
        q_proj.reshape(tok_count, q_heads, HEAD_SIZE), cosine_values, sine_values
    ).astype(jnp.bfloat16)
    query_rotated = query_rotated.reshape(tok_count, kv_heads, group_repeats, HEAD_SIZE)
    key_rotated = apply_pair_rotation(
        key_projected.reshape(tok_count, kv_heads, HEAD_SIZE), cosine_values, sine_values
    ).astype(jnp.bfloat16)
    value_reduced = value_projected.astype(jnp.bfloat16).reshape(tok_count, kv_heads, HEAD_SIZE)
    block_rows = min(512, tok_count)
    block_count = tok_count // block_rows
    q_blocks = query_rotated.reshape(block_count, block_rows, kv_heads, group_repeats, HEAD_SIZE)
    seg_blocks = seg_row.reshape(block_count, block_rows)
    pos_blocks = positions.reshape(block_count, block_rows)

    def masked_scores(q_block, seg_block, pos_block):
        raw_scores = (
            jnp.einsum("qgrd,kgd->grqk", q_block, key_rotated, preferred_element_type=jnp.float32)
            * score_scale
        )
        allowed = (seg_block[:, None] == seg_row[None, :]) & (
            positions[None, :] <= pos_block[:, None]
        )
        return jnp.where(allowed, raw_scores, negative_big)

    def forward_block(inputs):
        q_block, seg_block, pos_block = inputs
        scores = masked_scores(q_block, seg_block, pos_block)
        highest_score = jnp.max(scores, axis=-1, keepdims=True)
        weights = jnp.exp(scores - highest_score)
        totals = jnp.sum(weights, axis=-1, keepdims=True)
        probs = (weights / totals).astype(jnp.bfloat16)
        heads_block = jnp.einsum(
            "grqk,kgd->qgrd", probs, value_reduced, preferred_element_type=jnp.float32
        )
        return (heads_block.astype(jnp.bfloat16), highest_score + jnp.log(totals))

    head_outputs, log_totals = lax.map(forward_block, (q_blocks, seg_blocks, pos_blocks))
    o_low = head_outputs.reshape(tok_count, q_heads * HEAD_SIZE)
    attn_terms = jnp.dot(o_low, wo, preferred_element_type=jnp.float32)
    attn = lax.psum(attn_terms, "tensor")
    h_full = x_full + attn
    r_moe = lax.rsqrt(jnp.mean(h_full * h_full, axis=-1, keepdims=True) + epsilon)
    h_hat = h_full * r_moe
    gain_two = g_moe.astype(jnp.float32)
    a_low = (h_hat * gain_two).astype(jnp.bfloat16)
    logits = jnp.dot(a_low, wr, preferred_element_type=jnp.float32)
    chosen = jnp.take_along_axis(logits, picks, axis=1)
    gates = jax.nn.softmax(chosen, axis=-1)
    top_count = picks.shape[1]
    experts_all = wr.shape[1]
    capacity = 9 * tok_count * top_count // (8 * experts_all)
    table, destination = slot_table(picks, drop_order.reshape(-1), experts_all, capacity)
    slot_tokens = table // top_count
    local_count = expert_gate.shape[0]
    h_cols = lax.dynamic_slice_in_dim(h_full, col_start, col_width, 1)
    d_out = cotangent.astype(jnp.float32)
    d_out_cols = lax.dynamic_slice_in_dim(d_out, col_start, col_width, 1)
    send_rows = jnp.concatenate([a_low, jnp.zeros((1, width), jnp.bfloat16)], axis=0)[slot_tokens]
    expert_in = lax.all_to_all(
        send_rows.reshape(ranks_dp, -1, width), "dp", split_axis=0, concat_axis=0, tiled=True
    )
    expert_in = expert_in.reshape(ranks_dp, local_count, capacity, width)
    gate_val = jnp.einsum(
        "sjcd,jdf->sjcf", expert_in, expert_gate, preferred_element_type=jnp.float32
    )
    up_val = jnp.einsum("sjcd,jdf->sjcf", expert_in, expert_up, preferred_element_type=jnp.float32)
    sigmoid_gate = jax.nn.sigmoid(gate_val)
    silu_gate = gate_val * sigmoid_gate
    hidden_low = (silu_gate * up_val).astype(jnp.bfloat16)
    slab_count = 4
    slab_rows = ranks_dp // slab_count
    out_pieces = []
    for slab_index in range(slab_count):
        lower = slab_index * slab_rows
        partial_out = jnp.einsum(
            "sjcf,jfd->sjcd",
            hidden_low[lower : lower + slab_rows],
            expert_down,
            preferred_element_type=jnp.float32,
        )
        out_pieces.append(
            lax.psum_scatter(
                partial_out.astype(jnp.bfloat16), "tensor", scatter_dimension=3, tiled=True
            )
        )
    expert_out = jnp.concatenate(out_pieces, axis=0).reshape(
        ranks_dp, local_count * capacity, col_width
    )
    returned = lax.all_to_all(expert_out, "dp", split_axis=0, concat_axis=0, tiled=True).reshape(
        experts_all * capacity, col_width
    )
    returned = jnp.concatenate([returned, jnp.zeros((1, col_width), jnp.bfloat16)], axis=0)
    pair_outs = returned[destination].reshape(tok_count, top_count, col_width).astype(jnp.float32)
    mixed = (h_cols + jnp.sum(gates[:, :, None] * pair_outs, axis=1)).astype(jnp.bfloat16)
    d_gate_terms = jnp.sum(pair_outs * d_out_cols[:, None, :], axis=2)
    d_pairs = (
        (gates[:, :, None] * d_out_cols[:, None, :]).astype(jnp.bfloat16).reshape(-1, col_width)
    )
    d_pairs = jnp.concatenate([d_pairs, jnp.zeros((1, col_width), jnp.bfloat16)], axis=0)
    d_send = d_pairs[table].reshape(ranks_dp, local_count * capacity, col_width)
    d_arrived = lax.all_to_all(d_send, "dp", split_axis=0, concat_axis=0, tiled=True)
    d_arrived = d_arrived.reshape(ranks_dp, local_count, capacity, col_width)
    grad_expert_gate = jnp.zeros(expert_gate.shape, jnp.float32)
    grad_expert_up = jnp.zeros(expert_up.shape, jnp.float32)
    grad_expert_down = jnp.zeros(expert_down.shape, jnp.float32)
    back_pieces = []
    for slab_index in range(slab_count):
        lower = slab_index * slab_rows
        upper = lower + slab_rows
        d_expert_out = lax.all_gather(d_arrived[lower:upper], "tensor", axis=3, tiled=True)
        d_hidden = jnp.einsum(
            "sjcd,jfd->sjcf", d_expert_out, expert_down, preferred_element_type=jnp.float32
        )
        grad_expert_down = grad_expert_down + jnp.einsum(
            "sjcf,sjcd->jfd",
            hidden_low[lower:upper],
            d_expert_out,
            preferred_element_type=jnp.float32,
        )
        slab_gate = gate_val[lower:upper]
        slab_sigmoid = sigmoid_gate[lower:upper]
        d_gate_low = (
            d_hidden * up_val[lower:upper] * slab_sigmoid * (1.0 + slab_gate * (1.0 - slab_sigmoid))
        ).astype(jnp.bfloat16)
        d_up_low = (d_hidden * silu_gate[lower:upper]).astype(jnp.bfloat16)
        slab_inputs = expert_in[lower:upper]
        grad_expert_gate = grad_expert_gate + jnp.einsum(
            "sjcd,sjcf->jdf", slab_inputs, d_gate_low, preferred_element_type=jnp.float32
        )
        grad_expert_up = grad_expert_up + jnp.einsum(
            "sjcd,sjcf->jdf", slab_inputs, d_up_low, preferred_element_type=jnp.float32
        )
        d_in_terms = jnp.einsum(
            "sjcf,jdf->sjcd", d_gate_low, expert_gate, preferred_element_type=jnp.float32
        ) + jnp.einsum("sjcf,jdf->sjcd", d_up_low, expert_up, preferred_element_type=jnp.float32)
        back_pieces.append(
            lax.psum_scatter(
                d_in_terms.astype(jnp.bfloat16), "tensor", scatter_dimension=3, tiled=True
            )
        )
    d_expert_in = jnp.concatenate(back_pieces, axis=0).reshape(
        ranks_dp, local_count * capacity, col_width
    )
    d_returned = lax.all_to_all(d_expert_in, "dp", split_axis=0, concat_axis=0, tiled=True).reshape(
        experts_all * capacity, col_width
    )
    d_returned = jnp.concatenate([d_returned, jnp.zeros((1, col_width), jnp.bfloat16)], axis=0)
    d_token_cols = jnp.sum(
        d_returned[destination].reshape(tok_count, top_count, col_width).astype(jnp.float32), axis=1
    )
    d_experts_full, d_gate_parts = (
        lax.all_gather(d_token_cols.astype(jnp.bfloat16), "tensor", axis=1, tiled=True).astype(
            d_token_cols.dtype
        ),
        lax.all_gather(d_gate_terms.astype(jnp.bfloat16), "tensor", axis=1, tiled=True).astype(
            d_gate_terms.dtype
        ),
    )
    d_gates = jnp.sum(d_gate_parts.reshape(tok_count, -1, top_count), axis=1)
    d_chosen = gates * (d_gates - jnp.sum(gates * d_gates, axis=-1, keepdims=True))
    one_hot = (picks[:, :, None] == jnp.arange(experts_all, dtype=jnp.int32)[None, None, :]).astype(
        jnp.float32
    )
    d_logits = jnp.sum(d_chosen[:, :, None] * one_hot, axis=1).astype(jnp.bfloat16)
    grad_router = jnp.dot(a_low.T, d_logits, preferred_element_type=jnp.float32)
    d_norm_moe = d_experts_full + jnp.dot(d_logits, wr.T, preferred_element_type=jnp.float32)
    grad_gain_moe = jnp.sum(d_norm_moe * h_hat, axis=0)
    d_scaled = d_norm_moe * gain_two
    d_h = d_out + r_moe * (d_scaled - h_hat * jnp.mean(d_scaled * h_hat, axis=-1, keepdims=True))
    d_h_low = d_h.astype(jnp.bfloat16)
    grad_out = jnp.dot(o_low.T, d_h_low, preferred_element_type=jnp.float32)
    d_heads = jnp.dot(d_h_low, wo.T, preferred_element_type=jnp.float32).astype(jnp.bfloat16)
    d_blocks = d_heads.reshape(block_count, block_rows, kv_heads, group_repeats, HEAD_SIZE)

    def backward_block(inputs):
        q_block, d_block, log_block, seg_block, pos_block = inputs
        scores = masked_scores(q_block, seg_block, pos_block)
        probs = jnp.exp(scores - log_block)
        d_probs = jnp.einsum(
            "qgrd,kgd->grqk", d_block, value_reduced, preferred_element_type=jnp.float32
        )
        centre = jnp.sum(probs * d_probs, axis=-1, keepdims=True)
        d_scores = (probs * (d_probs - centre)).astype(jnp.bfloat16)
        d_query = (
            jnp.einsum("grqk,kgd->qgrd", d_scores, key_rotated, preferred_element_type=jnp.float32)
            * score_scale
        )
        d_key = (
            jnp.einsum("grqk,qgrd->kgd", d_scores, q_block, preferred_element_type=jnp.float32)
            * score_scale
        )
        d_value = jnp.einsum(
            "grqk,qgrd->kgd",
            probs.astype(jnp.bfloat16),
            d_block,
            preferred_element_type=jnp.float32,
        )
        return (d_query, d_key, d_value)

    d_query_all, d_key_parts, d_value_parts = lax.map(
        backward_block, (q_blocks, d_blocks, log_totals, seg_blocks, pos_blocks)
    )
    d_query_low = unrotate_pairs(
        d_query_all.reshape(tok_count, q_heads, HEAD_SIZE), cosine_values, sine_values
    )
    d_query_low = d_query_low.astype(jnp.bfloat16).reshape(tok_count, q_heads * HEAD_SIZE)
    d_key_low = unrotate_pairs(jnp.sum(d_key_parts, axis=0), cosine_values, sine_values)
    d_key_low = d_key_low.astype(jnp.bfloat16).reshape(tok_count, kv_heads * HEAD_SIZE)
    d_value_low = (
        jnp.sum(d_value_parts, axis=0).astype(jnp.bfloat16).reshape(tok_count, kv_heads * HEAD_SIZE)
    )
    grad_query = jnp.dot(x_low.T, d_query_low, preferred_element_type=jnp.float32)
    grad_key = jnp.dot(x_low.T, d_key_low, preferred_element_type=jnp.float32)
    grad_value = jnp.dot(x_low.T, d_value_low, preferred_element_type=jnp.float32)
    d_norm_terms = (
        jnp.dot(d_query_low, wq.T, preferred_element_type=jnp.float32)
        + jnp.dot(d_key_low, wk.T, preferred_element_type=jnp.float32)
        + jnp.dot(d_value_low, wv.T, preferred_element_type=jnp.float32)
    )
    d_norm_attn = lax.psum(d_norm_terms.astype(jnp.bfloat16), "tensor").astype(jnp.float32)
    grad_gain_attn = jnp.sum(d_norm_attn * x_hat, axis=0)
    d_scaled_in = d_norm_attn * gain_one
    d_input = d_h + r_attn * (
        d_scaled_in - x_hat * jnp.mean(d_scaled_in * x_hat, axis=-1, keepdims=True)
    )
    grad_tokens = lax.dynamic_slice_in_dim(d_input, col_start, col_width, 1)
    grad_query, grad_key, grad_value, grad_out, grad_router, grad_gain_attn, grad_gain_moe = (
        lax.psum_scatter(grad_query, "dp", scatter_dimension=0, tiled=True),
        lax.psum_scatter(grad_key, "dp", scatter_dimension=0, tiled=True),
        lax.psum_scatter(grad_value, "dp", scatter_dimension=0, tiled=True),
        lax.psum_scatter(grad_out, "dp", scatter_dimension=1, tiled=True),
        lax.psum_scatter(grad_router, "dp", scatter_dimension=0, tiled=True),
        lax.psum_scatter(grad_gain_attn, "dp", scatter_dimension=0, tiled=True),
        lax.psum_scatter(grad_gain_moe, "dp", scatter_dimension=0, tiled=True),
    )
    return (
        mixed,
        grad_tokens,
        grad_query,
        grad_key,
        grad_value,
        grad_out,
        grad_router,
        grad_gain_attn,
        grad_gain_moe,
        grad_expert_gate,
        grad_expert_up,
        grad_expert_down,
    )


def mm(a, b):
    return jnp.dot(a, b, preferred_element_type=F32)


def mm_nt(a, b):
    return lax.dot_general(a, b, (((1,), (1,)), ((), ())), preferred_element_type=F32)


def mm_tn(a, b):
    return lax.dot_general(a, b, (((0,), (0,)), ((), ())), preferred_element_type=F32)


def bytes_of(arrays):
    return sum(int(np.prod(a.shape)) * jnp.dtype(a.dtype).itemsize for a in arrays)


def after(v, *done):
    return lax.optimization_barrier((v, *done))[0]


def sync(*values):
    return lax.optimization_barrier(values)


def kernel_call(body, outs, ins, scratch=(), flops=0, name=None):
    smem = pl.BlockSpec(memory_space=pltpu.SMEM)
    vmem = pl.BlockSpec(memory_space=pltpu.VMEM)
    nbytes = bytes_of(list(ins[1:]) + list(outs))
    need = nbytes + bytes_of(scratch) + (24 << 20)
    return pl.pallas_call(
        body,
        out_shape=[sds(o.shape, o.dtype) for o in outs],
        in_specs=[smem] + [vmem] * (len(ins) - 1),
        out_specs=[vmem] * len(outs),
        scratch_shapes=list(scratch),
        compiler_params=pltpu.CompilerParams(vmem_limit_bytes=min(need, VMEM_LIMIT)),
        cost_estimate=pl.CostEstimate(flops=int(flops), bytes_accessed=nbytes, transcendentals=0),
        name=name,
    )(*ins)


def sds(shape, dtype):
    return jax.ShapeDtypeStruct(shape, dtype)


def slots_body(capacity, idx, picks_ref, order_ref, pos_ref):
    experts, tok = pos_ref.shape
    ids = lax.broadcasted_iota(jnp.int32, (experts, tok), 0)
    never = 1 << 28
    order = jnp.full((experts, tok), never, jnp.int32)
    for k in range(picks_ref.shape[0]):
        order = jnp.where(picks_ref[k : k + 1, :] == ids, order_ref[k : k + 1, :], order)
    limit = jnp.zeros((experts, 1), jnp.int32)
    step = 1
    while step < picks_ref.shape[0] * tok:
        step *= 2
    while step:
        tried = limit + step
        count = jnp.sum((order < tried).astype(F32), axis=1, keepdims=True)
        limit = jnp.where(count <= capacity, tried, limit)
        step //= 2
    kept = order < limit
    rows = lax.broadcasted_iota(jnp.int32, (tok, tok), 0)
    cols = lax.broadcasted_iota(jnp.int32, (tok, tok), 1)
    before = (rows < cols).astype(F32).astype(BF16)
    place = mm(kept.astype(F32).astype(BF16), before)
    pos_ref[...] = jnp.where(kept, place, jnp.where(order < never, -1.0, -2.0)).astype(BF16)


def place_body(nz, idx, *refs):
    out = refs[-1]
    rows, cols = refs[0].shape[0], out.shape[1]
    for k in range(nz):
        base = lax.rem(idx[1] - k + nz, nz) * 2
        for q in range(2):
            block = base + (idx[2] if q == 0 else 1 - idx[2])
            out[pl.ds(pl.multiple_of(block * rows, rows), rows), :] = refs[q * nz + k][:, :cols]


def place_both_body(nz, idx, *refs):
    out = refs[-1]
    rows = refs[0].shape[0]
    for k in range(nz):
        base = lax.rem(idx[1] - k + nz, nz) * 2
        for q in range(2):
            block = base + (idx[2] if q == 0 else 1 - idx[2])
            at = pl.ds(pl.multiple_of(block * rows, rows), rows)
            out[0, at, :] = refs[q * nz + k][:, refs[0].shape[1] - out.shape[2] :]
            out[1, at, :] = refs[2 * nz + k][q]


def rotate(v, cos, sin, lane_low):
    swapped = jnp.where(lane_low, pltpu.roll(v, 96, 1), pltpu.roll(v, 32, 1))
    return v * cos + swapped * sin


def low_lanes(tok):
    return lax.rem(lax.broadcasted_iota(jnp.int32, (tok, 128), 1), 64) < 32


def attend_body(nz, idx, *refs):
    blocks = refs[: 2 * nz]
    x_ref, seg_row, seg_col, cos_ref, sin_ref = refs[2 * nz : 2 * nz + 5]
    refs = refs[2 * nz + 5 :]
    (o_ref, q_ref, k_ref, v_ref, w_ref, aux_ref), heads_p, (bias_ref, qkv_ref) = refs[:6], refs[6:-2], refs[-2:]
    place_body(nz, idx, *blocks, w_ref)
    tok, width = x_ref.shape
    qd, kd = q_ref.shape[1], k_ref.shape[1]
    used = qd + 2 * kd
    aux = w_ref[:, used:].astype(F32).T
    aux_ref[...] = aux.astype(BF16)
    x = x_ref[...].astype(F32)
    r1 = lax.rsqrt(jnp.mean(x * x, axis=1, keepdims=True) + epsilon)
    x_low = (x * r1 * aux[64:65, :]).astype(BF16)
    qkv_ref[...] = mm(x_low, w_ref[:, :used])
    lanes = low_lanes(tok)
    cos, sin = cos_ref[...], sin_ref[...]
    for b in range(qd // 128):
        rot = rotate(qkv_ref[:, b * 128 : b * 128 + 128], cos, sin, lanes).astype(BF16)
        q_ref[:, b * 128 : b * 128 + 128] = (rot.astype(F32) * HEAD_SIZE**-0.5).astype(BF16)
    for b in range(kd // 128):
        rot = rotate(qkv_ref[:, qd + b * 128 : qd + b * 128 + 128], cos, sin, lanes)
        k_ref[:, b * 128 : b * 128 + 128] = rot.astype(BF16)
    v_ref[...] = qkv_ref[:, qd + kd :].astype(BF16)
    rows = lax.broadcasted_iota(jnp.int32, (tok, tok), 0)
    cols = lax.broadcasted_iota(jnp.int32, (tok, tok), 1)
    allowed = (seg_col[...] == seg_row[...]) & (cols <= rows)
    bias_ref[...] = jnp.where(allowed, 0.0, negative_big)
    heads, groups = qd // HEAD_SIZE, kd // HEAD_SIZE
    for h in range(heads):
        g = h // (heads // groups)
        a, b = h * HEAD_SIZE, g * HEAD_SIZE
        s = mm_nt(q_ref[:, a : a + HEAD_SIZE], k_ref[:, b : b + HEAD_SIZE]) + bias_ref[...]
        e = jnp.exp(s - jnp.max(s, axis=1, keepdims=True))
        p = (e / jnp.sum(e, axis=1, keepdims=True)).astype(BF16)
        heads_p[h][...] = p
        o_ref[:, a : a + HEAD_SIZE] = mm(p, v_ref[:, b : b + HEAD_SIZE]).astype(BF16)


def column_places(idx, width):
    x, c = idx[3], idx[4]
    part = width // 4

    def at(b):
        return pl.ds(pl.multiple_of(b * part, 128), part)

    return [at(2 * x + c), at(2 * (1 - x) + c)], [at(2 * x + 1 - c), at(2 * (1 - x) + 1 - c)]


def out_body(idx, x_ref, o0, o1, o2, o3, w01, w23, aux_ref, h_ref, low_ref, ring_ref):
    tok, width = x_ref.shape
    attn = mm_nt(o0[...], w01[0]) + mm_nt(o1[...], w01[1])
    attn = attn + (mm_nt(o2[...], w23[0]) + mm_nt(o3[...], w23[1]))
    h = x_ref[...].astype(F32) + attn
    h_ref[...] = h
    r2 = lax.rsqrt(jnp.mean(h * h, axis=1, keepdims=True) + epsilon)
    low_ref[...] = (h * r2 * aux_ref[64:66, :].astype(F32)[1:2, :]).astype(BF16)
    part = width // 4
    for m, at in enumerate(column_places(idx, width)[0]):
        ring_ref[:, m * part : m * part + part] = low_ref[:, at]


def masked_gates(logits, pos):
    picked = pos > -1.5
    shown = jnp.where(picked, logits, negative_big)
    e = jnp.where(picked, jnp.exp(shown - jnp.max(shown, axis=0, keepdims=True)), 0.0)
    return e / jnp.sum(e, axis=0, keepdims=True)


def split16(v):
    high = v.astype(BF16)
    return high, (v - high.astype(F32)).astype(BF16)


def experts_body(
    local, idx, aux_ref, sel_ref, selt_ref, slot_ref, slott_ref, *refs
):
    rows_hbm, d_hbm, (gu_hbm, down_hbm), refs = refs[:4], refs[4:8], refs[8:10], refs[10:]
    dx_hbm, y_hbm, (xe_hbm, d0_hbm, dgu_hbm, hd_hbm) = refs[:2], refs[2:4], refs[4:8]
    am_s, an_s, dm_s, dn_s, gu_s, down_s = refs[8:14]
    dx_out, y_out, (xe_s, d0_s, dgu_s, hd_s) = refs[14:16], refs[16:18], refs[18:22]
    pos_s, gate_s, y_s, dx_s, dgr_s, oh_s, oht_s, in_sem, w_sem, out_sem = refs[22:]
    tok, width = am_s.shape[1], xe_s.shape[3]
    half = pos_s.shape[0] // 2
    x, c = idx[3], idx[4]
    part = width // 4
    sides = column_places(idx, width)
    hidden = down_s.shape[1]
    both, slots = 2 * PAD, local * PAD

    def arriving(q):
        pairs = [(rows_hbm[q], am_s.at[q]), (rows_hbm[2 + q], an_s.at[q])]
        for i, d_s in enumerate((dm_s, dn_s)):
            for m in range(2):
                pairs.append((d_hbm[2 * i + m].at[q], d_s.at[q, :, m * part : m * part + part]))
        return [pltpu.make_async_copy(h, v, in_sem.at[q, i]) for i, (h, v) in enumerate(pairs)]

    weights = [pltpu.make_async_copy(gu_hbm, gu_s, w_sem.at[0]), pltpu.make_async_copy(down_hbm, down_s, w_sem.at[1])]
    for cp in arriving(0):
        cp.start()
    for cp in arriving(1):
        cp.start()
    for cp in weights:
        cp.start()
    leaving = []

    def leave(src, dst):
        cp = pltpu.make_async_copy(src, dst, out_sem.at[len(leaving)])
        cp.start()
        leaving.append(cp)

    sel, selt = sel_ref[...], selt_ref[...]
    for q in range(2):
        for cp in arriving(q):
            cp.wait()
        for d_s, core in ((dm_s, c), (dn_s, 1 - c)):
            for m, chip in enumerate((x, 1 - x)):
                at = pl.ds(pl.multiple_of((2 * chip + core) * 128, 128), 128)
                pos_s[:, at] = d_s[q, tok:, m * part : m * part + 128]
        pos = pos_s[...]
        logits = jnp.zeros(pos.shape, F32)
        for rows, places in zip((am_s, an_s), sides):
            for m, at in enumerate(places):
                logits = logits + mm_nt(aux_ref[: pos.shape[0], at], rows[q, :, m * part : m * part + part])
        gates = masked_gates(logits, pos.astype(F32))
        hot = (mm(sel, pos) == slot_ref[...]).astype(F32).astype(BF16)
        oh_s[q] = hot
        oht_s[q] = (mm_tn(pos, selt) == slott_ref[...]).astype(F32).astype(BF16)
        high, low = split16(gates)
        spread = (mm_nt(hot, high) + mm_nt(hot, low)) * sel.astype(F32)
        gate_s[:, q] = jnp.sum(spread, axis=1, keepdims=True).reshape(local, PAD, 1)
        for rows, outs in (((am_s, an_s), xe_s), ((dm_s, dn_s), d0_s)):
            for side, places in enumerate(sides):
                got = mm(hot, rows[side][q, :tok, :]).astype(BF16)
                for m, at in enumerate(places):
                    outs[:, q, :, at] = got[:, m * part : m * part + part].reshape(local, PAD, part)
    leave(xe_s, xe_hbm)
    leave(d0_s, d0_hbm)
    for cp in weights:
        cp.wait()
    for j in range(local):
        gu = mm(xe_s[j].reshape(both, width), gu_s[j])
        t = mm_nt(d0_s[j].reshape(both, width), down_s[j])
        gate = gate_s[j].reshape(both, 1)
        g, u = gu[:, :hidden], gu[:, hidden:]
        sg = jax.nn.sigmoid(g)
        silu = g * sg
        hd = (silu * u).astype(BF16)
        dhd = gate * t
        dg = (dhd * u * sg * (1.0 + g * (1.0 - sg))).astype(BF16)
        du = (dhd * silu).astype(BF16)
        dgate = jnp.sum(hd.astype(F32) * t, axis=1, keepdims=True)
        dgr_s[j] = jnp.broadcast_to(dgate, (both, dgr_s.shape[3])).reshape(2, PAD, dgr_s.shape[3])
        hd_s[j] = (hd.astype(F32) * gate).astype(BF16).reshape(2, PAD, hidden)
        dgu = jnp.concatenate([dg, du], axis=1)
        dgu_s[j] = dgu.reshape(2, PAD, 2 * hidden)
        dx_s[j] = mm_nt(dgu, gu_s[j]).astype(BF16).reshape(2, PAD, width)
        y = mm(hd, down_s[j])
        y_s[j] = (y.astype(BF16).astype(F32) * gate).astype(BF16).reshape(2, PAD, width)
    leave(hd_s, hd_hbm)
    leave(dgu_s, dgu_hbm)
    for q in range(2):
        hot, hott = oh_s[q], oht_s[q]

        def scatter(rows_s, outs):
            for out, places in zip(outs, sides):
                rows = [rows_s[:, q, :, at].reshape(slots, part) for at in places]
                out[q, :tok, :] = mm(hott, jnp.concatenate(rows, axis=1)).astype(BF16)

        scatter(dx_s, dx_out)
        spread = (dgr_s[:, q].reshape(slots, -1) * sel.astype(F32)).astype(BF16)
        pos_s[...] = mm_tn(spread, hot).astype(BF16)
        for out, at in zip(dx_out, (c, 1 - c)):
            out[q, tok:, :tok] = pos_s[pl.ds(pl.multiple_of(at * half, half), half), :]
            out[q, tok:, tok:] = jnp.zeros((half, out.shape[2] - tok), BF16)
        for v, h in zip(dx_out, dx_hbm):
            leave(v.at[q], h.at[q])
        scatter(y_s, y_out)
        for v, h in zip(y_out, y_hbm):
            leave(v.at[q], h.at[q])
    for cp in leaving:
        cp.wait()


def experts_call(idx, a, d, gu, down, aux_t, sel, slot_col, slot_row):
    local, width, hidden2 = gu.shape
    hidden = hidden2 // 2
    experts = sel.shape[1]
    tok = a[0].shape[0]
    rows = tok + experts // 2
    slots = local * PAD
    big = (local, 2, PAD, width)
    outs = [sds((2, n, width // 2), BF16) for n in (rows, rows, tok, tok)]
    outs += [sds(big, BF16), sds(big, BF16), sds((local, 2, PAD, hidden2), BF16), sds((local, 2, PAD, hidden), BF16)]
    kept = [idx, aux_t, sel, sel.T, slot_col, slot_row]
    scratch = [pltpu.VMEM((2, n, width // 2), BF16) for n in (tok, tok, tok + experts, tok + experts)]
    scratch += [pltpu.VMEM(v.shape, v.dtype) for v in [gu, down] + outs]
    scratch += [
        pltpu.VMEM((experts, tok), BF16), pltpu.VMEM((local, 2, PAD, 1), F32), pltpu.VMEM(big, BF16), pltpu.VMEM(big, BF16),
        pltpu.VMEM((local, 2, PAD, experts), F32), pltpu.VMEM((2, slots, tok), BF16), pltpu.VMEM((2, tok, slots), BF16),
    ]
    scratch += [pltpu.SemaphoreType.DMA((2, 6)), pltpu.SemaphoreType.DMA((2,)), pltpu.SemaphoreType.DMA((20,))]
    moved = [*a, *d, gu, down]
    smem = pl.BlockSpec(memory_space=pltpu.SMEM)
    vmem = pl.BlockSpec(memory_space=pltpu.VMEM)
    hbm = pl.BlockSpec(memory_space=pl.ANY)
    return pl.pallas_call(
        functools.partial(experts_body, local),
        out_shape=outs,
        in_specs=[smem] + [vmem] * 5 + [hbm] * len(moved),
        out_specs=[hbm] * len(outs),
        scratch_shapes=scratch,
        compiler_params=pltpu.CompilerParams(vmem_limit_bytes=VMEM_LIMIT),
        cost_estimate=pl.CostEstimate(
            flops=16 * slots * tok * width + 36 * slots * width * hidden,
            bytes_accessed=bytes_of(moved + outs),
            transcendentals=0,
        ),
        name="experts",
    )(*kept, *moved)


def in_ring_order(nz, idx, blocks_s, groups, outs):
    bases = [lax.rem(idx[1] - k + nz, nz) * 2 for k in range(nz)]
    for k in range(nz):
        outs[k][...] = blocks_s[bases[k] + idx[2]]
    for out, group in zip(outs[nz:], groups):
        for i, k in enumerate(group):
            out[i] = blocks_s[bases[k] + 1 - idx[2]]


def sent_groups(nz):
    early = [list(range(1, nz)), [0]]
    late = [[1], list(range(2, nz)), [0]]
    return [g for g in early if g], [g for g in late if g]


def hidden_back_body(nz, idx, fm_ref, fn_ref, h_ref, low_ref, aux_ref, pos_ref, dout_ref, o_ref, w_ref,
                     dh_ref, do_ref, *refs):
    outs, (full_s, dg_s, rs_s) = refs[:-3], refs[-3:]
    tok, width = h_ref.shape
    c, experts = idx[4], pos_ref.shape[0]
    half = experts // 2
    part = width // 4
    for ref, places in zip((fm_ref, fn_ref), column_places(idx, width)):
        for m, at in enumerate(places):
            full_s[:, at] = ref[:tok, m * part : m * part + part].astype(F32)
    for ref, at in ((fm_ref, c), (fn_ref, 1 - c)):
        dg_s[pl.ds(pl.multiple_of(at * half, half), half), :] = ref[tok:, :tok].astype(F32)
    low = low_ref[...]
    router = aux_ref[:experts, :]
    gates = masked_gates(mm_nt(router, low), pos_ref[...].astype(F32))
    dgates = dg_s[...]
    dlogits = (gates * (dgates - jnp.sum(gates * dgates, axis=0, keepdims=True))).astype(BF16)
    h = h_ref[...]
    r2 = lax.rsqrt(jnp.mean(h * h, axis=1, keepdims=True) + epsilon)
    ah = h * r2
    da = full_s[...] + mm_tn(dlogits, router)
    gain_grad = jnp.sum(da * ah, axis=0, keepdims=True)
    scaled = da * aux_ref[64:66, :].astype(F32)[1:2, :]
    dh = dout_ref[...].astype(F32) + r2 * (scaled - ah * jnp.mean(scaled * ah, axis=1, keepdims=True))
    full_s[...] = dh
    cols = dh_ref.shape[1]
    t = idx[3] * 2 + c
    dh_ref[...] = full_s[:, pl.ds(pl.multiple_of(t * cols, 128), cols)]
    dhb = dh.astype(BF16)
    do_ref[...] = mm(dhb, w_ref[0]).astype(BF16)
    turned = mm_tn(dhb, o_ref[...]).astype(BF16)
    side = jnp.concatenate([mm(dlogits, low), gain_grad, jnp.zeros((63, width), F32)], axis=0)
    side = side.T.astype(BF16)
    rows = rs_s.shape[1]
    for i in range(2 * nz):
        rs_s[i, :, :cols] = turned[i * rows : i * rows + rows]
        rs_s[i, :, cols:] = side[i * rows : i * rows + rows]
    in_ring_order(nz, idx, rs_s, sent_groups(nz)[0], outs)


def attend_back_body(nz, idx, do_ref, v_ref, k_ref, q_ref, cos_ref, sin_ref, x_ref, aux_ref, w_ref, *refs):
    heads_p, refs = refs[: q_ref.shape[1] // HEAD_SIZE], refs[q_ref.shape[1] // HEAD_SIZE :]
    dm_ref, dn_ref, outs, (dq_s, dqkv_s, dxn_s, rs_ref) = refs[0], refs[1], refs[2:-4], refs[-4:]
    tok, width = x_ref.shape
    qd, kd = q_ref.shape[1], k_ref.shape[1]
    heads, groups = qd // HEAD_SIZE, kd // HEAD_SIZE
    scale = HEAD_SIZE**-0.5
    each = heads // groups
    for g in range(groups):
        b = g * HEAD_SIZE
        kg, vg = k_ref[:, b : b + HEAD_SIZE], v_ref[:, b : b + HEAD_SIZE]
        dk = jnp.zeros((tok, HEAD_SIZE), F32)
        dv = jnp.zeros((tok, HEAD_SIZE), F32)
        for h in range(g * each, (g + 1) * each):
            a = h * HEAD_SIZE
            doh = do_ref[:, a : a + HEAD_SIZE]
            p = heads_p[h][...].astype(F32)
            dp = mm_nt(doh, vg)
            ds = (p * (dp - jnp.sum(p * dp, axis=1, keepdims=True))).astype(BF16)
            dq_s[:, a : a + HEAD_SIZE] = mm(ds, kg) * scale
            dk = dk + mm_tn(ds, q_ref[:, a : a + HEAD_SIZE])
            dv = dv + mm_tn(heads_p[h][...], doh)
        dq_s[:, qd + b : qd + b + HEAD_SIZE] = dk
        dqkv_s[:, qd + kd + b : qd + kd + b + HEAD_SIZE] = dv.astype(BF16)
    lanes = low_lanes(tok)
    cos, sin = cos_ref[...], -sin_ref[...]
    for b in range((qd + kd) // 128):
        at = slice(b * 128, b * 128 + 128)
        dqkv_s[:, at] = rotate(dq_s[:, at], cos, sin, lanes).astype(BF16)
    used = qd + 2 * kd
    x = x_ref[...].astype(F32)
    r1 = lax.rsqrt(jnp.mean(x * x, axis=1, keepdims=True) + epsilon)
    xh = x * r1
    gain = aux_ref[64:65, :].astype(F32)
    x_low = (xh * gain).astype(BF16)
    dqkv = dqkv_s[...]
    rows = width // rs_ref.shape[0]
    grads = mm_tn(x_low, dqkv).astype(BF16)
    dxn = mm_nt(dqkv, w_ref[:, :used])
    gain_high, gain_low = split16(jnp.sum(dxn * xh, axis=0, keepdims=True))
    pads = jnp.zeros((14, rows), BF16)
    for i in range(rs_ref.shape[0]):
        rs_ref[i, :rows, :] = grads[i * rows : i * rows + rows, :]
        at = slice(i * rows, i * rows + rows)
        tail = jnp.concatenate([gain_high[:, at].astype(F32), gain_low[:, at].astype(F32), pads.astype(F32)], axis=0)
        rs_ref[i, rows:, :] = jnp.zeros((16, used), BF16)
        rs_ref[i, rows:, :rows] = tail.astype(BF16)
    in_ring_order(nz, idx, rs_ref, sent_groups(nz)[1], outs)
    total = jnp.sum(dxn * xh * gain, axis=1, keepdims=True)
    high, low = split16(total)
    lane = lax.broadcasted_iota(jnp.int32, (tok, 128), 1)
    side = jnp.where(lane == 0, high.astype(F32), jnp.where(lane == 1, low.astype(F32), 0.0)).astype(BF16)
    cols = width // 4
    for i in range(4):
        dxn_s[i] = dxn[:, i * cols : i * cols + cols].astype(BF16)
    ix, c = idx[3], idx[4]
    for ref, core in ((dm_ref, c), (dn_ref, 1 - c)):
        ref[:, :cols] = dxn_s[2 * ix + core]
        ref[:, cols : 2 * cols] = dxn_s[2 * (1 - ix) + core]
        ref[:, 2 * cols :] = side


def early_end_body(idx, kept, side, ring, out_ref, router_ref, gain_ref):
    total = kept[...].astype(F32) + side[...].astype(F32) + ring[...].astype(F32)
    cols, experts = out_ref.shape[0], router_ref.shape[1]
    out_ref[...] = total[:, :cols].T
    router_ref[...] = total[:, cols : cols + experts]
    gain_ref[...] = total[:, cols:].T[experts : experts + 8]


def late_end_body(idx, kept, side, ring, query_ref, key_ref, value_ref, gain_ref):
    total = kept[...].astype(F32) + side[...].astype(F32) + ring[...].astype(F32)
    rows, qd = query_ref.shape
    kd = key_ref.shape[1]
    gain_ref[...] = total[rows : rows + 8, : gain_ref.shape[1]]
    query_ref[...] = total[:rows, :qd]
    key_ref[...] = total[:rows, qd : qd + kd]
    value_ref[...] = total[:rows, qd + kd :]


def expert_grads_body(count, *refs):
    xe, d0, dgu, hd = (refs[i * count : i * count + count] for i in range(4))
    gate_ref, up_ref, down_ref = refs[4 * count :]
    hidden = gate_ref.shape[2]

    def join(group, at=slice(None)):
        return jnp.concatenate([r[0, :, :, at].reshape(2 * PAD, -1) for r in group], axis=0)

    d_gu, hd_all = join(dgu), join(hd)
    for b in range(gate_ref.shape[1] // BLK):
        at = slice(b * BLK, b * BLK + BLK)
        both = mm_tn(join(xe, at), d_gu)
        gate_ref[0, at, :] = both[:, :hidden]
        up_ref[0, at, :] = both[:, hidden:]
        down_ref[0, :, at] = mm_tn(hd_all, join(d0, at))


class ExpertGrads:
    def __init__(self, xe, d0, dgu, hd, pieces=4):
        self.ins, self.outs = (*xe, *d0, *dgu, *hd), {}
        self.count, self.pieces = len(xe), pieces
        self.local, _, _, self.width = xe[0].shape
        self.hidden = hd[0].shape[3]

    def run(self, piece):
        local, width, hidden, count = self.local, self.width, self.hidden, self.count
        each = local // self.pieces
        first = each * piece

        def whole(n):
            return pl.BlockSpec((1, 2, PAD, n), lambda e: (e + first, 0, 0, 0))

        slots = count * 2 * PAD * each
        earlier = list(self.outs[0]) if self.outs else []
        body = functools.partial(expert_grads_body, count)
        n = len(self.ins)

        def with_earlier(*refs):
            body(*refs[:n], *refs[n + len(earlier) :])

        self.outs[0] = pl.pallas_call(
            with_earlier,
            grid=(each,),
            out_shape=[sds((local, width, hidden), F32), sds((local, width, hidden), F32), sds((local, hidden, width), F32)],
            in_specs=[whole(width)] * (2 * count) + [whole(2 * hidden)] * count + [whole(hidden)] * count
            + [pl.BlockSpec(memory_space=pl.ANY)] * len(earlier),
            out_specs=[pl.BlockSpec((1, width, hidden), lambda e: (e + first, 0, 0))] * 2
            + [pl.BlockSpec((1, hidden, width), lambda e: (e + first, 0, 0))],
            input_output_aliases={n + i: i for i in range(len(earlier))},
            compiler_params=pltpu.CompilerParams(vmem_limit_bytes=32 << 20),
            cost_estimate=pl.CostEstimate(
                flops=6 * slots * width * hidden, bytes_accessed=slots * width * 4 + 12 * each * width * hidden, transcendentals=0
            ),
            name="expert_grads",
        )(*self.ins, *earlier)


def add16(a, b):
    return (a.astype(F32) + b.astype(F32)).astype(BF16)


def on_device_gathered(
    tokens,
    document_numbers,
    picks,
    drop_order,
    w_query,
    key_matrix,
    value_matrix,
    w_out,
    w_router,
    gain_attn,
    gain_moe,
    expert_gate,
    expert_up,
    expert_down,
    cotangent,
):
    n_dp = lax.axis_size("dp")
    nz = n_dp // 2
    r, t = lax.axis_index("dp"), lax.axis_index("tensor")
    z, y, x, c = r // 2, r % 2, t // 2, t % 2
    idx = jnp.stack([r, z, y, x, c]).astype(jnp.int32)

    def shift_z(v):
        return lax.ppermute(v, "dp", [(i, ((i // 2 + 1) % nz) * 2 + i % 2) for i in range(n_dp)])

    def swap_y(v):
        return lax.ppermute(v, "dp", [(i, i ^ 1) for i in range(n_dp)])

    def swap_x(v):
        return lax.ppermute(v, "tensor", [(i, i ^ 2) for i in range(4)])

    def swap_c(v):
        return lax.ppermute(v, "tensor", [(i, i ^ 1) for i in range(4)])

    tok, width = tokens.shape
    rows = w_query.shape[0]
    qd, kd = w_query.shape[1], key_matrix.shape[1]
    used = qd + 2 * kd
    experts = w_router.shape[1]
    local, _, hidden = expert_gate.shape
    capacity = 9 * tok * picks.shape[1] // (8 * experts)
    cols = width // 4

    aux = jnp.concatenate(
        [w_router, gain_attn[:, None], gain_moe[:, None], jnp.zeros((rows, 128 - experts - 2), BF16)], axis=1
    )
    wz = [jnp.concatenate([w_query, key_matrix, value_matrix, aux, w_out.T], axis=1)]
    wy, wx = [], []

    def out_pair(k):
        return swap_x(jnp.stack([wz[k][:, used + 128 :], wy[k][:, used + 128 :]]))

    pos = kernel_call(
        functools.partial(slots_body, capacity),
        [sds((experts, tok), BF16)],
        [idx, picks.T, drop_order.reshape(tok, -1).T],
        name="slots",
    )[0]
    part = tok // 4
    def quarter(t):
        slots = jnp.pad(lax.dynamic_slice_in_dim(pos, t * part, part, 1), ((0, 0), (0, cols - part)))
        return jnp.concatenate([lax.dynamic_slice_in_dim(cotangent, t * cols, cols, 1), slots], axis=0)

    d_own, d_far = quarter(t), quarter(2 * (1 - x) + c)

    class Rows:
        def __init__(self, own):
            self.z, self.y, self.cz, self.cy = {0: own}, {}, {}, {}

        def ring(self, k):
            self.z[k] = shift_z(self.z[k - 1])

        def side(self, k):
            self.y[k] = swap_y(self.z[k])

        def core_ring(self, k):
            self.cz[k] = swap_c(self.z[k])

        def core_side(self, k):
            self.cy[k] = swap_c(self.y[k])

        def all(self, k):
            return [v[k] for v in (self.z, self.y, self.cz, self.cy)]

    class Split(Rows):
        def __init__(self, own, far):
            super().__init__(own)
            self.far, self.s, self.x, self.cs, self.cx = far, {}, {}, {}, {}

        def chip(self, k):
            self.s[k] = jnp.stack([self.z[k], self.y[k]])
            self.x[k] = swap_x(self.s[k] if k else self.y[0])

        def core_own(self, k):
            self.cs[k] = swap_c(self.s[k])

        def core(self, k):
            if k == 0:
                self.x[0] = jnp.stack([self.far, self.x[0]])
            self.cx[k] = swap_c(self.x[k])

        def all(self, k):
            return [v[k] for v in (self.s, self.x, self.cs, self.cx)]

    def meet(*items):
        places = [(getattr(o, n), k) for o, names, k in items for n in names.split()]
        values = sync(*[d[k] for d, k in places])
        for (d, k), v in zip(places, values):
            d[k] = v

    last = nz - 1
    for k in range(last):
        wz.append(shift_z(wz[k]))
        wy.append(swap_y(wz[k]))
        if k:
            wx.append(out_pair(k - 1))
        if k == 0:
            wz[1], wy[0], d_own, d_far = sync(wz[1], wy[0], d_own, d_far)
        else:
            wz[k + 1], wy[k] = sync(wz[k + 1], wy[k])
    wx.append(out_pair(last - 1))
    wy.append(swap_y(wz[last]))
    d = Split(after(d_own, wz[last]), d_far)
    d.ring(1)
    gu = jnp.concatenate(sync(expert_gate, expert_up, wz[last])[:2], axis=2)
    wy[last], wx[0], gu = sync(wy[last], wx[0], gu)
    wx.append(out_pair(last))

    positions = np.arange(tok, dtype=np.float32)
    inverse = rope_base ** (-(2.0 * np.arange(HEAD_SIZE // 2, dtype=np.float32)) / HEAD_SIZE)
    angles = positions[:, None] * inverse.astype(np.float32)[None, :]
    cos = jnp.asarray(np.tile(np.cos(angles), (1, 4)).astype(np.float32))
    sin = np.sin(angles)
    sin = jnp.asarray(np.tile(np.concatenate([-sin, sin], axis=1), (1, 2)).astype(np.float32))
    heads = qd // HEAD_SIZE
    seg_row = document_numbers.reshape(1, tok)
    o, q, k_rot, v, w_all, aux_t, *heads_p = kernel_call(
        functools.partial(attend_body, nz),
        [sds((tok, qd), BF16), sds((tok, qd), BF16), sds((tok, kd), BF16), sds((tok, kd), BF16),
         sds((width, used + 128), BF16), sds((128, width), BF16)] + [sds((tok, tok), BF16)] * heads,
        [idx, *wz, *wy, tokens, seg_row, seg_row.T, cos, sin],
        scratch=[pltpu.VMEM((tok, tok), F32), pltpu.VMEM((tok, used), F32)],
        flops=4e9,
        name="attend",
    )
    o, d.z[1], d.z[0], *wx[1:] = sync(o, d.z[1], d.z[0], *wx[1:])
    o_x, o_c0 = swap_x(o), swap_c(o)
    d.ring(2)
    d.side(0)
    wo = kernel_call(
        functools.partial(place_both_body, nz), [sds((2, width, qd), BF16)], [idx, *wz, *wy, *wx], name="place"
    )[0]
    wo_c = swap_c(wo)
    slot_ids = np.arange(local * PAD)
    sel = (r * local + slot_ids[:, None] // PAD == jnp.arange(experts)[None, :]).astype(BF16)
    slot_col = jnp.asarray((slot_ids % PAD).astype(np.float32)[:, None])
    slot_row = jnp.asarray((slot_ids % PAD).astype(np.float32)[None, :])
    o_x, o_c0, wo_c, sel, d.z[2], d.y[0] = sync(o_x, o_c0, wo_c, sel, d.z[2], d.y[0])
    d.ring(3)
    d.side(1)
    d.side(2)
    d.chip(0)
    d.core_own(0)
    o_c1 = swap_c(o_x)
    h, low, ring0 = kernel_call(
        out_body,
        [sds((tok, width), F32), sds((tok, width), BF16), sds((tok, 2 * cols), BF16)],
        [idx, tokens, o, o_x, o_c0, o_c1, wo, wo_c, aux_t],
        flops=5e9,
        name="out",
    )
    ring0, d.y[1], d.y[2], d.z[3], d.x[0], d.cs[0] = sync(ring0, d.y[1], d.y[2], d.z[3], d.x[0], d.cs[0])
    a = Rows(ring0)
    done = {}

    def run_experts(k):
        done[k] = experts_call(idx, a.all(k), d.all(k), gu, expert_down, aux_t, sel, slot_col, slot_row)

    class Sums:
        def __init__(self, at):
            self.at, self.c, self.s, self.y, self.total = at, {}, {}, {}, {}

        def core(self, k):
            self.c[k] = swap_c(done[k][self.at + 1])

        def side(self, k):
            m, n = done[k][self.at], self.c[k]
            self.s[k] = add16(m[0], n[0])
            self.y[k] = swap_y(add16(m[1], n[1]))

        def ring(self, k):
            total = self.s[k].astype(F32) + self.y[k].astype(F32)
            if self.total:
                total = total + self.total[0].astype(F32)
            total = total.astype(BF16)
            self.total[0] = total if k == 0 else shift_z(total)

    class SplitSums(Sums):
        def __init__(self, at):
            super().__init__(at)
            self.x = {}

        def chip(self, k):
            self.x[k] = swap_x(add16(done[k][self.at][:, :, cols:], self.c[k][:, :, cols:]))

        def side(self, k):
            m, n, far = done[k][self.at], self.c[k], self.x[k]
            own = [(m[q, :, :cols].astype(F32) + n[q, :, :cols].astype(F32) + far[q].astype(F32)).astype(BF16) for q in (0, 1)]
            self.s[k] = own[0]
            self.y[k] = swap_y(own[1])

    sx, sy = Sums(0), SplitSums(2)

    class Ran:
        out = done

    ran = Ran()
    a.ring(1)
    a.side(0)
    d.chip(1)
    d.core(0)
    meet((a, "z", 1), (a, "y", 0), (d, "x", 1), (d, "cx", 0))
    a.core_side(0)
    a.core_ring(0)
    d.core_own(1)
    meet((a, "cy cz", 0), (d, "cs x", 1))
    a.ring(2)
    a.side(1)
    d.side(3)
    d.chip(2)
    run_experts(0)
    meet((a, "z", 2), (a, "y", 1), (ran, "out", 0), (d, "y", 3), (d, "x", 2), (d, "x", 1))
    a.core_side(1)
    a.core_ring(1)
    d.core(1)
    meet((a, "cy cz", 1), (d, "cx", 1), (d, "x", 2), (ran, "out", 0))
    a.ring(3)
    a.side(2)
    d.chip(3)
    d.core_own(2)
    d.core(2)
    run_experts(1)
    meet((a, "z", 3), (a, "y", 2), (ran, "out", 1), (d, "x", 3), (d, "cx cs", 2))
    a.side(3)
    a.core_side(2)
    a.core_ring(2)
    sx.core(1)
    sy.core(0)
    meet((a, "cy cz", 2), (sx, "c", 1), (sy, "c", 0), (ran, "out", 1), (d, "x", 3))
    sx.side(1)
    sy.chip(0)
    d.core_own(3)
    d.core(3)
    run_experts(2)
    meet((a, "y", 3), (sx, "s y", 1), (sy, "x", 0), (ran, "out", 2), (d, "cs cx", 3))
    sx.ring(1)
    a.core_side(3)
    a.core_ring(3)
    sx.core(2)
    sy.core(1)
    meet((a, "cy cz", 3), (sx, "c", 2), (ran, "out", 2), (sy, "c", 1))
    sx.side(2)
    sy.chip(1)
    sy.side(0)
    run_experts(3)
    meet((sx, "s y", 2), (sx, "total", 0), (sy, "x", 1), (sy, "s y", 0), (ran, "out", 3))
    grads = ExpertGrads(*[[done[k][i] for k in range(nz)] for i in range(4, 8)])
    sx.ring(2)
    sx.core(3)
    sy.core(2)
    meet((sx, "c", 3), (ran, "out", 3), (sy, "c", 2))
    sx.side(3)
    sx.core(0)
    sy.chip(2)
    sy.core(3)
    grads.run(0)
    grads.run(1)
    meet((sx, "s y", 3), (sx, "total", 0), (sx, "c", 0), (sy, "x", 1), (sy, "x", 2), (sy, "c", 3), (grads, "outs", 0))
    sx.ring(3)
    sx.side(0)
    sy.chip(3)
    grads.run(2)
    meet((sx, "s y", 0), (sx, "total", 0), (sy, "x", 2), (sy, "x", 3), (grads, "outs", 0))
    sx.ring(0)
    far = swap_x(sx.total[0])
    sy.side(1)
    sy.side(2)
    grads.run(3)
    sx.total[0], far, *rest = sync(sx.total[0], far, sy.s[1], sy.y[1], sy.s[2], sy.y[2], sy.x[3], grads.outs[0])
    sy.s[1], sy.y[1], sy.s[2], sy.y[2], sy.x[3], grads.outs[0] = rest
    mine = sx.total[0].astype(F32) + jnp.concatenate([far[:, cols:], far[:, :cols]], axis=1).astype(F32)
    head, tail = mine[:tok], sx.total[0][tok:].astype(F32) + far[tok:].astype(F32)
    fm = jnp.concatenate([head.astype(BF16), tail.astype(BF16)], axis=0)
    fn = swap_c(fm)
    fm, fn, sy.y[1], sy.x[3] = sync(fm, fn, sy.y[1], sy.x[3])
    sy.side(3)
    sy.ring(1)
    groups = sent_groups(nz)

    def blocks_of(n, width, groups):
        return [sds((n, width), BF16)] * nz + [sds((len(g), n, width), BF16) for g in groups]

    d_h, d_o, *early = kernel_call(
        functools.partial(hidden_back_body, nz),
        [sds((tok, cols), F32), sds((tok, qd), BF16)] + blocks_of(rows, qd + 128, groups[0]),
        [idx, fm, fn, h, low, aux_t, pos, cotangent, o, wo],
        scratch=[pltpu.VMEM((tok, width), F32), pltpu.VMEM((experts, tok), F32), pltpu.VMEM((n_dp, rows, qd + 128), BF16)],
        flops=3e9,
        name="hidden_back",
    )
    d_o, early, sy.total[0], sy.s[3], sy.y[3] = sync(d_o, early, sy.total[0], sy.s[3], sy.y[3])

    class Weights:
        def __init__(self, v, groups):
            self.kept, self.sent, self.groups, self.y, self.total = v[:nz], v[nz:], groups, {}, {}

        def side(self, i):
            got = swap_y(self.sent[i])
            for at, k in enumerate(self.groups[i]):
                self.y[k] = got[at]

        def ring(self, k):
            total = self.kept[k].astype(F32) + self.y[k].astype(F32)
            if self.total:
                total = total + self.total[0].astype(F32)
            self.total[0] = shift_z(total.astype(BF16))

        def last(self):
            return self.kept[0], self.y[0], self.total[0]

    early = Weights(early, groups[0])
    early.side(0)
    sy.ring(2)
    dxm, dxn, *late = kernel_call(
        functools.partial(attend_back_body, nz),
        [sds((tok, 2 * cols + 128), BF16), sds((tok, 2 * cols + 128), BF16)] + blocks_of(rows + 16, used, groups[1]),
        [idx, d_o, v, k_rot, q, cos, sin, tokens, aux_t, w_all, *heads_p],
        scratch=[
            pltpu.VMEM((tok, used), F32), pltpu.VMEM((tok, used), BF16), pltpu.VMEM((4, tok, cols), BF16),
            pltpu.VMEM((n_dp, rows + 16, used), BF16),
        ],
        flops=5e9,
        name="attend_back",
    )
    late, dxm, dxn, early.y, early.sent, sy.total[0] = sync(late, dxm, dxn, early.y, early.sent, sy.total[0])
    late = Weights(late, groups[1])
    late.side(0)
    sy.ring(3)
    got = swap_c(dxn)
    late.y, late.sent, early.sent, early.y, got = sync(late.y, late.sent, early.sent, early.y, got)
    late.side(1)
    late.ring(1)
    early.ring(1)
    ours = dxm.astype(F32) + got.astype(F32)
    mean_part = ours[:, 2 * cols] + ours[:, 2 * cols + 1]
    high, lowp = split16(mean_part)
    send = jnp.concatenate(
        [ours[:, cols : 2 * cols].astype(BF16), high[:, None], lowp[:, None], jnp.zeros((tok, 126), BF16)], axis=1
    )
    got = swap_x(send)
    late.y, late.sent, late.total[0], early.total[0], got, sy.total[0] = sync(
        late.y, late.sent, late.total[0], early.total[0], got, sy.total[0]
    )
    late.side(2)
    late.ring(2)
    early.side(1)
    early.ring(2)
    y_sum = sy.s[0].astype(F32) + sy.y[0].astype(F32) + sy.total[0].astype(F32)
    mixed = (y_sum + lax.dynamic_slice_in_dim(h, t * cols, cols, 1)).astype(BF16)
    x_full = tokens.astype(F32)
    r1 = lax.rsqrt(jnp.mean(x_full * x_full, axis=-1, keepdims=True) + epsilon)
    d_norm = ours[:, :cols] + got[:, :cols].astype(F32)
    mean = (mean_part + got[:, cols].astype(F32) + got[:, cols + 1].astype(F32))[:, None] / width
    x_cols = lax.dynamic_slice_in_dim(tokens, t * cols, cols, 1).astype(F32) * r1
    gain_row = lax.dynamic_slice_in_dim(aux_t[64:65], t * cols, cols, 1).astype(F32)
    grad_tokens = d_h + r1 * (d_norm * gain_row - x_cols * mean)
    late.y, late.total[0], early.y, early.total[0], grad_tokens, mixed = sync(
        late.y, late.total[0], early.y, early.total[0], grad_tokens, mixed
    )
    late.ring(3)
    early.ring(3)
    late.total[0], early.total[0] = sync(late.total[0], early.total[0])
    grad_out, grad_router, gain_rows = kernel_call(
        early_end_body,
        [sds((qd, rows), F32), sds((rows, experts), F32), sds((8, rows), F32)],
        [idx, *early.last()],
        name="early_end",
    )
    grad_gain_moe = gain_rows[0]
    grad_query, grad_key, grad_value, gain_rows = kernel_call(
        late_end_body,
        [sds((rows, qd), F32), sds((rows, kd), F32), sds((rows, kd), F32), sds((8, rows), F32)],
        [idx, *late.last()],
        name="late_end",
    )
    gain_part = gain_rows[0] + gain_rows[1]
    gain_part = gain_part + swap_c(gain_part)
    grad_gain_attn = gain_part + swap_x(gain_part)
    grad_gate, grad_up, grad_down = grads.outs[0]
    return (
        mixed,
        grad_tokens,
        grad_query,
        grad_key,
        grad_value,
        grad_out,
        grad_router,
        grad_gain_attn,
        grad_gain_moe,
        grad_gate,
        grad_up,
        grad_down,
    )


def solution(mesh):
    few = mesh.shape["tensor"] == 4 and mesh.shape["dp"] in (4, 8)
    return jax.shard_map(
        on_device_gathered if few else on_device,
        mesh=mesh,
        in_specs=(
            P("dp", None),
            P("dp", None),
            P("dp", None),
            P("dp", None),
            P("dp", "tensor"),
            P("dp", "tensor"),
            P("dp", "tensor"),
            P("tensor", "dp"),
            P("dp", None),
            P("dp"),
            P("dp"),
            P("dp", None, "tensor"),
            P("dp", None, "tensor"),
            P("dp", "tensor", None),
            P("dp", None),
        ),
        out_specs=(
            P("dp", "tensor"),
            P("dp", "tensor"),
            P("dp", "tensor"),
            P("dp", "tensor"),
            P("dp", "tensor"),
            P("tensor", "dp"),
            P("dp", None),
            P("dp"),
            P("dp"),
            P("dp", None, "tensor"),
            P("dp", None, "tensor"),
            P("dp", "tensor", None),
        ),
        check_vma=False,
    )
```
